32 devices in a mesh: seq: 8 (over y, x, core), tp: 4 (over z).
Axes of the slice: x: 2, y: 2, z: 4, core: 2. Of those that a mesh axis runs over, the one named last changes fastest.
Arguments:
- token_ids: int32 [64, 4], replicated, may hold values from 0 to 51199
- embedding: bfloat16 [51200, 2048], P(('seq', 'tp')), may hold values from -8 to 8
- group_of: int32 [64], replicated, may hold values from 0 to 7, as said below
- prefix_len: int32 [8], replicated, may hold values from 1 to 512, as said below
- tail_len: int32 [64], replicated, may hold values from 1 to 128, as said below
- block_map: int32 [128, 2], P('seq'), may hold values from -1 to 71, as said below
- k_cache: bfloat16 [2, 16384, 2048], P(None, 'seq', 'tp'), may hold values from -100 to 100
- v_cache: bfloat16 [2, 16384, 2048], P(None, 'seq', 'tp'), may hold values from -12 to 12
- ln_gain: float32 [2, 2048], replicated, may hold values from 0.25 to 1.75
- ln_bias: float32 [2, 2048], replicated, may hold values from -1.5 to 1.5
- w_qkv: bfloat16 [2, 2048, 3, 2048], P(None, 'seq', None, 'tp'), may hold values from -0.125 to 0.125
- w_fc1: bfloat16 [2, 2048, 8192], P(None, 'seq', 'tp'), may hold values from -0.125 to 0.125
- b_fc1: float32 [2, 8192], P(None, 'tp'), may hold values from -2.5 to 2.5
- w_out: bfloat16 [2, 2048, 2048], P(None, ('tp', 'seq')), may hold values from -0.125 to 0.125
- w_fc2: bfloat16 [2, 8192, 2048], P(None, ('tp', 'seq')), may hold values from -0.0625 to 0.0625
Outputs:
- hidden_out: float32 [64, 4, 2048], replicated
The draws below stay inside these ranges and needn't reach their ends.
Inputs may be any that keep to these rules, and one draw needn't show every extreme that they name: `group_of`: every group holds exactly 8 requests. `prefix_len`: some group's prompt is 512 long. `tail_len`: some request's tail is 128 long. `block_map`: row b gives the segment held by cache block b (slots b * 128 to b * 128 + 127): g for group g's prompt, 8 + r for request r's tail, -1 for none; and its rank within the segment. A segment of length L holds ranks 0 to ceil(L / 128) - 1, each in exactly one block; a block with segment -1 has rank 0.
All inputs are finite; a program needn't handle non-finite values.
Results may differ from the reference program's by a relative error of at most 0.04.
The reference program's roundings to bfloat16 on the way count: a program that leaves them out, or rounds other values in their place, can miss the bound.
Values may be sent and summed in bfloat16 or wider, within the bound.
No kernel may reach another device: no remote copies, remote signals or barrier semaphores. Data moves between devices by JAX's collectives and lax.ppermute only.
A program may use at most 192 MiB of HBM per device.

```python
import math
import jax
import jax.numpy as jnp
import numpy as np
from jax import lax

D = 2048
HEADS = 32
HEAD_DIM = 64
FF = 8192
ROT = 32
VOCAB = 51200
LAYERS = 2
NEW = 4
RPG = 8
BLOCK = 128
REQS = 64
GROUPS = 8
SLOTS = 16384
NBLK = 128
PREFIX_MAX = 512
TAIL_MAX = 128


def layout_helper(key):
    key_prompt = jax.random.fold_in(key, 101)
    key_prompt_top = jax.random.fold_in(key, 102)
    key_tail = jax.random.fold_in(key, 103)
    key_tail_top = jax.random.fold_in(key, 104)
    key_order = jax.random.fold_in(key, 105)
    prompt_lengths = jax.random.randint(key_prompt, (GROUPS,), 1, PREFIX_MAX + 1).astype(jnp.int32)
    prompt_lengths = prompt_lengths.at[jax.random.randint(key_prompt_top, (), 0, GROUPS)].set(PREFIX_MAX)
    tail_lengths = jax.random.randint(key_tail, (REQS,), 1, TAIL_MAX + 1).astype(jnp.int32)
    tail_lengths = tail_lengths.at[jax.random.randint(key_tail_top, (), 0, REQS)].set(TAIL_MAX)
    lengths = jnp.concatenate([prompt_lengths, tail_lengths])
    block_counts = (lengths + BLOCK - 1) // BLOCK
    segment_count = GROUPS + REQS
    order = jax.random.permutation(key_order, segment_count).astype(jnp.int32)
    sizes_sorted = block_counts[order]
    ends = jnp.cumsum(sizes_sorted).astype(jnp.int32)
    starts = ends - sizes_sorted
    block_ids = jnp.arange(NBLK, dtype=jnp.int32)
    where_in = jnp.searchsorted(ends, block_ids, side='right').astype(jnp.int32)
    used = where_in < segment_count
    clipped = jnp.minimum(where_in, segment_count - 1)
    segment = jnp.where(used, order[clipped], -1)
    rank = jnp.where(used, block_ids - starts[clipped], 0)
    return (prompt_lengths, tail_lengths, jnp.stack([segment, rank], axis=1).astype(jnp.int32))


def draw_prefix_len(key, part):
    return layout_helper(key)[0]


def draw_tail_len(key, part):
    return layout_helper(key)[1]


def draw_block_map(key, part):
    return layout_helper(key)[2]


def draw_group_of(key, part):
    order = jax.random.permutation(jax.random.fold_in(key, 201), REQS).astype(jnp.int32)
    return (order // RPG).astype(jnp.int32)


def draw_embedding(key, part):
    column = jnp.arange(D, dtype=jnp.float32) / D
    base = jnp.clip(jax.random.normal(key, (VOCAB, D), jnp.float32), -4.0, 4.0)
    spread = 0.6 * jnp.exp(column * jnp.log(3.0))
    return (base * spread[None, :]).astype(jnp.bfloat16)


def draw_k_cache(key, part):
    base = jnp.clip(jax.random.normal(key, (LAYERS, SLOTS, D), jnp.float32), -5.0, 5.0)
    return base.astype(jnp.bfloat16)


def set_ends(values, stream_key, least, high):
    shape = values.shape
    spot = [jax.random.randint(jax.random.fold_in(stream_key, axis), (), 0, shape[axis]) for axis in range(len(shape))]
    values = values.at[tuple(spot)].set(least)
    longest = shape.index(max(shape))
    spot[longest] = (spot[longest] + 1) % shape[longest]
    return values.at[tuple(spot)].set(high)


def levels(key, shape, split, smallest, high):
    def one(position, shards_of):
        steps = jax.random.uniform(jax.random.fold_in(jax.random.fold_in(key, 6), position), (shards_of,), jnp.float32, smallest / len(split), high / len(split))
        return jnp.repeat(jnp.exp(steps), shape[position] // shards_of).reshape((-1,) + (1,) * (len(shape) - position - 1))

    level = one(*split[0])
    for cut in split[1:]:
        level = level * one(*cut)
    return level


def rank_table(count, skew):
    weights = [(1 << 20) // math.isqrt(grade ** skew) + 1 for grade in range(1, count + 1)]
    deviation = 1 + sum(weights) // (1 << 30)
    return np.cumsum(np.array([max(1, weight // deviation) for weight in weights]))


def ranked_ids(stream_key, extent, amount, lean):
    grid = rank_table(amount, lean)
    ticket = jax.random.randint(jax.random.fold_in(stream_key, 1), extent, 0, int(grid[amount - 1]))
    standing = jnp.searchsorted(jnp.asarray(grid, jnp.int32), ticket, side="right")
    return jax.random.permutation(jax.random.fold_in(stream_key, 2), amount)[standing].astype(jnp.int32)


def scatter_about(rng, shape, width, reach, split=(), held_as=jnp.bfloat16):
    loudness = levels(rng, shape, split, -0.22, 0.18) if split else 1.0
    drawn = jax.random.normal(rng, shape, jnp.float32) * width * loudness
    return jnp.minimum(jnp.maximum(drawn, -reach), reach).astype(held_as)


def setup_inputs(seed: int = 0) -> dict:
    keys = jax.random.split(jax.random.key(seed), 16)
    return {
        "token_ids": set_ends(ranked_ids(keys[0], (REQS, NEW), VOCAB, 2), jax.random.fold_in(keys[0], 3), 0, VOCAB - 1).astype(jnp.int32),
        "embedding": draw_embedding(jax.random.fold_in(keys[15], 71), 0),
        "group_of": draw_group_of(jax.random.fold_in(keys[15], 71), 0),
        "prefix_len": draw_prefix_len(jax.random.fold_in(keys[15], 71), 0),
        "tail_len": draw_tail_len(jax.random.fold_in(keys[15], 71), 0),
        "block_map": draw_block_map(jax.random.fold_in(keys[15], 71), 0),
        "k_cache": draw_k_cache(jax.random.fold_in(keys[15], 71), 0),
        "v_cache": scatter_about(keys[7], (LAYERS, SLOTS, D), 2.0, 12.0, ((1, 8), (2, 4))),
        "ln_gain": jnp.clip(1.0 + 0.15 * jax.random.normal(keys[8], (LAYERS, D), jnp.float32), 0.25, 1.75),
        "ln_bias": scatter_about(keys[9], (LAYERS, D), 0.3, 1.5, (), jnp.float32),
        "w_qkv": scatter_about(keys[10], (LAYERS, D, 3, D), D ** -0.5, 0.125, ((1, 8), (3, 4))),
        "w_fc1": scatter_about(keys[11], (LAYERS, D, FF), D ** -0.5, 0.125, ((1, 8), (2, 4))),
        "b_fc1": scatter_about(keys[12], (LAYERS, FF), 0.5, 2.5, ((1, 4),), jnp.float32),
        "w_out": scatter_about(keys[13], (LAYERS, D, D), D ** -0.5, 0.125, ((1, 32),)),
        "w_fc2": scatter_about(keys[14], (LAYERS, FF, D), FF ** -0.5, 0.0625, ((1, 32),)),
    }


def layer_norm(values, gain_row, bias_row):
    average = lax.optimization_barrier(jnp.mean(values, axis=-1, keepdims=True))
    centred = values - average
    variance = lax.optimization_barrier(jnp.mean(centred * centred, axis=-1, keepdims=True))
    return centred * lax.rsqrt(variance + 1e-05) * gain_row + bias_row

def rotary(values, positions):
    half_width = ROT // 2
    frequency = jnp.exp(jnp.arange(half_width, dtype=jnp.float32) * (-2.0 * math.log(10000.0) / ROT))
    angles = positions.astype(jnp.float32)[:, None] * frequency[None, :]
    cosine = jnp.cos(angles)[:, None, :]
    sine_part = jnp.sin(angles)[:, None, :]
    low_half = values[..., :half_width]
    high_half = values[..., half_width:ROT]
    return jnp.concatenate([low_half * cosine - high_half * sine_part, high_half * cosine + low_half * sine_part, values[..., ROT:]], axis=-1)

def rounded_weights(weights):
    return lax.optimization_barrier(weights.astype(jnp.bfloat16)).astype(jnp.float32)

def reference(token_ids, embedding, group_of, prefix_len, tail_len, block_map, k_cache, v_cache, ln_gain, ln_bias, w_qkv, w_fc1, b_fc1, w_out, w_fc2):
    groups = prefix_len.shape[0]
    requests = group_of.shape[0]
    new_tokens = token_ids.shape[1]
    very_negative = -1e+30
    score_scale = 1.0 / math.sqrt(HEAD_DIM)
    prompt_blocks = PREFIX_MAX // BLOCK
    tail_blocks = TAIL_MAX // BLOCK
    widest = max(prompt_blocks, tail_blocks)
    seg_blk = block_map[:, 0]
    rank_blk = block_map[:, 1]
    target = jnp.where(seg_blk >= 0, seg_blk, groups + requests).astype(jnp.int32)
    table = jnp.zeros((groups + requests, widest), jnp.int32).at[target, rank_blk].set(jnp.arange(NBLK, dtype=jnp.int32), mode='drop')
    members = jnp.argsort(group_of, stable=True).astype(jnp.int32).reshape(groups, RPG)
    prompt_valid = jnp.arange(prompt_blocks * BLOCK, dtype=jnp.int32)[None, :] < prefix_len[:, None]
    tail_valid = jnp.arange(tail_blocks * BLOCK, dtype=jnp.int32)[None, :] < tail_len[:, None]
    states = embedding[token_ids].astype(jnp.float32)
    shared_len = prefix_len[group_of]

    def attend(layer_index, queries, keys_new, values_new, token_step):
        key_blocks = k_cache[layer_index].reshape(NBLK, BLOCK, HEADS, HEAD_DIM)
        value_blocks = v_cache[layer_index].reshape(NBLK, BLOCK, HEADS, HEAD_DIM)
        visible = jnp.arange(new_tokens, dtype=jnp.int32) <= token_step

        def one_group(group_index):
            member_ids = members[group_index]
            prompt_ids = table[group_index, :prompt_blocks]
            tail_ids = table[groups + member_ids, :tail_blocks]
            keys_p = key_blocks[prompt_ids].reshape(-1, HEADS, HEAD_DIM).astype(jnp.float32)
            vals_p = value_blocks[prompt_ids].reshape(-1, HEADS, HEAD_DIM).astype(jnp.float32)
            keys_t = key_blocks[tail_ids].reshape(RPG, -1, HEADS, HEAD_DIM).astype(jnp.float32)
            vals_t = value_blocks[tail_ids].reshape(RPG, -1, HEADS, HEAD_DIM).astype(jnp.float32)
            keys_n = keys_new[member_ids].astype(jnp.float32)
            vals_n = values_new[member_ids].astype(jnp.float32)
            query_rows = queries[member_ids].astype(jnp.float32)
            valid_p = prompt_valid[group_index][None, None, :]
            valid_t = tail_valid[member_ids][:, None, :]
            valid_n = visible[None, None, :]
            score_p = jnp.einsum('rhd,shd->rhs', query_rows, keys_p) * score_scale
            score_t = jnp.einsum('rhd,rshd->rhs', query_rows, keys_t) * score_scale
            score_n = jnp.einsum('rhd,rjhd->rhj', query_rows, keys_n) * score_scale
            top_p = lax.optimization_barrier(jnp.max(jnp.where(valid_p, score_p, very_negative), axis=2))
            top_t = lax.optimization_barrier(jnp.max(jnp.where(valid_t, score_t, very_negative), axis=2))
            top_n = lax.optimization_barrier(jnp.max(jnp.where(valid_n, score_n, very_negative), axis=2))
            top_value = jnp.maximum(jnp.maximum(top_p, top_t), top_n)[..., None]
            weight_p = jnp.where(valid_p, jnp.exp(score_p - top_value), 0.0)
            weight_t = jnp.where(valid_t, jnp.exp(score_t - top_value), 0.0)
            weight_n = jnp.where(valid_n, jnp.exp(score_n - top_value), 0.0)
            denom = lax.optimization_barrier(jnp.sum(weight_p, axis=2)) + lax.optimization_barrier(jnp.sum(weight_t, axis=2)) + lax.optimization_barrier(jnp.sum(weight_n, axis=2))
            summed = jnp.einsum('rhs,shd->rhd', rounded_weights(weight_p), vals_p)
            summed = summed + jnp.einsum('rhs,rshd->rhd', rounded_weights(weight_t), vals_t)
            summed = summed + jnp.einsum('rhj,rjhd->rhd', rounded_weights(weight_n), vals_n)
            return summed / denom[..., None]
        outputs = lax.map(one_group, jnp.arange(groups, dtype=jnp.int32))
        gathered = jnp.zeros((requests, HEADS, HEAD_DIM), jnp.float32).at[members.reshape(-1)].set(outputs.reshape(requests, HEADS, HEAD_DIM))
        return gathered.astype(jnp.bfloat16).reshape(requests, D)
    new_keys = [jnp.zeros((requests, new_tokens, HEADS, HEAD_DIM), jnp.bfloat16) for layer_index in range(LAYERS)]
    new_values = [jnp.zeros((requests, new_tokens, HEADS, HEAD_DIM), jnp.bfloat16) for layer_index in range(LAYERS)]
    results = []
    for token_step in range(new_tokens):
        hidden_state = states[:, token_step]
        positions = shared_len + tail_len + token_step
        for layer_index in range(LAYERS):
            normed = layer_norm(hidden_state, ln_gain[layer_index], ln_bias[layer_index]).astype(jnp.bfloat16)
            joined = jnp.dot(normed, w_qkv[layer_index].reshape(D, 3 * D), preferred_element_type=jnp.float32)
            joined = joined.reshape(requests, 3, HEADS, HEAD_DIM)
            queries = rotary(joined[:, 0], positions).astype(jnp.bfloat16)
            key_rows = rotary(joined[:, 1], positions).astype(jnp.bfloat16)
            value_rows = joined[:, 2].astype(jnp.bfloat16)
            new_keys[layer_index] = new_keys[layer_index].at[:, token_step].set(key_rows)
            new_values[layer_index] = new_values[layer_index].at[:, token_step].set(value_rows)
            attended = attend(layer_index, queries, new_keys[layer_index], new_values[layer_index], token_step)
            pre_act = jnp.dot(normed, w_fc1[layer_index], preferred_element_type=jnp.float32) + b_fc1[layer_index]
            activated = jax.nn.gelu(pre_act, approximate=True).astype(jnp.bfloat16)
            update = jnp.dot(attended, w_out[layer_index], preferred_element_type=jnp.float32)
            update = update + jnp.dot(activated, w_fc2[layer_index], preferred_element_type=jnp.float32)
            hidden_state = hidden_state + update
        results.append(hidden_state)
    return jnp.stack(results, axis=1)
```

```python
import functools
import math

import jax
import jax.numpy as jnp
from jax import lax
from jax.experimental import pallas as pl
from jax.experimental.pallas import tpu as pltpu
from jax.sharding import PartitionSpec as P

HEADS = 32
HEAD_DIM = 64
ROT = 32
LAYERS = 2
BLOCK = 128
SPAN = 512


very_negative = -1e30


def layer_norm(values, gain_row, bias_row):
    average = jnp.mean(values, axis=-1, keepdims=True)
    centred = values - average
    variance = jnp.mean(centred * centred, axis=-1, keepdims=True)
    return centred * lax.rsqrt(variance + 1e-05) * gain_row + bias_row


def rotary(values, positions):
    half_width = ROT // 2
    frequency = jnp.exp(
        jnp.arange(half_width, dtype=jnp.float32) * (-2.0 * math.log(10000.0) / ROT)
    )
    angles = positions.astype(jnp.float32)[:, None] * frequency[None, :]
    cosine = jnp.cos(angles)[:, None, :]
    sine_part = jnp.sin(angles)[:, None, :]
    low_half = values[..., :half_width]
    high_half = values[..., half_width:ROT]
    return jnp.concatenate(
        [
            low_half * cosine - high_half * sine_part,
            high_half * cosine + low_half * sine_part,
            values[..., ROT:],
        ],
        axis=-1,
    )


def combine_parts(left_part, right_part):
    max_left, sum_left, out_left = left_part
    max_right, sum_right, out_right = right_part
    top_value = jnp.maximum(max_left, max_right)
    scale_left = jnp.exp(max_left - top_value)
    scale_right = jnp.exp(max_right - top_value)
    return (
        top_value,
        sum_left * scale_left + sum_right * scale_right,
        out_left * scale_left[..., None] + out_right * scale_right[..., None],
    )


def full_total(values):
    return lax.psum(values, ("seq", "tp"))


def per_device_any(
    token_ids,
    embedding,
    group_of,
    prefix_len,
    tail_len,
    block_map,
    k_cache,
    v_cache,
    ln_gain,
    ln_bias,
    w_qkv,
    w_fc1,
    b_fc1,
    w_out,
    w_fc2,
):
    tp_count = lax.axis_size("tp")
    seq_index = lax.axis_index("seq")
    tp_index = lax.axis_index("tp")
    requests = token_ids.shape[0]
    new_tokens = token_ids.shape[1]
    groups = prefix_len.shape[0]
    heads_local = HEADS // tp_count
    width_local = heads_local * HEAD_DIM
    score_scale = 1.0 / math.sqrt(HEAD_DIM)
    vocab_rows = embedding.shape[0]
    first_row = (seq_index * tp_count + tp_index) * vocab_rows
    local_ids = token_ids.reshape(-1) - first_row
    inside = (local_ids >= 0) & (local_ids < vocab_rows)
    picked = jnp.take(embedding, jnp.clip(local_ids, 0, vocab_rows - 1), axis=0).astype(jnp.float32)
    picked = jnp.where(inside[:, None], picked, 0.0)
    start_states = full_total(picked).reshape(requests, new_tokens, -1)
    group_hit = group_of[:, None] == jnp.arange(groups, dtype=jnp.int32)[None, :]
    shared_len = jnp.sum(jnp.where(group_hit, prefix_len[None, :], 0), axis=1)
    base_positions = shared_len + tail_len
    seg_len = jnp.concatenate([prefix_len, tail_len])
    seg_count = seg_len.shape[0]
    blocks_local = block_map.shape[0]
    seg_blk = block_map[:, 0]
    rank_blk = block_map[:, 1]
    seg_hit = seg_blk[:, None] == jnp.arange(seg_count, dtype=jnp.int32)[None, :]
    len_blk = jnp.sum(jnp.where(seg_hit, seg_len[None, :], 0), axis=1)
    slot_positions = rank_blk[:, None] * BLOCK + jnp.arange(BLOCK, dtype=jnp.int32)[None, :]
    live_slot = ((seg_blk[:, None] >= 0) & (slot_positions < len_blk[:, None])).reshape(-1)
    seg_slot = jnp.broadcast_to(seg_blk[:, None], (blocks_local, BLOCK)).reshape(-1)
    own_tail = seg_slot[None, :] == (groups + jnp.arange(requests, dtype=jnp.int32))[:, None]
    own_prompt = seg_slot[None, :] == group_of[:, None]
    allowed = (own_tail | own_prompt) & live_slot[None, :]
    step_count = allowed.shape[1] // SPAN
    allowed_steps = allowed.reshape(requests, step_count, SPAN).transpose(1, 0, 2)
    rows_local = w_qkv.shape[1]
    unit_count = w_fc2.shape[1]
    sub_width = w_out.shape[1]
    token_index = jnp.arange(new_tokens, dtype=jnp.int32)
    new_keys = [
        jnp.zeros((requests, new_tokens, heads_local, HEAD_DIM), jnp.bfloat16)
        for layer_index in range(LAYERS)
    ]
    new_values = [
        jnp.zeros((requests, new_tokens, heads_local, HEAD_DIM), jnp.bfloat16)
        for layer_index in range(LAYERS)
    ]
    results = []
    for token_step in range(new_tokens):
        hidden_state = start_states[:, token_step]
        positions = base_positions + token_step
        for layer_index in range(LAYERS):
            normed = layer_norm(hidden_state, ln_gain[layer_index], ln_bias[layer_index]).astype(
                jnp.bfloat16
            )
            my_rows = lax.dynamic_slice_in_dim(normed, seq_index * rows_local, rows_local, 1)
            part_proj = jnp.dot(
                my_rows,
                w_qkv[layer_index].reshape(rows_local, -1),
                preferred_element_type=jnp.float32,
            )
            part_fc1 = jnp.dot(my_rows, w_fc1[layer_index], preferred_element_type=jnp.float32)
            attention_proj, fc1_all = lax.psum((part_proj, part_fc1), "seq")
            pre_act = lax.dynamic_slice_in_dim(fc1_all, seq_index * unit_count, unit_count, 1)
            pre_act = (
                pre_act
                + lax.dynamic_slice_in_dim(
                    b_fc1[layer_index], seq_index * unit_count, unit_count, 0
                )[None, :]
            )
            activated = jax.nn.gelu(pre_act, approximate=True).astype(jnp.bfloat16)
            attention_proj = attention_proj.reshape(requests, 3, heads_local, HEAD_DIM)
            queries = rotary(attention_proj[:, 0], positions).astype(jnp.bfloat16)
            key_rows = rotary(attention_proj[:, 1], positions).astype(jnp.bfloat16)
            value_rows = attention_proj[:, 2].astype(jnp.bfloat16)
            new_keys[layer_index] = new_keys[layer_index].at[:, token_step].set(key_rows)
            new_values[layer_index] = new_values[layer_index].at[:, token_step].set(value_rows)
            key_steps = k_cache[layer_index].reshape(step_count, SPAN, heads_local, HEAD_DIM)
            value_steps = v_cache[layer_index].reshape(step_count, SPAN, heads_local, HEAD_DIM)

            def cache_step(carry, inputs):
                run_max, run_sum, run_out = carry
                key_block, value_block, allow_block = inputs
                scores = (
                    jnp.einsum(
                        "rhd,shd->hrs", queries, key_block, preferred_element_type=jnp.float32
                    )
                    * score_scale
                )
                scores = jnp.where(allow_block[None], scores, very_negative)
                next_max = jnp.maximum(run_max, jnp.max(scores, axis=2))
                weights = jnp.where(allow_block[None], jnp.exp(scores - next_max[..., None]), 0.0)
                shrink = jnp.exp(run_max - next_max)
                next_sum = run_sum * shrink + jnp.sum(weights, axis=2)
                next_out = run_out * shrink[..., None] + jnp.einsum(
                    "hrs,shd->hrd",
                    weights.astype(jnp.bfloat16),
                    value_block,
                    preferred_element_type=jnp.float32,
                )
                return ((next_max, next_sum, next_out), None)

            start_carry = (
                jnp.full((heads_local, requests), very_negative, jnp.float32),
                jnp.zeros((heads_local, requests), jnp.float32),
                jnp.zeros((heads_local, requests, HEAD_DIM), jnp.float32),
            )
            (part_max, part_sum, part_out), unused = lax.scan(
                cache_step, start_carry, (key_steps, value_steps, allowed_steps)
            )
            cache_max = lax.pmax(part_max, "seq")
            factor = jnp.exp(part_max - cache_max)
            cache_sum, cache_out = (
                lax.psum((part_sum * factor).astype(jnp.bfloat16), "seq").astype(jnp.float32),
                lax.psum((part_out * factor[..., None]).astype(jnp.bfloat16), "seq").astype(
                    jnp.float32
                ),
            )
            visible = (token_index <= token_step)[None, None, :]
            fresh_scores = (
                jnp.einsum(
                    "rhd,rjhd->hrj",
                    queries,
                    new_keys[layer_index],
                    preferred_element_type=jnp.float32,
                )
                * score_scale
            )
            fresh_scores = jnp.where(visible, fresh_scores, very_negative)
            fresh_max = jnp.max(fresh_scores, axis=2)
            fresh_weights = jnp.where(visible, jnp.exp(fresh_scores - fresh_max[..., None]), 0.0)
            fresh_sum = jnp.sum(fresh_weights, axis=2)
            fresh_out = jnp.einsum(
                "hrj,rjhd->hrd",
                fresh_weights.astype(jnp.bfloat16),
                new_values[layer_index],
                preferred_element_type=jnp.float32,
            )
            joint_max, denom_total, weighted = combine_parts(
                (cache_max, cache_sum, cache_out), (fresh_max, fresh_sum, fresh_out)
            )
            attended = (weighted / denom_total[..., None]).astype(jnp.bfloat16)
            attended = attended.transpose(1, 0, 2).reshape(requests, width_local)
            my_cols = lax.dynamic_slice_in_dim(attended, seq_index * sub_width, sub_width, 1)
            update = jnp.dot(my_cols, w_out[layer_index], preferred_element_type=jnp.float32)
            update = update + jnp.dot(
                activated, w_fc2[layer_index], preferred_element_type=jnp.float32
            )
            hidden_state = hidden_state + full_total(update)
        results.append(hidden_state)
    stacked = jnp.stack(results, axis=1)
    return stacked


def swap_cores(values, seq_count):
    return lax.ppermute(values, "seq", [(i, i ^ 1) for i in range(seq_count)])


def compiler_params(megabytes=32):
    return pltpu.CompilerParams(vmem_limit_bytes=megabytes * 2**20)


def whole(memory_space=pltpu.VMEM):
    return pl.BlockSpec(memory_space=memory_space)


def layer_block(layer_index, shape):
    return pl.BlockSpec((1,) + shape, lambda step: (layer_index,) + (0,) * len(shape))


def same_block(shape):
    return pl.BlockSpec(shape, lambda step: (0,) * len(shape))


def order_kernel(token_ref, group_ref, prefix_ref, tail_ref, rank_ref, id_ref, position_ref, count_ref):
    requests, new_tokens = token_ref.shape
    groups = prefix_ref.shape[0]
    per_group = requests // groups
    for group in range(groups):
        count_ref[group] = 0

    def place(request, unused):
        group = group_ref[request]
        seat = count_ref[group]
        count_ref[group] = seat + 1
        rank = group * per_group + seat
        rank_ref[request] = rank
        start = prefix_ref[group] + tail_ref[request]
        for token in range(new_tokens):
            id_ref[rank * new_tokens + token] = token_ref[request, token]
            position_ref[rank * new_tokens + token] = start + token
        return unused

    lax.fori_loop(0, requests, place, 0)


def order_requests(token_ids, group_of, prefix_len, tail_len):
    requests, new_tokens = token_ids.shape
    rows = requests * new_tokens
    smem = whole(pltpu.SMEM)
    return pl.pallas_call(
        order_kernel,
        out_shape=(
            jax.ShapeDtypeStruct((requests,), jnp.int32),
            jax.ShapeDtypeStruct((rows,), jnp.int32),
            jax.ShapeDtypeStruct((rows,), jnp.int32),
        ),
        in_specs=[smem] * 4,
        out_specs=(smem, smem, smem),
        scratch_shapes=[pltpu.SMEM((prefix_len.shape[0],), jnp.int32)],
        name="order_requests",
    )(token_ids, group_of, prefix_len, tail_len)


def state_total(part_ref, state_ref):
    total = part_ref[0].astype(jnp.float32)
    for source in range(1, part_ref.shape[0]):
        total = total + part_ref[source].astype(jnp.float32)
    if state_ref is not None:
        total = total + state_ref[...]
    return total


def norm_kernel(has_state, tp_count, *refs):
    if has_state:
        part_ref, state_ref, gain_ref, bias_ref, next_ref, cut_ref = refs
    else:
        part_ref, gain_ref, bias_ref, next_ref, cut_ref = refs
        state_ref = None
    state = state_total(part_ref, state_ref)
    next_ref[...] = state
    average = jnp.mean(state, axis=-1, keepdims=True)
    centred = state - average
    variance = jnp.mean(centred * centred, axis=-1, keepdims=True)
    gain = gain_ref[0, 0][None, :]
    bias = bias_ref[0, 0][None, :]
    normed = (centred * lax.rsqrt(variance + 1e-05) * gain + bias).astype(jnp.bfloat16)
    width = cut_ref.shape[2]
    for place in range(cut_ref.shape[0]):
        start = (place // tp_count) * width
        cut_ref[place] = normed[:, start : start + width]


def norm_rows(parts, state, ln_gain, ln_bias, layer_index, devices, tp_count):
    count, rows, width = parts.shape
    cut = width // (devices // tp_count)
    gains = [ln_gain[:, None, :], ln_bias[:, None, :]]
    operands = [parts] + ([] if state is None else [state]) + gains
    in_specs = [same_block(parts.shape)] + ([] if state is None else [same_block(state.shape)])
    in_specs += [layer_block(layer_index, (1, width))] * 2
    return pl.pallas_call(
        functools.partial(norm_kernel, state is not None, tp_count),
        grid=(1,),
        out_shape=(
            jax.ShapeDtypeStruct((rows, width), jnp.float32),
            jax.ShapeDtypeStruct((devices, rows, cut), jnp.bfloat16),
        ),
        in_specs=in_specs,
        out_specs=(same_block((rows, width)), same_block((devices, rows, cut))),
        compiler_params=compiler_params(),
        name="norm_rows",
    )(*operands)


def last_kernel(part_ref, state_ref, out_ref):
    state = state_total(part_ref, state_ref).astype(jnp.bfloat16)
    for place in range(out_ref.shape[0]):
        out_ref[place] = state


def last_rows(parts, state):
    return pl.pallas_call(
        last_kernel,
        out_shape=jax.ShapeDtypeStruct(parts.shape, jnp.bfloat16),
        in_specs=[whole(), whole()],
        out_specs=whole(),
        compiler_params=compiler_params(),
        name="last_rows",
    )(parts, state)


def project_kernel(parity_ref, hidden_ref, qkv_ref, fc1_ref, out_ref):
    parity = parity_ref[0]
    chips = out_ref.shape[0]
    rows, depth = hidden_ref.shape
    unit = fc1_ref.shape[2] // (2 * chips)
    share = rows // (2 * chips)
    hidden = hidden_ref[...]
    picked = []
    for chip in range(chips):
        place = 2 * chip + parity
        columns = pl.ds(pl.multiple_of(place * unit, unit), unit)
        out_ref[chip, :rows] = jnp.dot(
            hidden, fc1_ref[0, :, columns], preferred_element_type=jnp.float32
        ).astype(jnp.bfloat16)
        picked.append(hidden_ref[pl.ds(pl.multiple_of(place * share, share), share), :])
    heads = jnp.dot(
        jnp.concatenate(picked, axis=0), qkv_ref[...], preferred_element_type=jnp.float32
    ).astype(jnp.bfloat16)
    for chip in range(chips):
        for piece in range(heads.shape[1] // unit):
            start = rows + piece * share
            out_ref[chip, start : start + share] = heads[
                chip * share : (chip + 1) * share, piece * unit : (piece + 1) * unit
            ]


def project(parity, hidden, weights_qkv, w_fc1, layer_index, chips):
    rows, depth = hidden.shape
    unit = w_fc1.shape[2] // (2 * chips)
    share = rows // (2 * chips)
    height = rows + share * (weights_qkv.shape[1] // unit)
    return pl.pallas_call(
        project_kernel,
        grid=(1,),
        out_shape=jax.ShapeDtypeStruct((chips, height, unit), jnp.bfloat16),
        in_specs=[
            whole(pltpu.SMEM),
            same_block(hidden.shape),
            same_block(weights_qkv.shape),
            layer_block(layer_index, w_fc1.shape[1:]),
        ],
        out_specs=same_block((chips, height, unit)),
        compiler_params=compiler_params(),
        name="project",
    )(parity, hidden, weights_qkv, w_fc1)


def activate_kernel(part_ref, bias_ref, keep_ref, down_ref, up_ref, gelu_ref, query_ref, key_ref, value_ref):
    total = part_ref[0].astype(jnp.float32)
    for chip in range(1, part_ref.shape[0]):
        total = total + part_ref[chip].astype(jnp.float32)
    rows, unit = gelu_ref.shape
    share, width = query_ref.shape
    gelu_ref[...] = jax.nn.gelu(total[:rows] + bias_ref[...], approximate=True).astype(jnp.bfloat16)
    pieces = width // unit

    def one(index):
        start = rows + index * pieces * share
        return jnp.concatenate(
            [total[start + i * share : start + (i + 1) * share] for i in range(pieces)], axis=1
        )

    def turned(values):
        return (
            values * keep_ref[...]
            + pltpu.roll(values, width - ROT // 2, 1) * down_ref[...]
            + pltpu.roll(values, ROT // 2, 1) * up_ref[...]
        )

    query_ref[...] = turned(one(0)).astype(jnp.bfloat16)
    key_ref[...] = turned(one(1)).astype(jnp.bfloat16)
    value_ref[...] = one(2).astype(jnp.bfloat16)


def activate(parts, bias, tables, rows):
    chips, height, unit = parts.shape
    share, width = tables[0].shape
    small = jax.ShapeDtypeStruct((share, width), jnp.bfloat16)
    return pl.pallas_call(
        activate_kernel,
        out_shape=(jax.ShapeDtypeStruct((rows, unit), jnp.bfloat16), small, small, small),
        in_specs=[whole()] * 5,
        out_specs=(whole(),) * 4,
        compiler_params=compiler_params(),
        name="activate",
    )(parts, bias, *tables)


def rotary_tables(positions, width):
    half = ROT // 2
    feature = lax.broadcasted_iota(jnp.int32, (1, width), 1) % HEAD_DIM
    frequency = jnp.exp((feature % half).astype(jnp.float32) * (-2.0 * math.log(10000.0) / ROT))
    angles = positions.astype(jnp.float32)[:, None] * frequency
    cosine, sine = jnp.cos(angles), jnp.sin(angles)
    return (
        jnp.where(feature < ROT, cosine, 1.0),
        jnp.where(feature < half, -sine, 0.0),
        jnp.where((feature >= half) & (feature < ROT), sine, 0.0),
    )


def attend_kernel(
    layer_index, new_tokens,
    place_ref, rank_ref, map_ref, prefix_ref, tail_ref, query_ref, new_key_ref, new_value_ref,
    key_hbm, value_hbm, out_ref, key_ref, value_ref, top_ref, sum_ref, mix_ref, semaphores,
):
    blocks = map_ref.shape[0]
    groups, tall, lanes = mix_ref.shape
    requests = rank_ref.shape[0]
    per_group = requests // groups
    share = per_group * new_tokens
    pairs = tall // (2 * share)
    chunks = semaphores.shape[1]
    chunk = key_ref.shape[0] // chunks
    scale = 1.0 / math.sqrt(HEAD_DIM)

    def copies(index):
        span = pl.ds(index * chunk, chunk)
        return (
            pltpu.make_async_copy(key_hbm.at[layer_index, span], key_ref.at[span], semaphores.at[0, index]),
            pltpu.make_async_copy(value_hbm.at[layer_index, span], value_ref.at[span], semaphores.at[1, index]),
        )

    for index in range(chunks):
        for copy in copies(index):
            copy.start()
    lane = lax.broadcasted_iota(jnp.int32, (share, lanes), 1)
    wide_lane = lax.broadcasted_iota(jnp.int32, (tall, BLOCK), 1)
    wide_row = lax.broadcasted_iota(jnp.int32, (tall, BLOCK), 0) % share
    top_ref[...] = jnp.full(top_ref.shape, very_negative, jnp.float32)
    sum_ref[...] = jnp.zeros(sum_ref.shape, jnp.float32)
    mix_ref[...] = jnp.zeros(mix_ref.shape, jnp.float32)

    def visit(group, keys, values, mask):
        rows = pl.ds(pl.multiple_of(group * share, share), share)
        scores = []
        for pair in range(pairs):
            both = query_ref[rows, pair * lanes : (pair + 1) * lanes]
            none = jnp.zeros_like(both)
            split = jnp.concatenate(
                [jnp.where(lane < HEAD_DIM, both, none), jnp.where(lane < HEAD_DIM, none, both)], axis=0
            )
            scores.append(
                lax.dot_general(
                    split, keys[:, pair * lanes : (pair + 1) * lanes], (((1,), (1,)), ((), ())),
                    preferred_element_type=jnp.float32,
                )
            )
        score = jnp.where(mask, jnp.concatenate(scores, axis=0) * scale, very_negative)
        top = jnp.max(score, axis=1, keepdims=True)
        weight = jnp.where(mask, jnp.exp(score - top), 0.0)
        total = jnp.sum(weight, axis=1, keepdims=True)
        rounded = weight.astype(jnp.bfloat16)
        mixed = jnp.concatenate(
            [
                jnp.dot(
                    rounded[pair * 2 * share : (pair + 1) * 2 * share],
                    values[:, pair * lanes : (pair + 1) * lanes],
                    preferred_element_type=jnp.float32,
                )
                for pair in range(pairs)
            ],
            axis=0,
        )
        old_top = top_ref[group]
        joint = jnp.maximum(old_top, top)
        shrink, scale_new = jnp.exp(old_top - joint), jnp.exp(top - joint)
        top_ref[group] = joint
        sum_ref[group] = sum_ref[group] * shrink + total * scale_new
        mix_ref[group] = mix_ref[group] * shrink + mixed * scale_new

    for block in range(blocks):
        if (block * BLOCK) % chunk == 0:
            for copy in copies(block * BLOCK // chunk):
                copy.wait()
        segment, depth = map_ref[block, 0], map_ref[block, 1]
        is_tail = segment >= groups
        request = jnp.clip(segment - groups, 0, requests - 1)
        prompt = jnp.clip(segment, 0, groups - 1)
        seat = rank_ref[request]
        group = jnp.where(is_tail, seat // per_group, prompt)
        length = jnp.where(is_tail, tail_ref[request], prefix_ref[prompt])
        live = jnp.where(segment < 0, 0, length - depth * BLOCK)
        first = jnp.where(is_tail, (seat % per_group) * new_tokens, 0)
        end = jnp.where(is_tail, first + new_tokens, share)
        mask = (wide_lane < live) & (wide_row >= first) & (wide_row < end)
        span = slice(block * BLOCK, (block + 1) * BLOCK)
        visit(group, key_ref[span, :], value_ref[span, :], mask)

    fill = jnp.zeros((BLOCK - share, new_key_ref.shape[1]), jnp.bfloat16)
    mask = (wide_lane // new_tokens == wide_row // new_tokens) & (wide_lane <= wide_row)
    visit(
        place_ref[0],
        jnp.concatenate([new_key_ref[...], fill], axis=0),
        jnp.concatenate([new_value_ref[...], fill], axis=0),
        mask,
    )

    for group in range(groups):
        total = sum_ref[group]
        empty = total <= 0.0
        mean = mix_ref[group] / jnp.where(empty, 1.0, total)
        level = jnp.where(empty, very_negative, top_ref[group] + jnp.log(jnp.where(empty, 1.0, total)))
        high = level.astype(jnp.bfloat16).astype(jnp.float32)
        middle = (level - high).astype(jnp.bfloat16).astype(jnp.float32)
        low = level - high - middle
        for head in range(2 * pairs):
            rows = slice(head * share, (head + 1) * share)
            own = mean[rows]
            if head % 2:
                own = pltpu.roll(own, lanes - HEAD_DIM, 1)
            packed = jnp.where(lane < HEAD_DIM, own, 0.0)
            packed = jnp.where(lane == HEAD_DIM, high[rows], packed)
            packed = jnp.where(lane == HEAD_DIM + 1, middle[rows], packed)
            packed = jnp.where(lane == HEAD_DIM + 2, low[rows], packed)
            out_ref[head, group * share : (group + 1) * share] = packed.astype(jnp.bfloat16)


def attend(place, rank, block_map, prefix_len, tail_len, query, new_key, new_value, k_cache, v_cache, layer_index, new_tokens):
    rows, width = query.shape
    groups = prefix_len.shape[0]
    slots = k_cache.shape[1]
    heads = width // HEAD_DIM
    tall = heads * (rows // groups)
    lanes = 2 * HEAD_DIM
    chunks = 4
    return pl.pallas_call(
        functools.partial(attend_kernel, layer_index, new_tokens),
        out_shape=jax.ShapeDtypeStruct((heads, rows, lanes), jnp.bfloat16),
        in_specs=[whole(pltpu.SMEM)] * 5 + [whole()] * 3 + [whole(pl.ANY)] * 2,
        out_specs=whole(),
        scratch_shapes=[
            pltpu.VMEM((slots, width), jnp.bfloat16),
            pltpu.VMEM((slots, width), jnp.bfloat16),
            pltpu.VMEM((groups, tall, 1), jnp.float32),
            pltpu.VMEM((groups, tall, 1), jnp.float32),
            pltpu.VMEM((groups, tall, lanes), jnp.float32),
            pltpu.SemaphoreType.DMA((2, chunks)),
        ],
        compiler_params=compiler_params(),
        name="attend",
    )(place, rank, block_map, prefix_len, tail_len, query, new_key, new_value, k_cache, v_cache)


def update_kernel(share, parity_ref, part_ref, gelu_ref, out_weight_ref, fc2_ref, out_ref):
    parity = parity_ref[0]
    pieces = out_ref.shape[0] // share
    attended, hidden = [], []
    for piece in range(pieces):
        rows = pl.ds(pl.multiple_of((2 * piece + parity) * share, share), share)
        parts = [part_ref[source, rows, :].astype(jnp.float32) for source in range(part_ref.shape[0])]
        levels = [
            part[:, HEAD_DIM : HEAD_DIM + 1] + part[:, HEAD_DIM + 1 : HEAD_DIM + 2] + part[:, HEAD_DIM + 2 : HEAD_DIM + 3]
            for part in parts
        ]
        top = functools.reduce(jnp.maximum, levels)
        scales = [jnp.exp(level - top) for level in levels]
        total = functools.reduce(jnp.add, scales)
        mixed = functools.reduce(jnp.add, [part * scale for part, scale in zip(parts, scales)])
        attended.append((mixed / total)[:, :HEAD_DIM].astype(jnp.bfloat16))
        hidden.append(gelu_ref[rows, :])
    out_ref[...] = (
        jnp.dot(jnp.concatenate(attended, axis=0), out_weight_ref[0], preferred_element_type=jnp.float32)
        + jnp.dot(jnp.concatenate(hidden, axis=0), fc2_ref[0], preferred_element_type=jnp.float32)
    ).astype(jnp.bfloat16)


def update(parity, parts, gelu, w_out, w_fc2, layer_index, share):
    rows = gelu.shape[0] // 2
    width = w_out.shape[2]
    return pl.pallas_call(
        functools.partial(update_kernel, share),
        grid=(1,),
        out_shape=jax.ShapeDtypeStruct((rows, width), jnp.bfloat16),
        in_specs=[
            whole(pltpu.SMEM),
            same_block(parts.shape),
            same_block(gelu.shape),
            layer_block(layer_index, w_out.shape[1:]),
            layer_block(layer_index, w_fc2.shape[1:]),
        ],
        out_specs=same_block((rows, width)),
        compiler_params=compiler_params(),
        name="update",
    )(parity, parts, gelu, w_out, w_fc2)


def per_device(
    token_ids, embedding, group_of, prefix_len, tail_len, block_map, k_cache, v_cache,
    ln_gain, ln_bias, w_qkv, w_fc1, b_fc1, w_out, w_fc2,
):
    seq_count, tp_count = lax.axis_size("seq"), lax.axis_size("tp")
    seq_index, tp_index = lax.axis_index("seq"), lax.axis_index("tp")
    devices = seq_count * tp_count
    chips = seq_count // 2
    core = seq_index % 2
    own = jnp.reshape(core, (1,)).astype(jnp.int32)
    other = 1 - own
    requests, new_tokens = token_ids.shape
    rows = requests * new_tokens
    share = rows // seq_count
    mine = rows // devices
    width = embedding.shape[1]
    width_local = k_cache.shape[2]
    unit = w_fc2.shape[1]
    same_core = [[s * tp_count + p for s in range(c, seq_count, 2) for p in range(tp_count)] for c in range(2)]
    same_core_seq = [list(range(c, seq_count, 2)) for c in range(2)]

    def to_owners(half):
        parts = half.reshape(devices // 2, mine, width)
        return lax.all_to_all(parts, ("seq", "tp"), 0, 0, axis_index_groups=same_core)

    rank, ids, positions = order_requests(token_ids, group_of, prefix_len, tail_len)
    vocab_rows = embedding.shape[0]
    local_ids = (ids - (seq_index * tp_count + tp_index) * vocab_rows).reshape(chips, 2, share)

    def pick(parity):
        chosen = lax.dynamic_index_in_dim(local_ids, parity, 1, keepdims=False).reshape(-1)
        hot = (chosen[:, None] == jnp.arange(vocab_rows, dtype=jnp.int32)[None, :]).astype(jnp.bfloat16)
        return jnp.dot(hot, embedding, preferred_element_type=jnp.float32).astype(jnp.bfloat16)

    arriving = swap_cores(pick(1 - core), seq_count)
    parts = to_owners(pick(core) + arriving)
    tables = rotary_tables(lax.dynamic_slice_in_dim(positions, seq_index * share, share, 0), width_local)
    place = jnp.reshape(seq_index, (1,)).astype(jnp.int32)
    state = None
    for layer_index in range(LAYERS):
        weights_qkv = w_qkv[layer_index].reshape(w_qkv.shape[1], -1)
        bias = lax.dynamic_slice_in_dim(b_fc1[layer_index], seq_index * unit, unit, 0)[None, :]
        state, cut = norm_rows(parts, state, ln_gain, ln_bias, layer_index, devices, tp_count)
        hidden = lax.all_to_all(cut, ("seq", "tp"), 0, 0).reshape(rows, -1)
        arriving = swap_cores(project(other, hidden, weights_qkv, w_fc1, layer_index, chips), seq_count)
        kept = project(own, hidden, weights_qkv, w_fc1, layer_index, chips)
        joined = lax.all_to_all(kept + arriving, "seq", 0, 0, axis_index_groups=same_core_seq)
        gelu, query, new_key, new_value = activate(joined, bias, tables, rows)
        queries = lax.all_gather(query, "seq").reshape(rows, width_local)
        parts = attend(
            place, rank, block_map, prefix_len, tail_len, queries, new_key, new_value,
            k_cache, v_cache, layer_index, new_tokens,
        )
        parts = lax.all_to_all(parts, "seq", 0, 0)
        arriving = swap_cores(update(other, parts, gelu, w_out, w_fc2, layer_index, share), seq_count)
        parts = to_owners(update(own, parts, gelu, w_out, w_fc2, layer_index, share) + arriving)
    last = lax.all_to_all(last_rows(parts, state), ("seq", "tp"), 0, 0, axis_index_groups=same_core)
    last = last.reshape(rows // 2, width)
    arriving = swap_cores(last, seq_count)
    wanted = (rank[:, None] * new_tokens + jnp.arange(new_tokens, dtype=jnp.int32)[None, :]).reshape(-1)
    index = jnp.arange(rows // 2, dtype=jnp.int32)

    def placed(half, parity):
        held = (2 * (index // share) + parity) * share + index % share
        hot = (wanted[:, None] == held[None, :]).astype(jnp.bfloat16)
        return jnp.dot(hot, half, preferred_element_type=jnp.float32)

    return (placed(last, core) + placed(arriving, 1 - core)).reshape(requests, new_tokens, width)


def solution(mesh):
    in_specs = (
        P(),
        P(("seq", "tp"), None),
        P(),
        P(),
        P(),
        P("seq", None),
        P(None, "seq", "tp"),
        P(None, "seq", "tp"),
        P(),
        P(),
        P(None, "seq", None, "tp"),
        P(None, "seq", "tp"),
        P(None, "tp"),
        P(None, ("tp", "seq"), None),
        P(None, ("tp", "seq"), None),
    )
    out_specs = P()
    seq_count, tp_count = mesh.shape["seq"], mesh.shape["tp"]
    fits = seq_count == HEADS // tp_count and seq_count == 8
    return jax.shard_map(
        per_device if fits else per_device_any, mesh=mesh, in_specs=in_specs, out_specs=out_specs, check_vma=False
    )
```

```python
import functools
import math

import jax
import jax.numpy as jnp
from jax import lax
from jax.experimental import pallas as pl
from jax.experimental.pallas import tpu as pltpu
from jax.sharding import PartitionSpec as P

HEADS = 32
HEAD_DIM = 64
ROT = 32
LAYERS = 2
BLOCK = 128
SPAN = 512
CHIPS = 4


very_negative = -1e30


def layer_norm(values, gain_row, bias_row):
    average = jnp.mean(values, axis=-1, keepdims=True)
    centred = values - average
    variance = jnp.mean(centred * centred, axis=-1, keepdims=True)
    return centred * lax.rsqrt(variance + 1e-05) * gain_row + bias_row


def rotary(values, positions):
    half_width = ROT // 2
    frequency = jnp.exp(
        jnp.arange(half_width, dtype=jnp.float32) * (-2.0 * math.log(10000.0) / ROT)
    )
    angles = positions.astype(jnp.float32)[:, None] * frequency[None, :]
    cosine = jnp.cos(angles)[:, None, :]
    sine_part = jnp.sin(angles)[:, None, :]
    low_half = values[..., :half_width]
    high_half = values[..., half_width:ROT]
    return jnp.concatenate(
        [
            low_half * cosine - high_half * sine_part,
            high_half * cosine + low_half * sine_part,
            values[..., ROT:],
        ],
        axis=-1,
    )


def combine_parts(left_part, right_part):
    max_left, sum_left, out_left = left_part
    max_right, sum_right, out_right = right_part
    top_value = jnp.maximum(max_left, max_right)
    scale_left = jnp.exp(max_left - top_value)
    scale_right = jnp.exp(max_right - top_value)
    return (
        top_value,
        sum_left * scale_left + sum_right * scale_right,
        out_left * scale_left[..., None] + out_right * scale_right[..., None],
    )


def full_total(values):
    return lax.psum(values, ("seq", "tp"))


def per_device_any(
    token_ids,
    embedding,
    group_of,
    prefix_len,
    tail_len,
    block_map,
    k_cache,
    v_cache,
    ln_gain,
    ln_bias,
    w_qkv,
    w_fc1,
    b_fc1,
    w_out,
    w_fc2,
):
    tp_count = lax.axis_size("tp")
    seq_index = lax.axis_index("seq")
    tp_index = lax.axis_index("tp")
    requests = token_ids.shape[0]
    new_tokens = token_ids.shape[1]
    groups = prefix_len.shape[0]
    heads_local = HEADS // tp_count
    width_local = heads_local * HEAD_DIM
    score_scale = 1.0 / math.sqrt(HEAD_DIM)
    vocab_rows = embedding.shape[0]
    first_row = (seq_index * tp_count + tp_index) * vocab_rows
    local_ids = token_ids.reshape(-1) - first_row
    inside = (local_ids >= 0) & (local_ids < vocab_rows)
    picked = jnp.take(embedding, jnp.clip(local_ids, 0, vocab_rows - 1), axis=0).astype(jnp.float32)
    picked = jnp.where(inside[:, None], picked, 0.0)
    start_states = full_total(picked).reshape(requests, new_tokens, -1)
    group_hit = group_of[:, None] == jnp.arange(groups, dtype=jnp.int32)[None, :]
    shared_len = jnp.sum(jnp.where(group_hit, prefix_len[None, :], 0), axis=1)
    base_positions = shared_len + tail_len
    seg_len = jnp.concatenate([prefix_len, tail_len])
    seg_count = seg_len.shape[0]
    blocks_local = block_map.shape[0]
    seg_blk = block_map[:, 0]
    rank_blk = block_map[:, 1]
    seg_hit = seg_blk[:, None] == jnp.arange(seg_count, dtype=jnp.int32)[None, :]
    len_blk = jnp.sum(jnp.where(seg_hit, seg_len[None, :], 0), axis=1)
    slot_positions = rank_blk[:, None] * BLOCK + jnp.arange(BLOCK, dtype=jnp.int32)[None, :]
    live_slot = ((seg_blk[:, None] >= 0) & (slot_positions < len_blk[:, None])).reshape(-1)
    seg_slot = jnp.broadcast_to(seg_blk[:, None], (blocks_local, BLOCK)).reshape(-1)
    own_tail = seg_slot[None, :] == (groups + jnp.arange(requests, dtype=jnp.int32))[:, None]
    own_prompt = seg_slot[None, :] == group_of[:, None]
    allowed = (own_tail | own_prompt) & live_slot[None, :]
    step_count = allowed.shape[1] // SPAN
    allowed_steps = allowed.reshape(requests, step_count, SPAN).transpose(1, 0, 2)
    rows_local = w_qkv.shape[1]
    unit_count = w_fc2.shape[1]
    sub_width = w_out.shape[1]
    token_index = jnp.arange(new_tokens, dtype=jnp.int32)
    new_keys = [
        jnp.zeros((requests, new_tokens, heads_local, HEAD_DIM), jnp.bfloat16)
        for layer_index in range(LAYERS)
    ]
    new_values = [
        jnp.zeros((requests, new_tokens, heads_local, HEAD_DIM), jnp.bfloat16)
        for layer_index in range(LAYERS)
    ]
    results = []
    for token_step in range(new_tokens):
        hidden_state = start_states[:, token_step]
        positions = base_positions + token_step
        for layer_index in range(LAYERS):
            normed = layer_norm(hidden_state, ln_gain[layer_index], ln_bias[layer_index]).astype(
                jnp.bfloat16
            )
            my_rows = lax.dynamic_slice_in_dim(normed, seq_index * rows_local, rows_local, 1)
            part_proj = jnp.dot(
                my_rows,
                w_qkv[layer_index].reshape(rows_local, -1),
                preferred_element_type=jnp.float32,
            )
            part_fc1 = jnp.dot(my_rows, w_fc1[layer_index], preferred_element_type=jnp.float32)
            attention_proj, fc1_all = lax.psum((part_proj, part_fc1), "seq")
            pre_act = lax.dynamic_slice_in_dim(fc1_all, seq_index * unit_count, unit_count, 1)
            pre_act = (
                pre_act
                + lax.dynamic_slice_in_dim(
                    b_fc1[layer_index], seq_index * unit_count, unit_count, 0
                )[None, :]
            )
            activated = jax.nn.gelu(pre_act, approximate=True).astype(jnp.bfloat16)
            attention_proj = attention_proj.reshape(requests, 3, heads_local, HEAD_DIM)
            queries = rotary(attention_proj[:, 0], positions).astype(jnp.bfloat16)
            key_rows = rotary(attention_proj[:, 1], positions).astype(jnp.bfloat16)
            value_rows = attention_proj[:, 2].astype(jnp.bfloat16)
            new_keys[layer_index] = new_keys[layer_index].at[:, token_step].set(key_rows)
            new_values[layer_index] = new_values[layer_index].at[:, token_step].set(value_rows)
            key_steps = k_cache[layer_index].reshape(step_count, SPAN, heads_local, HEAD_DIM)
            value_steps = v_cache[layer_index].reshape(step_count, SPAN, heads_local, HEAD_DIM)

            def cache_step(carry, inputs):
                run_max, run_sum, run_out = carry
                key_block, value_block, allow_block = inputs
                scores = (
                    jnp.einsum(
                        "rhd,shd->hrs", queries, key_block, preferred_element_type=jnp.float32
                    )
                    * score_scale
                )
                scores = jnp.where(allow_block[None], scores, very_negative)
                next_max = jnp.maximum(run_max, jnp.max(scores, axis=2))
                weights = jnp.where(allow_block[None], jnp.exp(scores - next_max[..., None]), 0.0)
                shrink = jnp.exp(run_max - next_max)
                next_sum = run_sum * shrink + jnp.sum(weights, axis=2)
                next_out = run_out * shrink[..., None] + jnp.einsum(
                    "hrs,shd->hrd",
                    weights.astype(jnp.bfloat16),
                    value_block,
                    preferred_element_type=jnp.float32,
                )
                return ((next_max, next_sum, next_out), None)

            start_carry = (
                jnp.full((heads_local, requests), very_negative, jnp.float32),
                jnp.zeros((heads_local, requests), jnp.float32),
                jnp.zeros((heads_local, requests, HEAD_DIM), jnp.float32),
            )
            (part_max, part_sum, part_out), unused = lax.scan(
                cache_step, start_carry, (key_steps, value_steps, allowed_steps)
            )
            cache_max = lax.pmax(part_max, "seq")
            factor = jnp.exp(part_max - cache_max)
            cache_sum, cache_out = (
                lax.psum((part_sum * factor).astype(jnp.bfloat16), "seq").astype(jnp.float32),
                lax.psum((part_out * factor[..., None]).astype(jnp.bfloat16), "seq").astype(
                    jnp.float32
                ),
            )
            visible = (token_index <= token_step)[None, None, :]
            fresh_scores = (
                jnp.einsum(
                    "rhd,rjhd->hrj",
                    queries,
                    new_keys[layer_index],
                    preferred_element_type=jnp.float32,
                )
                * score_scale
            )
            fresh_scores = jnp.where(visible, fresh_scores, very_negative)
            fresh_max = jnp.max(fresh_scores, axis=2)
            fresh_weights = jnp.where(visible, jnp.exp(fresh_scores - fresh_max[..., None]), 0.0)
            fresh_sum = jnp.sum(fresh_weights, axis=2)
            fresh_out = jnp.einsum(
                "hrj,rjhd->hrd",
                fresh_weights.astype(jnp.bfloat16),
                new_values[layer_index],
                preferred_element_type=jnp.float32,
            )
            joint_max, denom_total, weighted = combine_parts(
                (cache_max, cache_sum, cache_out), (fresh_max, fresh_sum, fresh_out)
            )
            attended = (weighted / denom_total[..., None]).astype(jnp.bfloat16)
            attended = attended.transpose(1, 0, 2).reshape(requests, width_local)
            my_cols = lax.dynamic_slice_in_dim(attended, seq_index * sub_width, sub_width, 1)
            update = jnp.dot(my_cols, w_out[layer_index], preferred_element_type=jnp.float32)
            update = update + jnp.dot(
                activated, w_fc2[layer_index], preferred_element_type=jnp.float32
            )
            hidden_state = hidden_state + full_total(update)
        results.append(hidden_state)
    stacked = jnp.stack(results, axis=1)
    return stacked


def swap_cores(values, seq_count):
    return lax.ppermute(values, "seq", [(i, i ^ 1) for i in range(seq_count)])


def compiler_params(megabytes=32):
    return pltpu.CompilerParams(vmem_limit_bytes=megabytes * 2**20)


def whole(memory_space=pltpu.VMEM):
    return pl.BlockSpec(memory_space=memory_space)


def layer_block(layer_index, shape):
    return pl.BlockSpec((1,) + shape, lambda step: (layer_index,) + (0,) * len(shape))


def same_block(shape):
    return pl.BlockSpec(shape, lambda step: (0,) * len(shape))


def order_kernel(new_tokens, group_ref, prefix_ref, tail_ref, map_ref, rank_ref, position_ref, visit_ref, count_ref):
    requests = group_ref.shape[0]
    groups = prefix_ref.shape[0]
    per_group = requests // groups
    blocks = map_ref.shape[1]
    for group in range(groups):
        count_ref[group] = 0

    def place(request, unused):
        group = group_ref[request]
        seat = count_ref[group]
        count_ref[group] = seat + 1
        rank = group * per_group + seat
        rank_ref[request] = rank
        start = prefix_ref[group] + tail_ref[request]
        for token in range(new_tokens):
            position_ref[rank * new_tokens + token] = start + token
        return unused

    lax.fori_loop(0, requests, place, 0)

    def look(block, unused):
        segment, depth = map_ref[0, block], map_ref[1, block]
        is_tail = segment >= groups
        request = jnp.clip(segment - groups, 0, requests - 1)
        prompt = jnp.clip(segment, 0, groups - 1)
        seat = rank_ref[request]
        first = jnp.where(is_tail, (seat % per_group) * new_tokens, 0)
        length = jnp.where(is_tail, tail_ref[request], prefix_ref[prompt])
        visit_ref[block] = jnp.where(is_tail, seat // per_group, prompt)
        visit_ref[blocks + block] = jnp.where(segment < 0, 0, length - depth * BLOCK)
        visit_ref[2 * blocks + block] = first
        visit_ref[3 * blocks + block] = jnp.where(is_tail, first + new_tokens, per_group * new_tokens)
        return unused

    lax.fori_loop(0, blocks, look, 0)


def order_requests(group_of, prefix_len, tail_len, block_map, new_tokens):
    requests = group_of.shape[0]
    smem = whole(pltpu.SMEM)
    return pl.pallas_call(
        functools.partial(order_kernel, new_tokens),
        out_shape=(
            jax.ShapeDtypeStruct((requests,), jnp.int32),
            jax.ShapeDtypeStruct((requests * new_tokens,), jnp.int32),
            jax.ShapeDtypeStruct((4 * block_map.shape[0],), jnp.int32),
        ),
        in_specs=[smem] * 4,
        out_specs=(smem, smem, smem),
        scratch_shapes=[pltpu.SMEM((prefix_len.shape[0],), jnp.int32)],
        name="order_requests",
    )(group_of, prefix_len, tail_len, block_map.T)


def embed_kernel(place_ref, token_ref, group_ref, table_hbm, near_ref, far_ref, table_ref, hot_ref, semaphores):
    core = place_ref[0] % 2
    first = place_ref[1] * table_ref.shape[0]
    new_tokens, requests = token_ref.shape
    rows = 2 * near_ref.shape[0]
    cuts = semaphores.shape[0]
    width = table_ref.shape[1] // cuts
    columns = [slice(cut * width, (cut + 1) * width) for cut in range(cuts)]
    copies = [
        pltpu.make_async_copy(table_hbm.at[:, column], table_ref.at[:, column], semaphores.at[cut])
        for cut, column in enumerate(columns)
    ]
    for copy in copies:
        copy.start()
    across = lax.broadcasted_iota(jnp.int32, (requests, requests), 1)
    down = lax.broadcasted_iota(jnp.int32, (requests, requests), 0)
    group_row = group_ref[0:1, :]
    group_column = jnp.sum(jnp.where(across == down, group_row, 0), axis=1, keepdims=True)
    ahead = (group_column < group_row) | ((group_column == group_row) & (down < across))
    rank_row = jnp.sum(jnp.where(ahead, 1, 0), axis=0, keepdims=True)
    line = lax.broadcasted_iota(jnp.int32, (rows, requests), 0)
    half, share = rows // 2, rows // CHIPS // 2
    parity = jnp.where(line < half, core, 1 - core)
    line = line % half
    line = ((line // share) * 2 + parity) * share + line % share
    ids = jnp.zeros((rows, 1), jnp.int32)
    for token in range(new_tokens):
        token_row = token_ref[token : token + 1, :]
        match = (rank_row == line // new_tokens) & (line % new_tokens == token)
        ids = ids + jnp.sum(jnp.where(match, token_row, 0), axis=1, keepdims=True)
    entry = lax.broadcasted_iota(jnp.int32, hot_ref.shape, 1)
    hot_ref[...] = jnp.where(entry == ids - first, 1.0, 0.0).astype(jnp.bfloat16)
    for copy, column in zip(copies, columns):
        copy.wait()
        chosen = jnp.dot(hot_ref[...], table_ref[:, column], preferred_element_type=jnp.float32)
        chosen = chosen.astype(jnp.bfloat16)
        near_ref[:, column] = chosen[:half]
        far_ref[:, column] = chosen[half:]


def embed(place, token_ids, group_of, embedding):
    rows = token_ids.shape[0] * token_ids.shape[1]
    half = jax.ShapeDtypeStruct((rows // 2, embedding.shape[1]), jnp.bfloat16)
    return pl.pallas_call(
        embed_kernel,
        out_shape=(half, half),
        in_specs=[whole(pltpu.SMEM), whole(), whole(), whole(pltpu.HBM)],
        out_specs=(whole(), whole()),
        scratch_shapes=[
            pltpu.VMEM(embedding.shape, jnp.bfloat16),
            pltpu.VMEM((rows, embedding.shape[0]), jnp.bfloat16),
            pltpu.SemaphoreType.DMA((4,)),
        ],
        compiler_params=compiler_params(56),
        name="embed",
    )(place, token_ids.T, group_of[None, :], embedding)


def state_total(part_ref, state_ref):
    total = part_ref[0].astype(jnp.float32)
    for source in range(1, part_ref.shape[0]):
        total = total + part_ref[source].astype(jnp.float32)
    if state_ref is not None:
        total = total + state_ref[...]
    return total


def norm_kernel(has_state, layer_index, tp_count, *refs):
    if has_state:
        part_ref, state_ref, gain_ref, bias_ref, next_ref, cut_ref = refs
    else:
        part_ref, gain_ref, bias_ref, next_ref, cut_ref = refs
        state_ref = None
    state = state_total(part_ref, state_ref)
    next_ref[...] = state
    average = jnp.mean(state, axis=-1, keepdims=True)
    centred = state - average
    variance = jnp.mean(centred * centred, axis=-1, keepdims=True)
    gain = gain_ref[layer_index : layer_index + 1, :]
    bias = bias_ref[layer_index : layer_index + 1, :]
    normed = (centred * lax.rsqrt(variance + 1e-05) * gain + bias).astype(jnp.bfloat16)
    width = cut_ref.shape[2]
    for place in range(cut_ref.shape[0]):
        start = (place // tp_count) * width
        cut_ref[place] = normed[:, start : start + width]


def norm_rows(parts, state, ln_gain, ln_bias, layer_index, devices, tp_count):
    count, rows, width = parts.shape
    cut = width // (devices // tp_count)
    operands = [parts] + ([] if state is None else [state]) + [ln_gain, ln_bias]
    return pl.pallas_call(
        functools.partial(norm_kernel, state is not None, layer_index, tp_count),
        out_shape=(
            jax.ShapeDtypeStruct((rows, width), jnp.float32),
            jax.ShapeDtypeStruct((devices, rows, cut), jnp.bfloat16),
        ),
        in_specs=[whole()] * len(operands),
        out_specs=(whole(), whole()),
        compiler_params=compiler_params(16),
        name="norm_rows",
    )(*operands)


def gather_kernel(tp_count, place_ref, part_ref, state_ref, out_ref):
    total = part_ref[0].astype(jnp.float32)
    for chip in range(1, part_ref.shape[0]):
        total = total + part_ref[chip].astype(jnp.float32)
    mine = state_ref.shape[0]
    owner = place_ref[1] % tp_count
    for place in range(tp_count):
        rows = slice(place * mine, (place + 1) * mine)
        total_rows = total[rows] + jnp.where(owner == place, 1.0, 0.0) * state_ref[...]
        out_ref[rows] = total_rows


def gather_rows(place, parts, state, tp_count):
    return pl.pallas_call(
        functools.partial(gather_kernel, tp_count),
        out_shape=jax.ShapeDtypeStruct(parts.shape[1:], jnp.float32),
        in_specs=[whole(pltpu.SMEM), whole(), whole()],
        out_specs=whole(),
        compiler_params=compiler_params(16),
        name="gather_rows",
    )(place, parts, state)


def last_kernel(a_ref, b_ref, c_ref, d_ref, out_ref):
    near = a_ref[...].astype(jnp.float32) + b_ref[...].astype(jnp.float32)
    far = c_ref[...].astype(jnp.float32) + d_ref[...].astype(jnp.float32)
    total = (near + far).astype(jnp.bfloat16)
    for place in range(out_ref.shape[0]):
        out_ref[place] = total


def last_rows(parts):
    return pl.pallas_call(
        last_kernel,
        out_shape=jax.ShapeDtypeStruct((CHIPS,) + parts[0].shape, jnp.bfloat16),
        in_specs=[whole()] * 4,
        out_specs=whole(),
        compiler_params=compiler_params(16),
        name="last_rows",
    )(*parts)


def project_kernel(joins, place_ref, hidden_ref, qkv_ref, fc1_ref, *refs):
    if joins:
        arrived_ref, head_ref, *unit_refs = refs
    else:
        out_ref = refs[0]
    seq_index = place_ref[0]
    parity = seq_index % 2 if joins else 1 - seq_index % 2
    here = seq_index // 2
    rows, depth = hidden_ref.shape
    width = qkv_ref.shape[1] // 3
    unit = fc1_ref.shape[2] // CHIPS // 2
    share = rows // CHIPS // 2
    half = rows // 2
    pieces = width // unit
    hidden = hidden_ref[...]
    tall = 2 * pieces * share

    def joined(values, start):
        if joins:
            values = values + arrived_ref[start : start + values.shape[0]].astype(jnp.float32)
        return values.astype(jnp.bfloat16)

    picked = jnp.concatenate(
        [
            hidden_ref[pl.ds(pl.multiple_of((2 * chip + parity) * share, share), share), :]
            for chip in range(CHIPS)
        ],
        axis=0,
    )
    heads = jnp.dot(picked, qkv_ref[...], preferred_element_type=jnp.float32)
    for piece in range(pieces):
        start = piece * half
        query = joined(heads[:, piece * unit : (piece + 1) * unit], start)
        if joins:
            for chip in range(CHIPS):
                head_ref[chip, tall + start : tall + start + half] = query
        else:
            out_ref[start : start + half] = query
    base = pieces * half
    for chip in range(CHIPS):
        for piece in range(2 * pieces):
            column = width + piece * unit
            start = base + (chip * 2 * pieces + piece) * share
            value = joined(heads[chip * share : (chip + 1) * share, column : column + unit], start)
            if joins:
                head_ref[chip, piece * share : (piece + 1) * share] = value
            else:
                out_ref[start : start + share] = value
    base = base + CHIPS * tall
    for distance in range(CHIPS):
        target = 2 * (here ^ distance) + parity
        columns = pl.ds(pl.multiple_of(target * unit, unit), unit)
        start = base + distance * rows
        pre = joined(jnp.dot(hidden, fc1_ref[0, :, columns], preferred_element_type=jnp.float32), start)
        if joins:
            unit_refs[distance][...] = pre
        else:
            out_ref[start : start + rows] = pre


def project(place, hidden, weights_qkv, w_fc1, layer_index, arrived=None):
    rows = hidden.shape[0]
    unit = w_fc1.shape[2] // CHIPS // 2
    pieces = weights_qkv.shape[1] // 3 // unit
    tall = 2 * pieces * (rows // CHIPS // 2)
    common = pieces * (rows // 2)

    def result(*shape):
        return jax.ShapeDtypeStruct(shape, jnp.bfloat16)

    if arrived is None:
        extra = []
        out_shape = result(common + CHIPS * (tall + rows), unit)
    else:
        extra = [arrived]
        out_shape = (result(CHIPS, tall + common, unit),) + (result(rows, unit),) * CHIPS
    return pl.pallas_call(
        functools.partial(project_kernel, arrived is not None),
        grid=(1,),
        out_shape=out_shape,
        in_specs=[
            whole(pltpu.SMEM),
            same_block(hidden.shape),
            same_block(weights_qkv.shape),
            layer_block(layer_index, w_fc1.shape[1:]),
        ]
        + [same_block(values.shape) for values in extra],
        out_specs=jax.tree.map(lambda leaf: same_block(leaf.shape), out_shape),
        compiler_params=compiler_params(),
        name="project",
    )(place, hidden, weights_qkv, w_fc1, *extra)


def activate_kernel(place_ref, part_ref, table_ref, query_ref, key_ref, value_ref):
    total = part_ref[0].astype(jnp.float32)
    for chip in range(1, part_ref.shape[0]):
        total = total + part_ref[chip].astype(jnp.float32)
    share, width = key_ref.shape
    half = query_ref.shape[0]
    unit = part_ref.shape[2]
    lanes = table_ref.shape[2]
    pieces = width // unit
    own = pl.ds(pl.multiple_of((place_ref[0] // 2) * share, share), share)

    def put(target_ref, start, height, span, scale):
        for piece in range(pieces):
            for column in range(0, unit, lanes):
                first = start + piece * height
                values = total[first : first + height, column : column + lanes]
                if span is not None:
                    values = (
                        values * table_ref[0, span]
                        + pltpu.roll(values, lanes - ROT // 2, 1) * table_ref[1, span]
                        + pltpu.roll(values, ROT // 2, 1) * table_ref[2, span]
                    )
                values = values.astype(jnp.bfloat16)
                if scale is not None:
                    values = (values.astype(jnp.float32) * scale).astype(jnp.bfloat16)
                column_out = piece * unit + column
                target_ref[:, column_out : column_out + lanes] = values

    put(key_ref, 0, share, own, None)
    put(value_ref, pieces * share, share, None, None)
    put(query_ref, 2 * pieces * share, half, slice(None), 1.0 / math.sqrt(HEAD_DIM))


def activate(place, parts, tables, width):
    half = tables.shape[1]
    small = jax.ShapeDtypeStruct((half // CHIPS, width), jnp.bfloat16)
    return pl.pallas_call(
        activate_kernel,
        out_shape=(jax.ShapeDtypeStruct((half, width), jnp.bfloat16), small, small),
        in_specs=[whole(pltpu.SMEM), whole(), whole()],
        out_specs=(whole(),) * 3,
        compiler_params=compiler_params(16),
        name="activate",
    )(place, parts, tables)


def rotary_tables(positions, width):
    half = ROT // 2
    feature = lax.broadcasted_iota(jnp.int32, (1, width), 1) % HEAD_DIM
    frequency = jnp.exp((feature % half).astype(jnp.float32) * (-2.0 * math.log(10000.0) / ROT))
    angles = positions.astype(jnp.float32)[:, None] * frequency
    cosine, sine = jnp.cos(angles), jnp.sin(angles)
    return jnp.stack(
        [
            jnp.where(feature < ROT, cosine, 1.0),
            jnp.where(feature < half, -sine, 0.0),
            jnp.where((feature >= half) & (feature < ROT), sine, 0.0),
        ]
    )


def attend_kernel(
    layer_index, new_tokens,
    place_ref, visit_ref, query_ref, far_query_ref, new_key_ref, new_value_ref,
    key_hbm, value_hbm, out_ref,
    key_ref, value_ref, both_ref, score_ref, top_ref, sum_ref, mix_ref, semaphores,
):
    blocks = visit_ref.shape[0] // 4
    groups, tall, lanes = mix_ref.shape
    share = new_key_ref.shape[0]
    heads = tall // share
    chunks = semaphores.shape[1]
    chunk = key_ref.shape[0] // chunks

    def copy(kind, index):
        span = pl.ds(index * chunk, chunk)
        source, target = ((key_hbm, key_ref), (value_hbm, value_ref))[kind]
        return pltpu.make_async_copy(
            source.at[layer_index, span], target.at[span], semaphores.at[kind, index]
        )

    for kind in range(2):
        for index in range(chunks):
            copy(kind, index).start()
    core = place_ref[0] % 2
    for chip in range(groups // 2):
        span = slice(chip * share, (chip + 1) * share)
        both_ref[2 * chip + core] = query_ref[span]
        both_ref[2 * chip + 1 - core] = far_query_ref[span]
    lane = lax.broadcasted_iota(jnp.int32, (share, lanes), 1)
    row = lax.broadcasted_iota(jnp.int32, (share, lanes), 0)
    top_ref[...] = jnp.full(top_ref.shape, very_negative, jnp.float32)
    sum_ref[...] = jnp.zeros(sum_ref.shape, jnp.float32)
    mix_ref[...] = jnp.zeros(mix_ref.shape, jnp.float32)

    def score(index, group, keys, mask):
        scores = []
        for pair in range(heads // 2):
            both = both_ref[group, :, pair * lanes : (pair + 1) * lanes]
            none = jnp.zeros_like(both)
            split = jnp.concatenate(
                [jnp.where(lane < HEAD_DIM, both, none), jnp.where(lane < HEAD_DIM, none, both)], axis=0
            )
            scores.append(
                lax.dot_general(
                    split, keys[:, pair * lanes : (pair + 1) * lanes], (((1,), (1,)), ((), ())),
                    preferred_element_type=jnp.float32,
                )
            )
        scores = jnp.concatenate(scores, axis=0).reshape(heads, share, BLOCK)
        scores = jnp.where(mask[None], scores, very_negative).reshape(tall, BLOCK)
        score_ref[index] = scores
        top_ref[group] = jnp.maximum(top_ref[group], scores)

    def mix(index, group, values):
        weight = jnp.exp(score_ref[index] - top_ref[group])
        sum_ref[group] += weight
        rounded = weight.astype(jnp.bfloat16)
        mix_ref[group] += jnp.concatenate(
            [
                jnp.dot(
                    rounded[pair * 2 * share : (pair + 1) * 2 * share],
                    values[:, pair * lanes : (pair + 1) * lanes],
                    preferred_element_type=jnp.float32,
                )
                for pair in range(heads // 2)
            ],
            axis=0,
        )

    own = place_ref[0]
    fill = jnp.zeros((BLOCK - share, new_key_ref.shape[1]), jnp.bfloat16)
    score(
        blocks, own, jnp.concatenate([new_key_ref[...], fill], axis=0),
        (lane // new_tokens == row // new_tokens) & (lane <= row),
    )
    owners = []
    for block in range(blocks):
        if (block * BLOCK) % chunk == 0:
            copy(0, block * BLOCK // chunk).wait()
        group, live, first, end = (visit_ref[field * blocks + block] for field in range(4))
        owners.append(group)
        score(
            block, group, key_ref[block * BLOCK : (block + 1) * BLOCK, :],
            (lane < live) & (row >= first) & (row < end),
        )
    for group in range(groups):
        top = jnp.max(top_ref[group], axis=1, keepdims=True)
        top_ref[group] = jnp.broadcast_to(top, (tall, lanes))
    mix(blocks, own, jnp.concatenate([new_value_ref[...], fill], axis=0))
    for block in range(blocks):
        if (block * BLOCK) % chunk == 0:
            copy(1, block * BLOCK // chunk).wait()
        mix(block, owners[block], value_ref[block * BLOCK : (block + 1) * BLOCK, :])

    level = jnp.zeros((tall, lanes), jnp.float32)
    column = lax.broadcasted_iota(jnp.int32, (tall, lanes), 1)

    def mean(group):
        total = jnp.sum(sum_ref[group], axis=1, keepdims=True)
        total = jnp.where(total <= 0.0, 1.0, total)
        own_level = jnp.where(column == group, top_ref[group] + jnp.log(total), 0.0)
        return mix_ref[group] / total, own_level

    for group in range(groups // 2):
        left, left_level = mean(group)
        right, right_level = mean(group + groups // 2)
        level = level + left_level + right_level
        for head in range(heads):
            rows = slice(head * share, (head + 1) * share)
            first, second = left[rows], right[rows]
            if head % 2:
                first = pltpu.roll(first, HEAD_DIM, 1)
            else:
                second = pltpu.roll(second, HEAD_DIM, 1)
            packed = jnp.where(lane < HEAD_DIM, first, second)
            out_ref[head, group * share : (group + 1) * share] = packed.astype(jnp.bfloat16)
    level = level.T[:groups]
    high = level.astype(jnp.bfloat16).astype(jnp.float32)
    middle = (level - high).astype(jnp.bfloat16).astype(jnp.float32)
    low = level - high - middle
    rest = jnp.concatenate([high, middle, low, jnp.zeros_like(low)], axis=0).astype(jnp.bfloat16)
    start = (groups // 2) * share
    for head in range(heads):
        column = head * share // lanes * lanes
        out_ref[head, start:] = rest[:, column : column + lanes]


def attend(place, visits, query, far_query, new_key, new_value, k_cache, v_cache, layer_index, new_tokens, groups):
    width = query.shape[1]
    rows = 2 * query.shape[0]
    slots = k_cache.shape[1]
    heads = width // HEAD_DIM
    share = rows // groups
    tall = heads * share
    lanes = 2 * HEAD_DIM
    chunks = 4
    state = pltpu.VMEM((groups, tall, lanes), jnp.float32)
    return pl.pallas_call(
        functools.partial(attend_kernel, layer_index, new_tokens),
        out_shape=jax.ShapeDtypeStruct((heads, rows // 2 + 4 * groups, lanes), jnp.bfloat16),
        in_specs=[whole(pltpu.SMEM)] * 2 + [whole()] * 4 + [whole(pltpu.HBM)] * 2,
        out_specs=whole(),
        scratch_shapes=[
            pltpu.VMEM((slots, width), jnp.bfloat16),
            pltpu.VMEM((slots, width), jnp.bfloat16),
            pltpu.VMEM((groups, share, width), jnp.bfloat16),
            pltpu.VMEM((visits.shape[0] // 4 + 1, tall, BLOCK), jnp.float32),
            state,
            state,
            state,
            pltpu.SemaphoreType.DMA((2, chunks)),
        ],
        compiler_params=compiler_params(24),
        name="attend",
    )(place, visits, query, far_query, new_key, new_value, k_cache, v_cache)


def update_kernel(
    layer_index, other, place_ref, part_ref, bias_ref, out_weight_ref, fc2_ref, *refs
):
    *unit_refs, out_ref, scale_ref = refs
    seq_index = place_ref[0]
    parity = 1 - seq_index % 2 if other else seq_index % 2
    sources, tall, lanes = part_ref.shape
    unit = unit_refs[0].shape[1]
    share = unit_refs[0].shape[0] // sources
    groups = (tall - (sources // 2) * share) // 4
    levels = []
    for source in range(sources):
        parts = part_ref[source, (sources // 2) * share :, :].astype(jnp.float32)
        levels.append(parts[:groups] + parts[groups : 2 * groups] + parts[2 * groups : 3 * groups])
    top = functools.reduce(jnp.maximum, levels)
    scales = [jnp.exp(level - top) for level in levels]
    total = functools.reduce(jnp.add, scales)
    scales = [scale / total for scale in scales]
    blank = jnp.zeros((lanes - groups * sources, lanes), jnp.float32)
    scale_ref[...] = jnp.concatenate(scales + [blank], axis=0).T
    place = seq_index % (lanes // share)
    scale = scale_ref[pl.ds(pl.multiple_of(place * share, share), share), :]
    scale = jnp.where(parity == 0, scale, pltpu.roll(scale, lanes - 1, 1))
    lane = lax.broadcasted_iota(jnp.int32, (share, lanes), 1)
    first, second = [], []
    for pair in range(CHIPS // 2):
        rows = pl.ds(pl.multiple_of((2 * pair + parity) * share, share), share)
        mixed = jnp.zeros((share, lanes), jnp.float32)
        for source in range(sources):
            column = source * groups + 2 * pair
            left = scale[:, column : column + 1]
            right = scale[:, column + groups // 2 : column + groups // 2 + 1]
            mixed = mixed + part_ref[source, rows, :].astype(jnp.float32) * jnp.where(
                lane < HEAD_DIM, left, right
            )
        first.append(mixed[:, :HEAD_DIM])
        second.append(pltpu.roll(mixed, HEAD_DIM, 1)[:, :HEAD_DIM])
    attended = jnp.concatenate(first + second, axis=0).astype(jnp.bfloat16)
    bias = bias_ref[
        layer_index : layer_index + 1, pl.ds(pl.multiple_of(seq_index * unit, unit), unit)
    ]
    hidden = []
    for piece in range(CHIPS):
        rows = pl.ds(pl.multiple_of((2 * piece + parity) * share, share), share)
        pre = functools.reduce(jnp.add, [ref[rows, :].astype(jnp.float32) for ref in unit_refs])
        hidden.append(jax.nn.gelu(pre + bias, approximate=True).astype(jnp.bfloat16))
    out_ref[...] = (
        jnp.dot(attended, out_weight_ref[0], preferred_element_type=jnp.float32)
        + jnp.dot(jnp.concatenate(hidden, axis=0), fc2_ref[0], preferred_element_type=jnp.float32)
    ).astype(jnp.bfloat16)


def update(place, parts, units, b_fc1, w_out, w_fc2, layer_index, other):
    rows = units[0].shape[0] // 2
    width = w_out.shape[2]
    lanes = parts.shape[2]
    return pl.pallas_call(
        functools.partial(update_kernel, layer_index, other),
        grid=(1,),
        out_shape=jax.ShapeDtypeStruct((rows, width), jnp.bfloat16),
        in_specs=[
            whole(pltpu.SMEM),
            same_block(parts.shape),
            same_block(b_fc1.shape),
            layer_block(layer_index, w_out.shape[1:]),
            layer_block(layer_index, w_fc2.shape[1:]),
        ]
        + [same_block(units[0].shape)] * len(units),
        out_specs=same_block((rows, width)),
        scratch_shapes=[pltpu.VMEM((lanes, lanes), jnp.float32)],
        compiler_params=compiler_params(),
        name="update",
    )(place, parts, b_fc1, w_out, w_fc2, *units)


def per_device(
    token_ids, embedding, group_of, prefix_len, tail_len, block_map, k_cache, v_cache,
    ln_gain, ln_bias, w_qkv, w_fc1, b_fc1, w_out, w_fc2,
):
    seq_count, tp_count = lax.axis_size("seq"), lax.axis_size("tp")
    seq_index, tp_index = lax.axis_index("seq"), lax.axis_index("tp")
    devices = seq_count * tp_count
    core = seq_index % 2
    place = jnp.stack([seq_index, seq_index * tp_count + tp_index]).astype(jnp.int32)
    requests, new_tokens = token_ids.shape
    rows = requests * new_tokens
    groups = prefix_len.shape[0]
    share = rows // seq_count
    mine = rows // devices
    width = embedding.shape[1]
    width_local = k_cache.shape[2]
    same_core = [[s * tp_count + p for s in range(c, seq_count, 2) for p in range(tp_count)] for c in range(2)]
    same_core_seq = [list(range(c, seq_count, 2)) for c in range(2)]

    def to_owners(half):
        parts = half.reshape(devices // 2, mine, width)
        return lax.all_to_all(parts, ("seq", "tp"), 0, 0, axis_index_groups=same_core)

    def to_chips(parts):
        return lax.all_to_all(parts, "seq", 0, 0, axis_index_groups=same_core_seq)

    near, far = embed(place, token_ids, group_of, embedding)
    parts = to_owners(near + swap_cores(far, seq_count))
    rank, positions, visits = order_requests(group_of, prefix_len, tail_len, block_map, new_tokens)
    own_positions = lax.dynamic_index_in_dim(positions.reshape(CHIPS, 2, share), core, 1, keepdims=False)
    tables = rotary_tables(own_positions.reshape(-1), 2 * HEAD_DIM)
    parts, tables, visits = lax.optimization_barrier((parts, tables, visits))
    state = None
    for layer_index in range(LAYERS):
        weights_qkv = w_qkv[layer_index].reshape(w_qkv.shape[1], -1)
        state, cut = norm_rows(parts, state, ln_gain, ln_bias, layer_index, devices, tp_count)
        hidden = lax.all_to_all(cut, ("seq", "tp"), 0, 0).reshape(rows, -1)
        arriving = swap_cores(project(place, hidden, weights_qkv, w_fc1, layer_index), seq_count)
        heads, *units = project(place, hidden, weights_qkv, w_fc1, layer_index, arriving)
        query, new_key, new_value = activate(place, to_chips(heads), tables, width_local)
        query, *units = lax.optimization_barrier((query, *units))
        units = units[:1] + [
            lax.ppermute(units[k], "seq", [(i, i ^ (2 * k)) for i in range(seq_count)])
            for k in range(1, CHIPS)
        ]
        parts = attend(
            place, visits, query, swap_cores(query, seq_count), new_key, new_value,
            k_cache, v_cache, layer_index, new_tokens, groups,
        )
        parts = lax.all_to_all(parts, "seq", 0, 0)
        arriving = swap_cores(update(place, parts, units, b_fc1, w_out, w_fc2, layer_index, True), seq_count)
        half = update(place, parts, units, b_fc1, w_out, w_fc2, layer_index, False) + arriving
        if layer_index < LAYERS - 1:
            parts = to_owners(half)
    last = gather_rows(place, to_chips(half.reshape(CHIPS, share, width)), state, tp_count)
    last = last.astype(jnp.bfloat16)
    last = [last] + [
        lax.ppermute(last, "tp", [(i, i ^ k) for i in range(tp_count)]) for k in range(1, tp_count)
    ]
    last = to_chips(last_rows(last)).reshape(rows // 2, width)
    arriving = swap_cores(last, seq_count)
    wanted = (rank[:, None] * new_tokens + jnp.arange(new_tokens, dtype=jnp.int32)[None, :]).reshape(-1)
    index = jnp.arange(rows // 2, dtype=jnp.int32)

    def placed(half, parity):
        held = (2 * (index // share) + parity) * share + index % share
        hot = (wanted[:, None] == held[None, :]).astype(jnp.bfloat16)
        return jnp.dot(hot, half, preferred_element_type=jnp.float32)

    return (placed(last, core) + placed(arriving, 1 - core)).reshape(requests, new_tokens, width)


def solution(mesh):
    in_specs = (
        P(),
        P(("seq", "tp"), None),
        P(),
        P(),
        P(),
        P("seq", None),
        P(None, "seq", "tp"),
        P(None, "seq", "tp"),
        P(),
        P(),
        P(None, "seq", None, "tp"),
        P(None, "seq", "tp"),
        P(None, "tp"),
        P(None, ("tp", "seq"), None),
        P(None, ("tp", "seq"), None),
    )
    out_specs = P()
    seq_count, tp_count = mesh.shape["seq"], mesh.shape["tp"]
    fits = tp_count == 4 and seq_count == HEADS // tp_count and seq_count == 2 * CHIPS
    return jax.shard_map(
        per_device if fits else per_device_any, mesh=mesh, in_specs=in_specs, out_specs=out_specs, check_vma=False
    )
```

```python
import functools
import math

import jax
import jax.numpy as jnp
from jax import lax
from jax.experimental import pallas as pl
from jax.experimental.pallas import tpu as pltpu
from jax.sharding import PartitionSpec as P

HEADS = 32
HEAD_DIM = 64
ROT = 32
LAYERS = 2
BLOCK = 128
SPAN = 512
CHIPS = 4
LANES = 128


very_negative = -1e30


def layer_norm(values, gain_row, bias_row):
    average = jnp.mean(values, axis=-1, keepdims=True)
    centred = values - average
    variance = jnp.mean(centred * centred, axis=-1, keepdims=True)
    return centred * lax.rsqrt(variance + 1e-05) * gain_row + bias_row


def rotary(values, positions):
    half_width = ROT // 2
    frequency = jnp.exp(
        jnp.arange(half_width, dtype=jnp.float32) * (-2.0 * math.log(10000.0) / ROT)
    )
    angles = positions.astype(jnp.float32)[:, None] * frequency[None, :]
    cosine = jnp.cos(angles)[:, None, :]
    sine_part = jnp.sin(angles)[:, None, :]
    low_half = values[..., :half_width]
    high_half = values[..., half_width:ROT]
    return jnp.concatenate(
        [
            low_half * cosine - high_half * sine_part,
            high_half * cosine + low_half * sine_part,
            values[..., ROT:],
        ],
        axis=-1,
    )


def combine_parts(left_part, right_part):
    max_left, sum_left, out_left = left_part
    max_right, sum_right, out_right = right_part
    top_value = jnp.maximum(max_left, max_right)
    scale_left = jnp.exp(max_left - top_value)
    scale_right = jnp.exp(max_right - top_value)
    return (
        top_value,
        sum_left * scale_left + sum_right * scale_right,
        out_left * scale_left[..., None] + out_right * scale_right[..., None],
    )


def full_total(values):
    return lax.psum(values, ("seq", "tp"))


def per_device_any(
    token_ids,
    embedding,
    group_of,
    prefix_len,
    tail_len,
    block_map,
    k_cache,
    v_cache,
    ln_gain,
    ln_bias,
    w_qkv,
    w_fc1,
    b_fc1,
    w_out,
    w_fc2,
):
    tp_count = lax.axis_size("tp")
    seq_index = lax.axis_index("seq")
    tp_index = lax.axis_index("tp")
    requests = token_ids.shape[0]
    new_tokens = token_ids.shape[1]
    groups = prefix_len.shape[0]
    heads_local = HEADS // tp_count
    width_local = heads_local * HEAD_DIM
    score_scale = 1.0 / math.sqrt(HEAD_DIM)
    vocab_rows = embedding.shape[0]
    first_row = (seq_index * tp_count + tp_index) * vocab_rows
    local_ids = token_ids.reshape(-1) - first_row
    inside = (local_ids >= 0) & (local_ids < vocab_rows)
    picked = jnp.take(embedding, jnp.clip(local_ids, 0, vocab_rows - 1), axis=0).astype(jnp.float32)
    picked = jnp.where(inside[:, None], picked, 0.0)
    start_states = full_total(picked).reshape(requests, new_tokens, -1)
    group_hit = group_of[:, None] == jnp.arange(groups, dtype=jnp.int32)[None, :]
    shared_len = jnp.sum(jnp.where(group_hit, prefix_len[None, :], 0), axis=1)
    base_positions = shared_len + tail_len
    seg_len = jnp.concatenate([prefix_len, tail_len])
    seg_count = seg_len.shape[0]
    blocks_local = block_map.shape[0]
    seg_blk = block_map[:, 0]
    rank_blk = block_map[:, 1]
    seg_hit = seg_blk[:, None] == jnp.arange(seg_count, dtype=jnp.int32)[None, :]
    len_blk = jnp.sum(jnp.where(seg_hit, seg_len[None, :], 0), axis=1)
    slot_positions = rank_blk[:, None] * BLOCK + jnp.arange(BLOCK, dtype=jnp.int32)[None, :]
    live_slot = ((seg_blk[:, None] >= 0) & (slot_positions < len_blk[:, None])).reshape(-1)
    seg_slot = jnp.broadcast_to(seg_blk[:, None], (blocks_local, BLOCK)).reshape(-1)
    own_tail = seg_slot[None, :] == (groups + jnp.arange(requests, dtype=jnp.int32))[:, None]
    own_prompt = seg_slot[None, :] == group_of[:, None]
    allowed = (own_tail | own_prompt) & live_slot[None, :]
    step_count = allowed.shape[1] // SPAN
    allowed_steps = allowed.reshape(requests, step_count, SPAN).transpose(1, 0, 2)
    rows_local = w_qkv.shape[1]
    unit_count = w_fc2.shape[1]
    sub_width = w_out.shape[1]
    token_index = jnp.arange(new_tokens, dtype=jnp.int32)
    new_keys = [
        jnp.zeros((requests, new_tokens, heads_local, HEAD_DIM), jnp.bfloat16)
        for layer_index in range(LAYERS)
    ]
    new_values = [
        jnp.zeros((requests, new_tokens, heads_local, HEAD_DIM), jnp.bfloat16)
        for layer_index in range(LAYERS)
    ]
    results = []
    for token_step in range(new_tokens):
        hidden_state = start_states[:, token_step]
        positions = base_positions + token_step
        for layer_index in range(LAYERS):
            normed = layer_norm(hidden_state, ln_gain[layer_index], ln_bias[layer_index]).astype(
                jnp.bfloat16
            )
            my_rows = lax.dynamic_slice_in_dim(normed, seq_index * rows_local, rows_local, 1)
            part_proj = jnp.dot(
                my_rows,
                w_qkv[layer_index].reshape(rows_local, -1),
                preferred_element_type=jnp.float32,
            )
            part_fc1 = jnp.dot(my_rows, w_fc1[layer_index], preferred_element_type=jnp.float32)
            attention_proj, fc1_all = lax.psum((part_proj, part_fc1), "seq")
            pre_act = lax.dynamic_slice_in_dim(fc1_all, seq_index * unit_count, unit_count, 1)
            pre_act = (
                pre_act
                + lax.dynamic_slice_in_dim(
                    b_fc1[layer_index], seq_index * unit_count, unit_count, 0
                )[None, :]
            )
            activated = jax.nn.gelu(pre_act, approximate=True).astype(jnp.bfloat16)
            attention_proj = attention_proj.reshape(requests, 3, heads_local, HEAD_DIM)
            queries = rotary(attention_proj[:, 0], positions).astype(jnp.bfloat16)
            key_rows = rotary(attention_proj[:, 1], positions).astype(jnp.bfloat16)
            value_rows = attention_proj[:, 2].astype(jnp.bfloat16)
            new_keys[layer_index] = new_keys[layer_index].at[:, token_step].set(key_rows)
            new_values[layer_index] = new_values[layer_index].at[:, token_step].set(value_rows)
            key_steps = k_cache[layer_index].reshape(step_count, SPAN, heads_local, HEAD_DIM)
            value_steps = v_cache[layer_index].reshape(step_count, SPAN, heads_local, HEAD_DIM)

            def cache_step(carry, inputs):
                run_max, run_sum, run_out = carry
                key_block, value_block, allow_block = inputs
                scores = (
                    jnp.einsum(
                        "rhd,shd->hrs", queries, key_block, preferred_element_type=jnp.float32
                    )
                    * score_scale
                )
                scores = jnp.where(allow_block[None], scores, very_negative)
                next_max = jnp.maximum(run_max, jnp.max(scores, axis=2))
                weights = jnp.where(allow_block[None], jnp.exp(scores - next_max[..., None]), 0.0)
                shrink = jnp.exp(run_max - next_max)
                next_sum = run_sum * shrink + jnp.sum(weights, axis=2)
                next_out = run_out * shrink[..., None] + jnp.einsum(
                    "hrs,shd->hrd",
                    weights.astype(jnp.bfloat16),
                    value_block,
                    preferred_element_type=jnp.float32,
                )
                return ((next_max, next_sum, next_out), None)

            start_carry = (
                jnp.full((heads_local, requests), very_negative, jnp.float32),
                jnp.zeros((heads_local, requests), jnp.float32),
                jnp.zeros((heads_local, requests, HEAD_DIM), jnp.float32),
            )
            (part_max, part_sum, part_out), unused = lax.scan(
                cache_step, start_carry, (key_steps, value_steps, allowed_steps)
            )
            cache_max = lax.pmax(part_max, "seq")
            factor = jnp.exp(part_max - cache_max)
            cache_sum, cache_out = (
                lax.psum((part_sum * factor).astype(jnp.bfloat16), "seq").astype(jnp.float32),
                lax.psum((part_out * factor[..., None]).astype(jnp.bfloat16), "seq").astype(
                    jnp.float32
                ),
            )
            visible = (token_index <= token_step)[None, None, :]
            fresh_scores = (
                jnp.einsum(
                    "rhd,rjhd->hrj",
                    queries,
                    new_keys[layer_index],
                    preferred_element_type=jnp.float32,
                )
                * score_scale
            )
            fresh_scores = jnp.where(visible, fresh_scores, very_negative)
            fresh_max = jnp.max(fresh_scores, axis=2)
            fresh_weights = jnp.where(visible, jnp.exp(fresh_scores - fresh_max[..., None]), 0.0)
            fresh_sum = jnp.sum(fresh_weights, axis=2)
            fresh_out = jnp.einsum(
                "hrj,rjhd->hrd",
                fresh_weights.astype(jnp.bfloat16),
                new_values[layer_index],
                preferred_element_type=jnp.float32,
            )
            joint_max, denom_total, weighted = combine_parts(
                (cache_max, cache_sum, cache_out), (fresh_max, fresh_sum, fresh_out)
            )
            attended = (weighted / denom_total[..., None]).astype(jnp.bfloat16)
            attended = attended.transpose(1, 0, 2).reshape(requests, width_local)
            my_cols = lax.dynamic_slice_in_dim(attended, seq_index * sub_width, sub_width, 1)
            update = jnp.dot(my_cols, w_out[layer_index], preferred_element_type=jnp.float32)
            update = update + jnp.dot(
                activated, w_fc2[layer_index], preferred_element_type=jnp.float32
            )
            hidden_state = hidden_state + full_total(update)
        results.append(hidden_state)
    stacked = jnp.stack(results, axis=1)
    return stacked


def swap_cores(values, seq_count):
    return lax.ppermute(values, "seq", [(i, i ^ 1) for i in range(seq_count)])


def in_hbm(values):
    return pltpu.with_memory_space_constraint(values, pltpu.HBM)


def compiler_params(megabytes=32):
    return pltpu.CompilerParams(vmem_limit_bytes=megabytes * 2**20)


def whole(memory_space=pltpu.VMEM):
    return pl.BlockSpec(memory_space=memory_space)


def layer_block(layer_index, shape):
    return pl.BlockSpec((1,) + shape, lambda step: (layer_index,) + (0,) * len(shape))


def same_block(shape):
    return pl.BlockSpec(shape, lambda step: (0,) * len(shape))


def order_kernel(new_tokens, group_ref, prefix_ref, tail_ref, map_ref, rank_ref, position_ref, visit_ref, count_ref):
    requests = group_ref.shape[0]
    groups = prefix_ref.shape[0]
    per_group = requests // groups
    blocks = map_ref.shape[1]
    for group in range(groups):
        count_ref[group] = 0

    def place(request, unused):
        group = group_ref[request]
        seat = count_ref[group]
        count_ref[group] = seat + 1
        rank = group * per_group + seat
        rank_ref[request] = rank
        start = prefix_ref[group] + tail_ref[request]
        for token in range(new_tokens):
            position_ref[rank * new_tokens + token] = start + token
        return unused

    lax.fori_loop(0, requests, place, 0)

    def look(block, unused):
        segment, depth = map_ref[0, block], map_ref[1, block]
        is_tail = segment >= groups
        request = jnp.clip(segment - groups, 0, requests - 1)
        prompt = jnp.clip(segment, 0, groups - 1)
        seat = rank_ref[request]
        first = jnp.where(is_tail, (seat % per_group) * new_tokens, 0)
        length = jnp.where(is_tail, tail_ref[request], prefix_ref[prompt])
        visit_ref[block] = jnp.where(is_tail, seat // per_group, prompt)
        visit_ref[blocks + block] = jnp.where(segment < 0, 0, length - depth * BLOCK)
        visit_ref[2 * blocks + block] = first
        visit_ref[3 * blocks + block] = jnp.where(is_tail, first + new_tokens, per_group * new_tokens)
        return unused

    lax.fori_loop(0, blocks, look, 0)


def order_requests(group_of, prefix_len, tail_len, block_map, new_tokens):
    requests = group_of.shape[0]
    smem = whole(pltpu.SMEM)
    return pl.pallas_call(
        functools.partial(order_kernel, new_tokens),
        out_shape=(
            jax.ShapeDtypeStruct((requests,), jnp.int32),
            jax.ShapeDtypeStruct((requests * new_tokens,), jnp.int32),
            jax.ShapeDtypeStruct((4 * block_map.shape[0],), jnp.int32),
        ),
        in_specs=[smem] * 4,
        out_specs=(smem, smem, smem),
        scratch_shapes=[pltpu.SMEM((prefix_len.shape[0],), jnp.int32)],
        name="order_requests",
    )(group_of, prefix_len, tail_len, block_map.T)


def thirds(values):
    high = values.astype(jnp.bfloat16).astype(jnp.float32)
    middle = (values - high).astype(jnp.bfloat16).astype(jnp.float32)
    return high, middle, values - high - middle


def row_block(rows):
    width = rows[0].shape[1]
    line = lax.broadcasted_iota(jnp.int32, (8, width), 0)
    block = jnp.zeros((8, width), jnp.float32)
    for index, row in enumerate(rows):
        block = jnp.where(line == index, row, block)
    return block


def column_to_row(column):
    return jnp.broadcast_to(column, (column.shape[0], LANES)).T[0:1]


def row_to_column(row):
    return jnp.broadcast_to(row, (LANES, row.shape[1])).T


def ranks(group_ref):
    requests = group_ref.shape[1]
    across = lax.broadcasted_iota(jnp.int32, (requests, requests), 1)
    down = lax.broadcasted_iota(jnp.int32, (requests, requests), 0)
    group_row = group_ref[0:1, :]
    group_column = jnp.sum(jnp.where(across == down, group_row, 0), axis=1, keepdims=True)
    ahead = (group_column < group_row) | ((group_column == group_row) & (down < across))
    return jnp.sum(jnp.where(ahead, 1, 0), axis=0, keepdims=True)


def row_sums(lines):
    block = row_block([part for line in lines for part in thirds(line)])
    return jnp.concatenate([block, jnp.zeros_like(block)], axis=0).astype(jnp.bfloat16)


def from_row_sums(block):
    block = block.astype(jnp.float32)
    line = lax.broadcasted_iota(jnp.int32, block.shape, 0)
    return [
        jnp.sum(jnp.where((line >= start) & (line < start + 3), block, 0.0), axis=0, keepdims=True)
        for start in (0, 3)
    ]


def embed_kernel(
    place_ref, token_ref, group_ref, table_hbm, near_ref, far_ref, own_ref,
    table_ref, hot_ref, row_ref, semaphores,
):
    core = place_ref[0] % 2
    first = place_ref[1] * table_ref.shape[1]
    new_tokens, requests = token_ref.shape
    rows, unit = near_ref.shape[1:]
    copies = []
    for chip in range(CHIPS):
        copies.append(
            pltpu.make_async_copy(
                table_hbm.at[:, pl.ds(chip * 2 * unit, 2 * unit)], table_ref.at[chip], semaphores.at[chip]
            )
        )
        copies[-1].start()
    rank_row = ranks(group_ref)
    line = lax.broadcasted_iota(jnp.int32, (rows, requests), 0)
    ids = jnp.zeros((rows, requests), jnp.int32)
    for token in range(new_tokens):
        match = (rank_row == line // new_tokens) & (line % new_tokens == token)
        ids = jnp.where(match, token_ref[token : token + 1, :], ids)
    ids = jnp.sum(ids, axis=1, keepdims=True) - first
    entry = lax.broadcasted_iota(jnp.int32, hot_ref.shape, 1)
    hot_ref[...] = jnp.where(entry == ids, 1.0, 0.0).astype(jnp.bfloat16)
    total = jnp.zeros((rows, LANES), jnp.float32)
    for chip, copy in enumerate(copies):
        copy.wait()
        chosen = jnp.dot(hot_ref[...], table_ref[chip], preferred_element_type=jnp.float32)
        for start in range(0, 2 * unit, LANES):
            total = total + chosen[:, start : start + LANES]
        chosen = chosen.astype(jnp.bfloat16)
        row_ref[:, chip * 2 * unit : (chip + 1) * 2 * unit] = chosen
        left, right = chosen[:, :unit], chosen[:, unit:]
        near_ref[chip] = jnp.where(core == 0, left, right)
        far_ref[chip * rows : (chip + 1) * rows] = jnp.where(core == 0, right, left)
    features = row_ref.shape[1]
    mean = jnp.sum(total, axis=1, keepdims=True) * (1.0 / features)
    squares = jnp.zeros((rows, LANES), jnp.float32)
    for start in range(0, features, LANES):
        centred = row_ref[:, start : start + LANES].astype(jnp.float32) - mean
        squares = squares + centred * centred
    variance = jnp.sum(squares, axis=1, keepdims=True) * (1.0 / features)
    held = (ids >= 0) & (ids < hot_ref.shape[1])
    scale = jnp.where(held, lax.rsqrt(variance + 1e-05), 0.0)
    mean, scale = column_to_row(mean), column_to_row(scale)
    own_ref[...] = row_block([mean, scale])
    far_ref[CHIPS * rows :] = row_sums([mean, scale])


def embed(place, token_ids, group_of, embedding, unit):
    rows = token_ids.shape[0] * token_ids.shape[1]
    return pl.pallas_call(
        embed_kernel,
        out_shape=(
            jax.ShapeDtypeStruct((CHIPS, rows, unit), jnp.bfloat16),
            pltpu.HBM((CHIPS * rows + 16, unit), jnp.bfloat16),
            jax.ShapeDtypeStruct((8, rows), jnp.float32),
        ),
        in_specs=[whole(pltpu.SMEM), whole(), whole(), whole(pltpu.HBM)],
        out_specs=(whole(),) * 3,
        scratch_shapes=[
            pltpu.VMEM((CHIPS, embedding.shape[0], 2 * unit), jnp.bfloat16),
            pltpu.VMEM((rows, embedding.shape[0]), jnp.bfloat16),
            pltpu.VMEM((rows, embedding.shape[1]), jnp.bfloat16),
            pltpu.SemaphoreType.DMA((CHIPS,)),
        ],
        compiler_params=compiler_params(24),
        name="embed",
    )(in_hbm(place), in_hbm(token_ids.T), in_hbm(group_of[None, :]), in_hbm(embedding))


def join_kernel(near_ref, far_ref, own_ref, out_ref):
    rows = near_ref.shape[1]
    for chip in range(CHIPS):
        far = far_ref[chip * rows : (chip + 1) * rows].astype(jnp.float32)
        out_ref[chip, :rows] = (near_ref[chip].astype(jnp.float32) + far).astype(jnp.bfloat16)
    mean, scale = from_row_sums(far_ref[CHIPS * rows :])
    lines = row_sums([mean + own_ref[0:1, :], scale + own_ref[1:2, :]])
    for chip in range(CHIPS):
        out_ref[chip, rows:] = lines


def join(near, far, own):
    chips, rows, unit = near.shape
    return pl.pallas_call(
        join_kernel,
        out_shape=pltpu.HBM((chips, rows + 16, unit), jnp.bfloat16),
        in_specs=[whole()] * 3,
        out_specs=whole(),
        compiler_params=compiler_params(16),
        name="join",
    )(near, far, own)


def gather_kernel(part_ref, out_ref):
    rows = part_ref.shape[1] - 16
    total = part_ref[0].astype(jnp.float32)
    for chip in range(1, CHIPS):
        total = total + part_ref[chip].astype(jnp.float32)
    out_ref[:rows] = total[:rows].astype(jnp.bfloat16)
    out_ref[rows:] = row_sums(from_row_sums(total[rows:]))


def gather(parts):
    return pl.pallas_call(
        gather_kernel,
        out_shape=jax.ShapeDtypeStruct(parts.shape[1:], jnp.bfloat16),
        in_specs=[whole()],
        out_specs=whole(),
        compiler_params=compiler_params(16),
        name="gather",
    )(parts)


def first_kernel(place_ref, a_ref, b_ref, c_ref, d_ref, gain_ref, bias_ref, start_ref, hidden_ref):
    rows, unit = hidden_ref.shape
    parts = [ref[...].astype(jnp.float32) for ref in (a_ref, b_ref, c_ref, d_ref)]
    total = (parts[0] + parts[1]) + (parts[2] + parts[3])
    mean, scale = (row_to_column(line) for line in from_row_sums(total[rows:]))
    columns = pl.ds(pl.multiple_of(place_ref[0] * unit, unit), unit)
    gain, bias = gain_ref[0:1, columns], bias_ref[0:1, columns]
    for start in range(0, unit, LANES):
        span = slice(start, start + LANES)
        state = total[:rows, span]
        start_ref[:, span] = state.astype(jnp.bfloat16)
        hidden_ref[:, span] = ((state - mean) * scale * gain[:, span] + bias[:, span]).astype(jnp.bfloat16)


def first_hidden(place, parts, ln_gain, ln_bias):
    one = jax.ShapeDtypeStruct((parts[0].shape[0] - 16, parts[0].shape[1]), jnp.bfloat16)
    return pl.pallas_call(
        first_kernel,
        out_shape=(one, one),
        in_specs=[whole(pltpu.SMEM)] + [whole()] * 6,
        out_specs=(whole(), whole()),
        compiler_params=compiler_params(16),
        name="first_hidden",
    )(in_hbm(place), *parts, ln_gain, ln_bias)


def state_total(part_ref, state_ref):
    total = part_ref[0].astype(jnp.float32)
    for source in range(1, part_ref.shape[0]):
        total = total + part_ref[source].astype(jnp.float32)
    if state_ref is not None:
        total = total + state_ref[...]
    return total


def norm_kernel(has_state, layer_index, tp_count, *refs):
    if has_state:
        part_ref, state_ref, gain_ref, bias_ref, next_ref, cut_ref = refs
    else:
        part_ref, gain_ref, bias_ref, next_ref, cut_ref = refs
        state_ref = None
    state = state_total(part_ref, state_ref)
    next_ref[...] = state
    average = jnp.mean(state, axis=-1, keepdims=True)
    centred = state - average
    variance = jnp.mean(centred * centred, axis=-1, keepdims=True)
    gain = gain_ref[layer_index : layer_index + 1, :]
    bias = bias_ref[layer_index : layer_index + 1, :]
    normed = (centred * lax.rsqrt(variance + 1e-05) * gain + bias).astype(jnp.bfloat16)
    width = cut_ref.shape[2]
    for place in range(cut_ref.shape[0]):
        start = (place // tp_count) * width
        cut_ref[place] = normed[:, start : start + width]


def norm_rows(parts, state, ln_gain, ln_bias, layer_index, devices, tp_count):
    count, rows, width = parts.shape
    cut = width // (devices // tp_count)
    operands = [parts] + ([] if state is None else [state]) + [ln_gain, ln_bias]
    return pl.pallas_call(
        functools.partial(norm_kernel, state is not None, layer_index, tp_count),
        out_shape=(
            jax.ShapeDtypeStruct((rows, width), jnp.float32),
            jax.ShapeDtypeStruct((devices, rows, cut), jnp.bfloat16),
        ),
        in_specs=[whole()] * len(operands),
        out_specs=(whole(), whole()),
        compiler_params=compiler_params(16),
        name="norm_rows",
    )(*operands)


def last_parts_kernel(tp_count, place_ref, part_ref, state_ref, out_ref):
    total = part_ref[0].astype(jnp.float32)
    for chip in range(1, part_ref.shape[0]):
        total = total + part_ref[chip].astype(jnp.float32)
    mine = state_ref.shape[0]
    owner = place_ref[1] % tp_count
    for place in range(tp_count):
        rows = slice(place * mine, (place + 1) * mine)
        total_rows = total[rows] + jnp.where(owner == place, 1.0, 0.0) * state_ref[...]
        out_ref[rows] = total_rows


def last_parts(place, parts, state, tp_count):
    return pl.pallas_call(
        functools.partial(last_parts_kernel, tp_count),
        out_shape=jax.ShapeDtypeStruct(parts.shape[1:], jnp.float32),
        in_specs=[whole(pltpu.SMEM), whole(), whole()],
        out_specs=whole(),
        compiler_params=compiler_params(16),
        name="last_parts",
    )(in_hbm(place), parts, state)


def last_kernel(a_ref, b_ref, c_ref, d_ref, out_ref):
    near = a_ref[...].astype(jnp.float32) + b_ref[...].astype(jnp.float32)
    far = c_ref[...].astype(jnp.float32) + d_ref[...].astype(jnp.float32)
    total = (near + far).astype(jnp.bfloat16)
    for place in range(out_ref.shape[0]):
        out_ref[place] = total


def last_rows(parts):
    return pl.pallas_call(
        last_kernel,
        out_shape=jax.ShapeDtypeStruct((CHIPS,) + parts[0].shape, jnp.bfloat16),
        in_specs=[whole()] * 4,
        out_specs=whole(),
        compiler_params=compiler_params(16),
        name="last_rows",
    )(*parts)


def core_parity(place_ref, other):
    return 1 - place_ref[0] % 2 if other else place_ref[0] % 2


def heads_kernel(joins, place_ref, hidden_ref, qkv_ref, *refs):
    arrived_ref, out_ref = refs if joins else (None, refs[0])
    parity = core_parity(place_ref, not joins)
    rows = hidden_ref.shape[0]
    width = qkv_ref.shape[1] // 3
    unit = out_ref.shape[-1]
    share = rows // CHIPS // 2
    half = rows // 2
    pieces = width // unit
    tall = 2 * pieces * share

    def joined(values, start):
        if joins:
            values = values + arrived_ref[start : start + values.shape[0]].astype(jnp.float32)
        return values.astype(jnp.bfloat16)

    picked = jnp.concatenate(
        [
            hidden_ref[pl.ds(pl.multiple_of((2 * chip + parity) * share, share), share), :]
            for chip in range(CHIPS)
        ],
        axis=0,
    )
    heads = jnp.dot(picked, qkv_ref[...], preferred_element_type=jnp.float32)
    for piece in range(pieces):
        start = piece * half
        query = joined(heads[:, piece * unit : (piece + 1) * unit], start)
        if joins:
            for chip in range(CHIPS):
                out_ref[chip, tall + start : tall + start + half] = query
        else:
            out_ref[start : start + half] = query
    base = pieces * half
    for chip in range(CHIPS):
        for piece in range(2 * pieces):
            column = width + piece * unit
            start = base + (chip * 2 * pieces + piece) * share
            value = joined(heads[chip * share : (chip + 1) * share, column : column + unit], start)
            if joins:
                out_ref[chip, piece * share : (piece + 1) * share] = value
            else:
                out_ref[start : start + share] = value


def project_heads(place, hidden, weights_qkv, unit, arrived=None):
    rows = hidden.shape[0]
    pieces = weights_qkv.shape[1] // 3 // unit
    tall = 2 * pieces * (rows // CHIPS // 2)
    common = pieces * (rows // 2)
    extra = [] if arrived is None else [arrived]
    shape = (common + CHIPS * tall, unit) if arrived is None else (CHIPS, tall + common, unit)
    return pl.pallas_call(
        functools.partial(heads_kernel, arrived is not None),
        out_shape=jax.ShapeDtypeStruct(shape, jnp.bfloat16),
        in_specs=[whole(pltpu.SMEM)] + [whole()] * (2 + len(extra)),
        out_specs=whole(),
        compiler_params=compiler_params(24),
        name="project_heads",
    )(in_hbm(place), hidden, weights_qkv, *extra)


def units_kernel(joins, place_ref, hidden_ref, fc1_ref, *refs):
    arrived_ref, out_refs = (refs[0], refs[1:]) if joins else (None, refs)
    parity = core_parity(place_ref, not joins)
    here = place_ref[0] // 2
    unit = fc1_ref.shape[2] // CHIPS // 2
    hidden = hidden_ref[...]
    for distance in range(CHIPS):
        target = 2 * (here ^ distance) + parity
        columns = pl.ds(pl.multiple_of(target * unit, unit), unit)
        pre = jnp.dot(hidden, fc1_ref[0, :, columns], preferred_element_type=jnp.float32)
        if joins:
            pre = pre + arrived_ref[distance].astype(jnp.float32)
            out_refs[distance][...] = pre.astype(jnp.bfloat16)
        else:
            out_refs[0][distance] = pre.astype(jnp.bfloat16)


def project_units(place, hidden, w_fc1, layer_index, arrived=None):
    rows = hidden.shape[0]
    unit = w_fc1.shape[2] // CHIPS // 2
    extra = [] if arrived is None else [arrived]
    if arrived is None:
        out_shape = jax.ShapeDtypeStruct((CHIPS, rows, unit), jnp.bfloat16)
    else:
        out_shape = (jax.ShapeDtypeStruct((rows, unit), jnp.bfloat16),) * CHIPS
    return pl.pallas_call(
        functools.partial(units_kernel, arrived is not None),
        grid=(1,),
        out_shape=out_shape,
        in_specs=[whole(pltpu.SMEM), same_block(hidden.shape), layer_block(layer_index, w_fc1.shape[1:])]
        + [same_block(values.shape) for values in extra],
        out_specs=jax.tree.map(lambda leaf: same_block(leaf.shape), out_shape),
        compiler_params=compiler_params(24),
        name="project_units",
    )(in_hbm(place), hidden, w_fc1, *extra)


def activate_kernel(place_ref, part_ref, table_ref, query_ref, key_ref, value_ref):
    total = part_ref[0].astype(jnp.float32)
    for chip in range(1, part_ref.shape[0]):
        total = total + part_ref[chip].astype(jnp.float32)
    share, width = key_ref.shape
    half = query_ref.shape[0]
    unit = part_ref.shape[2]
    lanes = table_ref.shape[2]
    pieces = width // unit
    own = pl.ds(pl.multiple_of((place_ref[0] // 2) * share, share), share)

    def put(target_ref, start, height, span, scale):
        for piece in range(pieces):
            for column in range(0, unit, lanes):
                first = start + piece * height
                values = total[first : first + height, column : column + lanes]
                if span is not None:
                    values = (
                        values * table_ref[0, span]
                        + pltpu.roll(values, lanes - ROT // 2, 1) * table_ref[1, span]
                        + pltpu.roll(values, ROT // 2, 1) * table_ref[2, span]
                    )
                values = values.astype(jnp.bfloat16)
                if scale is not None:
                    values = (values.astype(jnp.float32) * scale).astype(jnp.bfloat16)
                column_out = piece * unit + column
                target_ref[:, column_out : column_out + lanes] = values

    put(key_ref, 0, share, own, None)
    put(value_ref, pieces * share, share, None, None)
    put(query_ref, 2 * pieces * share, half, slice(None), 1.0 / math.sqrt(HEAD_DIM))


def activate(place, parts, tables, width):
    half = tables.shape[1]
    small = jax.ShapeDtypeStruct((half // CHIPS, width), jnp.bfloat16)
    return pl.pallas_call(
        activate_kernel,
        out_shape=(jax.ShapeDtypeStruct((half, width), jnp.bfloat16), small, small),
        in_specs=[whole(pltpu.SMEM), whole(), whole()],
        out_specs=(whole(),) * 3,
        compiler_params=compiler_params(16),
        name="activate",
    )(in_hbm(place), parts, tables)


def rotary_tables(positions, width):
    half = ROT // 2
    feature = lax.broadcasted_iota(jnp.int32, (1, width), 1) % HEAD_DIM
    frequency = jnp.exp((feature % half).astype(jnp.float32) * (-2.0 * math.log(10000.0) / ROT))
    angles = positions.astype(jnp.float32)[:, None] * frequency
    cosine, sine = jnp.cos(angles), jnp.sin(angles)
    return jnp.stack(
        [
            jnp.where(feature < ROT, cosine, 1.0),
            jnp.where(feature < half, -sine, 0.0),
            jnp.where((feature >= half) & (feature < ROT), sine, 0.0),
        ]
    )


def attend_kernel(
    layer_index, new_tokens,
    place_ref, visit_ref, query_ref, far_query_ref, new_key_ref, new_value_ref,
    key_hbm, value_hbm, out_ref,
    key_ref, value_ref, both_ref, score_ref, top_ref, sum_ref, mix_ref, semaphores,
):
    blocks = visit_ref.shape[0] // 4
    groups, tall, lanes = mix_ref.shape
    share = new_key_ref.shape[0]
    heads = tall // share
    chunks = semaphores.shape[1]
    chunk = key_ref.shape[0] // chunks

    def copy(kind, index):
        span = pl.ds(index * chunk, chunk)
        source, target = ((key_hbm, key_ref), (value_hbm, value_ref))[kind]
        return pltpu.make_async_copy(
            source.at[layer_index, span], target.at[span], semaphores.at[kind, index]
        )

    for kind in range(2):
        for index in range(chunks):
            copy(kind, index).start()
    core = place_ref[0] % 2
    for chip in range(groups // 2):
        span = slice(chip * share, (chip + 1) * share)
        both_ref[2 * chip + core] = query_ref[span]
        both_ref[2 * chip + 1 - core] = far_query_ref[span]
    lane = lax.broadcasted_iota(jnp.int32, (share, lanes), 1)
    row = lax.broadcasted_iota(jnp.int32, (share, lanes), 0)
    top_ref[...] = jnp.full(top_ref.shape, very_negative, jnp.float32)
    sum_ref[...] = jnp.zeros(sum_ref.shape, jnp.float32)
    mix_ref[...] = jnp.zeros(mix_ref.shape, jnp.float32)

    def score(index, group, keys, mask):
        scores = []
        for pair in range(heads // 2):
            both = both_ref[group, :, pair * lanes : (pair + 1) * lanes]
            none = jnp.zeros_like(both)
            split = jnp.concatenate(
                [jnp.where(lane < HEAD_DIM, both, none), jnp.where(lane < HEAD_DIM, none, both)], axis=0
            )
            scores.append(
                lax.dot_general(
                    split, keys[:, pair * lanes : (pair + 1) * lanes], (((1,), (1,)), ((), ())),
                    preferred_element_type=jnp.float32,
                )
            )
        scores = jnp.concatenate(scores, axis=0).reshape(heads, share, BLOCK)
        scores = jnp.where(mask[None], scores, very_negative).reshape(tall, BLOCK)
        score_ref[index] = scores
        top_ref[group] = jnp.maximum(top_ref[group], scores)

    def mix(index, group, values):
        weight = jnp.exp(score_ref[index] - top_ref[group])
        sum_ref[group] += weight
        rounded = weight.astype(jnp.bfloat16)
        mix_ref[group] += jnp.concatenate(
            [
                jnp.dot(
                    rounded[pair * 2 * share : (pair + 1) * 2 * share],
                    values[:, pair * lanes : (pair + 1) * lanes],
                    preferred_element_type=jnp.float32,
                )
                for pair in range(heads // 2)
            ],
            axis=0,
        )

    own = place_ref[0]
    fill = jnp.zeros((BLOCK - share, new_key_ref.shape[1]), jnp.bfloat16)
    score(
        blocks, own, jnp.concatenate([new_key_ref[...], fill], axis=0),
        (lane // new_tokens == row // new_tokens) & (lane <= row),
    )
    owners = []
    for block in range(blocks):
        if (block * BLOCK) % chunk == 0:
            copy(0, block * BLOCK // chunk).wait()
        group, live, first, end = (visit_ref[field * blocks + block] for field in range(4))
        owners.append(group)
        score(
            block, group, key_ref[block * BLOCK : (block + 1) * BLOCK, :],
            (lane < live) & (row >= first) & (row < end),
        )
    for group in range(groups):
        top = jnp.max(top_ref[group], axis=1, keepdims=True)
        top_ref[group] = jnp.broadcast_to(top, (tall, lanes))
    mix(blocks, own, jnp.concatenate([new_value_ref[...], fill], axis=0))
    for block in range(blocks):
        if (block * BLOCK) % chunk == 0:
            copy(1, block * BLOCK // chunk).wait()
        mix(block, owners[block], value_ref[block * BLOCK : (block + 1) * BLOCK, :])

    level = jnp.zeros((tall, lanes), jnp.float32)
    column = lax.broadcasted_iota(jnp.int32, (tall, lanes), 1)

    def mean(group):
        total = jnp.sum(sum_ref[group], axis=1, keepdims=True)
        total = jnp.where(total <= 0.0, 1.0, total)
        own_level = jnp.where(column == group, top_ref[group] + jnp.log(total), 0.0)
        return mix_ref[group] / total, own_level

    for group in range(groups // 2):
        left, left_level = mean(group)
        right, right_level = mean(group + groups // 2)
        level = level + left_level + right_level
        for head in range(heads):
            rows = slice(head * share, (head + 1) * share)
            first, second = left[rows], right[rows]
            if head % 2:
                first = pltpu.roll(first, HEAD_DIM, 1)
            else:
                second = pltpu.roll(second, HEAD_DIM, 1)
            packed = jnp.where(lane < HEAD_DIM, first, second)
            out_ref[head, group * share : (group + 1) * share] = packed.astype(jnp.bfloat16)
    level = level.T[:groups]
    high = level.astype(jnp.bfloat16).astype(jnp.float32)
    middle = (level - high).astype(jnp.bfloat16).astype(jnp.float32)
    low = level - high - middle
    rest = jnp.concatenate([high, middle, low, jnp.zeros_like(low)], axis=0).astype(jnp.bfloat16)
    start = (groups // 2) * share
    for head in range(heads):
        column = head * share // lanes * lanes
        out_ref[head, start:] = rest[:, column : column + lanes]


def attend(place, visits, query, far_query, new_key, new_value, k_cache, v_cache, layer_index, new_tokens, groups):
    width = query.shape[1]
    rows = 2 * query.shape[0]
    slots = k_cache.shape[1]
    heads = width // HEAD_DIM
    share = rows // groups
    tall = heads * share
    lanes = 2 * HEAD_DIM
    chunks = 4
    state = pltpu.VMEM((groups, tall, lanes), jnp.float32)
    return pl.pallas_call(
        functools.partial(attend_kernel, layer_index, new_tokens),
        out_shape=jax.ShapeDtypeStruct((heads, rows // 2 + 4 * groups, lanes), jnp.bfloat16),
        in_specs=[whole(pltpu.SMEM)] * 2 + [whole()] * 4 + [whole(pltpu.HBM)] * 2,
        out_specs=whole(),
        scratch_shapes=[
            pltpu.VMEM((slots, width), jnp.bfloat16),
            pltpu.VMEM((slots, width), jnp.bfloat16),
            pltpu.VMEM((groups, share, width), jnp.bfloat16),
            pltpu.VMEM((visits.shape[0] // 4 + 1, tall, BLOCK), jnp.float32),
            state,
            state,
            state,
            pltpu.SemaphoreType.DMA((2, chunks)),
        ],
        compiler_params=compiler_params(24),
        name="attend",
    )(in_hbm(place), in_hbm(visits), query, far_query, new_key, new_value, in_hbm(k_cache), in_hbm(v_cache))


def update_kernel(
    layer_index, other, tp_count, has_start, place_ref, part_ref, bias_ref, out_weight_ref, fc2_ref, *refs
):
    *unit_refs, out_ref, scale_ref = refs
    if has_start:
        *unit_refs, start_ref = unit_refs
    seq_index = place_ref[0]
    parity = 1 - seq_index % 2 if other else seq_index % 2
    sources, tall, lanes = part_ref.shape
    unit = unit_refs[0].shape[1]
    share = unit_refs[0].shape[0] // sources
    groups = (tall - (sources // 2) * share) // 4
    levels = []
    for source in range(sources):
        parts = part_ref[source, (sources // 2) * share :, :].astype(jnp.float32)
        levels.append(parts[:groups] + parts[groups : 2 * groups] + parts[2 * groups : 3 * groups])
    top = functools.reduce(jnp.maximum, levels)
    scales = [jnp.exp(level - top) for level in levels]
    total = functools.reduce(jnp.add, scales)
    scales = [scale / total for scale in scales]
    blank = jnp.zeros((lanes - groups * sources, lanes), jnp.float32)
    scale_ref[...] = jnp.concatenate(scales + [blank], axis=0).T
    place = seq_index % (lanes // share)
    scale = scale_ref[pl.ds(pl.multiple_of(place * share, share), share), :]
    scale = jnp.where(parity == 0, scale, pltpu.roll(scale, lanes - 1, 1))
    lane = lax.broadcasted_iota(jnp.int32, (share, lanes), 1)
    first, second = [], []
    for pair in range(CHIPS // 2):
        rows = pl.ds(pl.multiple_of((2 * pair + parity) * share, share), share)
        mixed = jnp.zeros((share, lanes), jnp.float32)
        for source in range(sources):
            column = source * groups + 2 * pair
            left = scale[:, column : column + 1]
            right = scale[:, column + groups // 2 : column + groups // 2 + 1]
            mixed = mixed + part_ref[source, rows, :].astype(jnp.float32) * jnp.where(
                lane < HEAD_DIM, left, right
            )
        first.append(mixed[:, :HEAD_DIM])
        second.append(pltpu.roll(mixed, HEAD_DIM, 1)[:, :HEAD_DIM])
    attended = jnp.concatenate(first + second, axis=0).astype(jnp.bfloat16)
    bias = bias_ref[
        layer_index : layer_index + 1, pl.ds(pl.multiple_of(seq_index * unit, unit), unit)
    ]
    hidden, started = [], []
    for piece in range(CHIPS):
        rows = pl.ds(pl.multiple_of((2 * piece + parity) * share, share), share)
        pre = functools.reduce(jnp.add, [ref[rows, :].astype(jnp.float32) for ref in unit_refs])
        hidden.append(jax.nn.gelu(pre + bias, approximate=True).astype(jnp.bfloat16))
        if has_start:
            started.append(start_ref[rows, :].astype(jnp.float32))
    change = jnp.dot(attended, out_weight_ref[0], preferred_element_type=jnp.float32) + jnp.dot(
        jnp.concatenate(hidden, axis=0), fc2_ref[0], preferred_element_type=jnp.float32
    )
    if not has_start:
        out_ref[...] = change.astype(out_ref.dtype)
        return
    started = jnp.concatenate(started, axis=0)
    for column in range(0, change.shape[1], unit):
        here = (seq_index * unit == column) & (place_ref[1] % tp_count == 0)
        out_ref[:, column : column + unit] = (
            change[:, column : column + unit] + jnp.where(here, started, 0.0)
        ).astype(out_ref.dtype)


def update(place, parts, units, start, b_fc1, w_out, w_fc2, layer_index, other, tp_count):
    rows = units[0].shape[0] // 2
    width = w_out.shape[2]
    lanes = parts.shape[2]
    extra = list(units) + ([] if start is None else [start])
    return pl.pallas_call(
        functools.partial(update_kernel, layer_index, other, tp_count, start is not None),
        grid=(1,),
        out_shape=jax.ShapeDtypeStruct((rows, width), jnp.bfloat16 if other else jnp.float32),
        in_specs=[
            whole(pltpu.SMEM),
            same_block(parts.shape),
            same_block(b_fc1.shape),
            layer_block(layer_index, w_out.shape[1:]),
            layer_block(layer_index, w_fc2.shape[1:]),
        ]
        + [same_block(units[0].shape)] * len(extra),
        out_specs=same_block((rows, width)),
        scratch_shapes=[pltpu.VMEM((lanes, lanes), jnp.float32)],
        compiler_params=compiler_params(),
        name="update",
    )(in_hbm(place), parts, b_fc1, w_out, w_fc2, *extra)


def per_device(
    token_ids, embedding, group_of, prefix_len, tail_len, block_map, k_cache, v_cache,
    ln_gain, ln_bias, w_qkv, w_fc1, b_fc1, w_out, w_fc2,
):
    seq_count, tp_count = lax.axis_size("seq"), lax.axis_size("tp")
    seq_index, tp_index = lax.axis_index("seq"), lax.axis_index("tp")
    devices = seq_count * tp_count
    core = seq_index % 2
    place = jnp.stack([seq_index, seq_index * tp_count + tp_index]).astype(jnp.int32)
    requests, new_tokens = token_ids.shape
    rows = requests * new_tokens
    groups = prefix_len.shape[0]
    share = rows // seq_count
    mine = rows // devices
    width = embedding.shape[1]
    width_local = k_cache.shape[2]
    unit = w_fc2.shape[1]
    same_core = [[s * tp_count + p for s in range(c, seq_count, 2) for p in range(tp_count)] for c in range(2)]
    same_core_seq = [list(range(c, seq_count, 2)) for c in range(2)]

    def to_owners(half):
        parts = half.reshape(devices // 2, mine, width)
        return lax.all_to_all(parts, ("seq", "tp"), 0, 0, axis_index_groups=same_core)

    def to_chips(parts):
        return lax.all_to_all(parts, "seq", 0, 0, axis_index_groups=same_core_seq)

    def from_tp(part):
        return [part] + [
            lax.ppermute(part, "tp", [(i, i ^ k) for i in range(tp_count)]) for k in range(1, tp_count)
        ]

    near, far, own = embed(place, token_ids, group_of, embedding, unit)
    parts = join(near, swap_cores(far, seq_count), own)
    gathered = gather(to_chips(parts))
    gathered, group_of = lax.optimization_barrier((gathered, group_of))
    rank, positions, visits = order_requests(group_of, prefix_len, tail_len, block_map, new_tokens)
    own_positions = lax.dynamic_index_in_dim(positions.reshape(CHIPS, 2, share), core, 1, keepdims=False)
    tables = rotary_tables(own_positions.reshape(-1), 2 * HEAD_DIM)
    weights_qkv = w_qkv[0].reshape(w_qkv.shape[1], -1)
    start, hidden = first_hidden(place, from_tp(gathered), ln_gain, ln_bias)
    state = None
    for layer_index in range(LAYERS):
        if layer_index:
            weights_qkv = w_qkv[layer_index].reshape(w_qkv.shape[1], -1)
            state, cut = norm_rows(parts, state, ln_gain, ln_bias, layer_index, devices, tp_count)
            hidden = lax.all_to_all(cut, ("seq", "tp"), 0, 0).reshape(rows, -1)
        arriving = swap_cores(project_heads(place, hidden, weights_qkv, unit), seq_count)
        heads = to_chips(project_heads(place, hidden, weights_qkv, unit, arriving))
        arriving = swap_cores(project_units(place, hidden, w_fc1, layer_index), seq_count)
        units = project_units(place, hidden, w_fc1, layer_index, arriving)
        query, new_key, new_value = activate(place, heads, tables, width_local)
        query, *units = lax.optimization_barrier((query, *units))
        units = units[:1] + [
            lax.ppermute(units[k], "seq", [(i, i ^ (2 * k)) for i in range(seq_count)])
            for k in range(1, CHIPS)
        ]
        parts = attend(
            place, visits, query, swap_cores(query, seq_count), new_key, new_value,
            k_cache, v_cache, layer_index, new_tokens, groups,
        )
        parts, *units = lax.optimization_barrier((parts, *units))
        parts = lax.all_to_all(parts, "seq", 0, 0)
        arriving, half = (
            update(place, parts, units, start, b_fc1, w_out, w_fc2, layer_index, other, tp_count)
            for other in (True, False)
        )
        half = (half + swap_cores(arriving, seq_count).astype(jnp.float32)).astype(jnp.bfloat16)
        start = None
        if layer_index < LAYERS - 1:
            parts = to_owners(half)
    last = last_parts(place, to_chips(half.reshape(CHIPS, share, width)), state, tp_count)
    last = from_tp(last.astype(jnp.bfloat16))
    last = to_chips(last_rows(last)).reshape(rows // 2, width)
    arriving = swap_cores(last, seq_count)
    wanted = (rank[:, None] * new_tokens + jnp.arange(new_tokens, dtype=jnp.int32)[None, :]).reshape(-1)
    index = jnp.arange(rows // 2, dtype=jnp.int32)

    def placed(half, parity):
        held = (2 * (index // share) + parity) * share + index % share
        hot = (wanted[:, None] == held[None, :]).astype(jnp.bfloat16)
        return jnp.dot(hot, half, preferred_element_type=jnp.float32)

    return (placed(last, core) + placed(arriving, 1 - core)).reshape(requests, new_tokens, width)


def solution(mesh):
    in_specs = (
        P(),
        P(("seq", "tp"), None),
        P(),
        P(),
        P(),
        P("seq", None),
        P(None, "seq", "tp"),
        P(None, "seq", "tp"),
        P(),
        P(),
        P(None, "seq", None, "tp"),
        P(None, "seq", "tp"),
        P(None, "tp"),
        P(None, ("tp", "seq"), None),
        P(None, ("tp", "seq"), None),
    )
    out_specs = P()
    seq_count, tp_count = mesh.shape["seq"], mesh.shape["tp"]
    fits = tp_count == 4 and seq_count == HEADS // tp_count and seq_count == 2 * CHIPS
    return jax.shard_map(
        per_device if fits else per_device_any, mesh=mesh, in_specs=in_specs, out_specs=out_specs, check_vma=False
    )
```

```python
import functools
import math

import jax
import jax.numpy as jnp
from jax import lax
from jax.experimental import pallas as pl
from jax.experimental.pallas import tpu as pltpu
from jax.sharding import PartitionSpec as P

HEADS = 32
HEAD_DIM = 64
ROT = 32
LAYERS = 2
BLOCK = 128
SPAN = 512
CHIPS = 4
LANES = 128


very_negative = -1e30


def layer_norm(values, gain_row, bias_row):
    average = jnp.mean(values, axis=-1, keepdims=True)
    centred = values - average
    variance = jnp.mean(centred * centred, axis=-1, keepdims=True)
    return centred * lax.rsqrt(variance + 1e-05) * gain_row + bias_row


def rotary(values, positions):
    half_width = ROT // 2
    frequency = jnp.exp(
        jnp.arange(half_width, dtype=jnp.float32) * (-2.0 * math.log(10000.0) / ROT)
    )
    angles = positions.astype(jnp.float32)[:, None] * frequency[None, :]
    cosine = jnp.cos(angles)[:, None, :]
    sine_part = jnp.sin(angles)[:, None, :]
    low_half = values[..., :half_width]
    high_half = values[..., half_width:ROT]
    return jnp.concatenate(
        [
            low_half * cosine - high_half * sine_part,
            high_half * cosine + low_half * sine_part,
            values[..., ROT:],
        ],
        axis=-1,
    )


def combine_parts(left_part, right_part):
    max_left, sum_left, out_left = left_part
    max_right, sum_right, out_right = right_part
    top_value = jnp.maximum(max_left, max_right)
    scale_left = jnp.exp(max_left - top_value)
    scale_right = jnp.exp(max_right - top_value)
    return (
        top_value,
        sum_left * scale_left + sum_right * scale_right,
        out_left * scale_left[..., None] + out_right * scale_right[..., None],
    )


def full_total(values):
    return lax.psum(values, ("seq", "tp"))


def per_device_any(
    token_ids,
    embedding,
    group_of,
    prefix_len,
    tail_len,
    block_map,
    k_cache,
    v_cache,
    ln_gain,
    ln_bias,
    w_qkv,
    w_fc1,
    b_fc1,
    w_out,
    w_fc2,
):
    tp_count = lax.axis_size("tp")
    seq_index = lax.axis_index("seq")
    tp_index = lax.axis_index("tp")
    requests = token_ids.shape[0]
    new_tokens = token_ids.shape[1]
    groups = prefix_len.shape[0]
    heads_local = HEADS // tp_count
    width_local = heads_local * HEAD_DIM
    score_scale = 1.0 / math.sqrt(HEAD_DIM)
    vocab_rows = embedding.shape[0]
    first_row = (seq_index * tp_count + tp_index) * vocab_rows
    local_ids = token_ids.reshape(-1) - first_row
    inside = (local_ids >= 0) & (local_ids < vocab_rows)
    picked = jnp.take(embedding, jnp.clip(local_ids, 0, vocab_rows - 1), axis=0).astype(jnp.float32)
    picked = jnp.where(inside[:, None], picked, 0.0)
    start_states = full_total(picked).reshape(requests, new_tokens, -1)
    group_hit = group_of[:, None] == jnp.arange(groups, dtype=jnp.int32)[None, :]
    shared_len = jnp.sum(jnp.where(group_hit, prefix_len[None, :], 0), axis=1)
    base_positions = shared_len + tail_len
    seg_len = jnp.concatenate([prefix_len, tail_len])
    seg_count = seg_len.shape[0]
    blocks_local = block_map.shape[0]
    seg_blk = block_map[:, 0]
    rank_blk = block_map[:, 1]
    seg_hit = seg_blk[:, None] == jnp.arange(seg_count, dtype=jnp.int32)[None, :]
    len_blk = jnp.sum(jnp.where(seg_hit, seg_len[None, :], 0), axis=1)
    slot_positions = rank_blk[:, None] * BLOCK + jnp.arange(BLOCK, dtype=jnp.int32)[None, :]
    live_slot = ((seg_blk[:, None] >= 0) & (slot_positions < len_blk[:, None])).reshape(-1)
    seg_slot = jnp.broadcast_to(seg_blk[:, None], (blocks_local, BLOCK)).reshape(-1)
    own_tail = seg_slot[None, :] == (groups + jnp.arange(requests, dtype=jnp.int32))[:, None]
    own_prompt = seg_slot[None, :] == group_of[:, None]
    allowed = (own_tail | own_prompt) & live_slot[None, :]
    step_count = allowed.shape[1] // SPAN
    allowed_steps = allowed.reshape(requests, step_count, SPAN).transpose(1, 0, 2)
    rows_local = w_qkv.shape[1]
    unit_count = w_fc2.shape[1]
    sub_width = w_out.shape[1]
    token_index = jnp.arange(new_tokens, dtype=jnp.int32)
    new_keys = [
        jnp.zeros((requests, new_tokens, heads_local, HEAD_DIM), jnp.bfloat16)
        for layer_index in range(LAYERS)
    ]
    new_values = [
        jnp.zeros((requests, new_tokens, heads_local, HEAD_DIM), jnp.bfloat16)
        for layer_index in range(LAYERS)
    ]
    results = []
    for token_step in range(new_tokens):
        hidden_state = start_states[:, token_step]
        positions = base_positions + token_step
        for layer_index in range(LAYERS):
            normed = layer_norm(hidden_state, ln_gain[layer_index], ln_bias[layer_index]).astype(
                jnp.bfloat16
            )
            my_rows = lax.dynamic_slice_in_dim(normed, seq_index * rows_local, rows_local, 1)
            part_proj = jnp.dot(
                my_rows,
                w_qkv[layer_index].reshape(rows_local, -1),
                preferred_element_type=jnp.float32,
            )
            part_fc1 = jnp.dot(my_rows, w_fc1[layer_index], preferred_element_type=jnp.float32)
            attention_proj, fc1_all = lax.psum((part_proj, part_fc1), "seq")
            pre_act = lax.dynamic_slice_in_dim(fc1_all, seq_index * unit_count, unit_count, 1)
            pre_act = (
                pre_act
                + lax.dynamic_slice_in_dim(
                    b_fc1[layer_index], seq_index * unit_count, unit_count, 0
                )[None, :]
            )
            activated = jax.nn.gelu(pre_act, approximate=True).astype(jnp.bfloat16)
            attention_proj = attention_proj.reshape(requests, 3, heads_local, HEAD_DIM)
            queries = rotary(attention_proj[:, 0], positions).astype(jnp.bfloat16)
            key_rows = rotary(attention_proj[:, 1], positions).astype(jnp.bfloat16)
            value_rows = attention_proj[:, 2].astype(jnp.bfloat16)
            new_keys[layer_index] = new_keys[layer_index].at[:, token_step].set(key_rows)
            new_values[layer_index] = new_values[layer_index].at[:, token_step].set(value_rows)
            key_steps = k_cache[layer_index].reshape(step_count, SPAN, heads_local, HEAD_DIM)
            value_steps = v_cache[layer_index].reshape(step_count, SPAN, heads_local, HEAD_DIM)

            def cache_step(carry, inputs):
                run_max, run_sum, run_out = carry
                key_block, value_block, allow_block = inputs
                scores = (
                    jnp.einsum(
                        "rhd,shd->hrs", queries, key_block, preferred_element_type=jnp.float32
                    )
                    * score_scale
                )
                scores = jnp.where(allow_block[None], scores, very_negative)
                next_max = jnp.maximum(run_max, jnp.max(scores, axis=2))
                weights = jnp.where(allow_block[None], jnp.exp(scores - next_max[..., None]), 0.0)
                shrink = jnp.exp(run_max - next_max)
                next_sum = run_sum * shrink + jnp.sum(weights, axis=2)
                next_out = run_out * shrink[..., None] + jnp.einsum(
                    "hrs,shd->hrd",
                    weights.astype(jnp.bfloat16),
                    value_block,
                    preferred_element_type=jnp.float32,
                )
                return ((next_max, next_sum, next_out), None)

            start_carry = (
                jnp.full((heads_local, requests), very_negative, jnp.float32),
                jnp.zeros((heads_local, requests), jnp.float32),
                jnp.zeros((heads_local, requests, HEAD_DIM), jnp.float32),
            )
            (part_max, part_sum, part_out), unused = lax.scan(
                cache_step, start_carry, (key_steps, value_steps, allowed_steps)
            )
            cache_max = lax.pmax(part_max, "seq")
            factor = jnp.exp(part_max - cache_max)
            cache_sum, cache_out = (
                lax.psum((part_sum * factor).astype(jnp.bfloat16), "seq").astype(jnp.float32),
                lax.psum((part_out * factor[..., None]).astype(jnp.bfloat16), "seq").astype(
                    jnp.float32
                ),
            )
            visible = (token_index <= token_step)[None, None, :]
            fresh_scores = (
                jnp.einsum(
                    "rhd,rjhd->hrj",
                    queries,
                    new_keys[layer_index],
                    preferred_element_type=jnp.float32,
                )
                * score_scale
            )
            fresh_scores = jnp.where(visible, fresh_scores, very_negative)
            fresh_max = jnp.max(fresh_scores, axis=2)
            fresh_weights = jnp.where(visible, jnp.exp(fresh_scores - fresh_max[..., None]), 0.0)
            fresh_sum = jnp.sum(fresh_weights, axis=2)
            fresh_out = jnp.einsum(
                "hrj,rjhd->hrd",
                fresh_weights.astype(jnp.bfloat16),
                new_values[layer_index],
                preferred_element_type=jnp.float32,
            )
            joint_max, denom_total, weighted = combine_parts(
                (cache_max, cache_sum, cache_out), (fresh_max, fresh_sum, fresh_out)
            )
            attended = (weighted / denom_total[..., None]).astype(jnp.bfloat16)
            attended = attended.transpose(1, 0, 2).reshape(requests, width_local)
            my_cols = lax.dynamic_slice_in_dim(attended, seq_index * sub_width, sub_width, 1)
            update = jnp.dot(my_cols, w_out[layer_index], preferred_element_type=jnp.float32)
            update = update + jnp.dot(
                activated, w_fc2[layer_index], preferred_element_type=jnp.float32
            )
            hidden_state = hidden_state + full_total(update)
        results.append(hidden_state)
    stacked = jnp.stack(results, axis=1)
    return stacked


def swap_cores(values, seq_count):
    return lax.ppermute(values, "seq", [(i, i ^ 1) for i in range(seq_count)])


def in_hbm(values):
    return pltpu.with_memory_space_constraint(values, pltpu.HBM)


def compiler_params(megabytes=32):
    return pltpu.CompilerParams(vmem_limit_bytes=megabytes * 2**20)


def whole(memory_space=pltpu.VMEM):
    return pl.BlockSpec(memory_space=memory_space)


def layer_block(layer_index, shape):
    return pl.BlockSpec((1,) + shape, lambda step: (layer_index,) + (0,) * len(shape))


def same_block(shape):
    return pl.BlockSpec(shape, lambda step: (0,) * len(shape))


def order_kernel(new_tokens, group_ref, prefix_ref, tail_ref, map_ref, rank_ref, position_ref, visit_ref, count_ref):
    requests = group_ref.shape[0]
    groups = prefix_ref.shape[0]
    per_group = requests // groups
    blocks = map_ref.shape[1]
    for group in range(groups):
        count_ref[group] = 0

    def place(request, unused):
        group = group_ref[request]
        seat = count_ref[group]
        count_ref[group] = seat + 1
        rank = group * per_group + seat
        rank_ref[request] = rank
        start = prefix_ref[group] + tail_ref[request]
        for token in range(new_tokens):
            position_ref[rank * new_tokens + token] = start + token
        return unused

    lax.fori_loop(0, requests, place, 0)

    def look(block, unused):
        segment, depth = map_ref[0, block], map_ref[1, block]
        is_tail = segment >= groups
        request = jnp.clip(segment - groups, 0, requests - 1)
        prompt = jnp.clip(segment, 0, groups - 1)
        seat = rank_ref[request]
        first = jnp.where(is_tail, (seat % per_group) * new_tokens, 0)
        length = jnp.where(is_tail, tail_ref[request], prefix_ref[prompt])
        visit_ref[block] = jnp.where(is_tail, seat // per_group, prompt)
        visit_ref[blocks + block] = jnp.where(segment < 0, 0, length - depth * BLOCK)
        visit_ref[2 * blocks + block] = first
        visit_ref[3 * blocks + block] = jnp.where(is_tail, first + new_tokens, per_group * new_tokens)
        return unused

    lax.fori_loop(0, blocks, look, 0)


def order_requests(group_of, prefix_len, tail_len, block_map, new_tokens):
    requests = group_of.shape[0]
    smem = whole(pltpu.SMEM)
    return pl.pallas_call(
        functools.partial(order_kernel, new_tokens),
        out_shape=(
            jax.ShapeDtypeStruct((requests,), jnp.int32),
            jax.ShapeDtypeStruct((requests * new_tokens,), jnp.int32),
            jax.ShapeDtypeStruct((4 * block_map.shape[0],), jnp.int32),
        ),
        in_specs=[smem] * 4,
        out_specs=(smem, smem, smem),
        scratch_shapes=[pltpu.SMEM((prefix_len.shape[0],), jnp.int32)],
        name="order_requests",
    )(group_of, prefix_len, tail_len, block_map.T)


def thirds(values):
    high = values.astype(jnp.bfloat16).astype(jnp.float32)
    middle = (values - high).astype(jnp.bfloat16).astype(jnp.float32)
    return high, middle, values - high - middle


def row_block(rows):
    width = rows[0].shape[1]
    line = lax.broadcasted_iota(jnp.int32, (8, width), 0)
    block = jnp.zeros((8, width), jnp.float32)
    for index, row in enumerate(rows):
        block = jnp.where(line == index, row, block)
    return block


def column_to_row(column):
    return jnp.broadcast_to(column, (column.shape[0], LANES)).T[0:1]


def row_to_column(row):
    return jnp.broadcast_to(row, (LANES, row.shape[1])).T


def ranks(group_ref):
    requests = group_ref.shape[1]
    across = lax.broadcasted_iota(jnp.int32, (requests, requests), 1)
    down = lax.broadcasted_iota(jnp.int32, (requests, requests), 0)
    group_row = group_ref[0:1, :]
    group_column = jnp.sum(jnp.where(across == down, group_row, 0), axis=1, keepdims=True)
    ahead = (group_column < group_row) | ((group_column == group_row) & (down < across))
    return jnp.sum(jnp.where(ahead, 1, 0), axis=0, keepdims=True)


def row_sums(lines):
    block = row_block([part for line in lines for part in thirds(line)])
    return jnp.concatenate([block, jnp.zeros_like(block)], axis=0).astype(jnp.bfloat16)


def from_row_sums(block):
    block = block.astype(jnp.float32)
    line = lax.broadcasted_iota(jnp.int32, block.shape, 0)
    return [
        jnp.sum(jnp.where((line >= start) & (line < start + 3), block, 0.0), axis=0, keepdims=True)
        for start in (0, 3)
    ]


def embed_kernel(
    token_ref, group_ref, table_hbm, near_ref, far_ref, own_ref,
    table_ref, hot_ref, row_ref, semaphores,
):
    core = lax.axis_index("seq") % 2
    first = (lax.axis_index("seq") * lax.axis_size("tp") + lax.axis_index("tp")) * table_ref.shape[1]
    new_tokens, requests = token_ref.shape
    rows, unit = near_ref.shape[1:]
    copies = []
    for chip in range(CHIPS):
        copies.append(
            pltpu.make_async_copy(
                table_hbm.at[:, pl.ds(chip * 2 * unit, 2 * unit)], table_ref.at[chip], semaphores.at[chip]
            )
        )
        copies[-1].start()
    rank_row = ranks(group_ref)
    line = lax.broadcasted_iota(jnp.int32, (rows, requests), 0)
    ids = jnp.zeros((rows, requests), jnp.int32)
    for token in range(new_tokens):
        match = (rank_row == line // new_tokens) & (line % new_tokens == token)
        ids = jnp.where(match, token_ref[token : token + 1, :], ids)
    ids = jnp.sum(ids, axis=1, keepdims=True) - first
    entry = lax.broadcasted_iota(jnp.int32, hot_ref.shape, 1)
    hot_ref[...] = jnp.where(entry == ids, 1.0, 0.0).astype(jnp.bfloat16)
    total = jnp.zeros((rows, LANES), jnp.float32)
    for chip, copy in enumerate(copies):
        copy.wait()
        chosen = jnp.dot(hot_ref[...], table_ref[chip], preferred_element_type=jnp.float32)
        for start in range(0, 2 * unit, LANES):
            total = total + chosen[:, start : start + LANES]
        chosen = chosen.astype(jnp.bfloat16)
        row_ref[:, chip * 2 * unit : (chip + 1) * 2 * unit] = chosen
        left, right = chosen[:, :unit], chosen[:, unit:]
        near_ref[chip] = jnp.where(core == 0, left, right)
        far_ref[chip * rows : (chip + 1) * rows] = jnp.where(core == 0, right, left)
    features = row_ref.shape[1]
    mean = jnp.sum(total, axis=1, keepdims=True) * (1.0 / features)
    squares = jnp.zeros((rows, LANES), jnp.float32)
    for start in range(0, features, LANES):
        centred = row_ref[:, start : start + LANES].astype(jnp.float32) - mean
        squares = squares + centred * centred
    variance = jnp.sum(squares, axis=1, keepdims=True) * (1.0 / features)
    held = (ids >= 0) & (ids < hot_ref.shape[1])
    scale = jnp.where(held, lax.rsqrt(variance + 1e-05), 0.0)
    mean, scale = column_to_row(mean), column_to_row(scale)
    own_ref[...] = row_block([mean, scale])
    far_ref[CHIPS * rows :] = row_sums([mean, scale])


def embed(token_ids, group_of, embedding, unit):
    rows = token_ids.shape[0] * token_ids.shape[1]
    return pl.pallas_call(
        embed_kernel,
        out_shape=(
            jax.ShapeDtypeStruct((CHIPS, rows, unit), jnp.bfloat16),
            pltpu.HBM((CHIPS * rows + 16, unit), jnp.bfloat16),
            jax.ShapeDtypeStruct((8, rows), jnp.float32),
        ),
        in_specs=[whole(), whole(), whole(pltpu.HBM)],
        out_specs=(whole(),) * 3,
        scratch_shapes=[
            pltpu.VMEM((CHIPS, embedding.shape[0], 2 * unit), jnp.bfloat16),
            pltpu.VMEM((rows, embedding.shape[0]), jnp.bfloat16),
            pltpu.VMEM((rows, embedding.shape[1]), jnp.bfloat16),
            pltpu.SemaphoreType.DMA((CHIPS,)),
        ],
        compiler_params=compiler_params(24),
        name="embed",
    )(in_hbm(token_ids.T), in_hbm(group_of[None, :]), in_hbm(embedding))


def join_kernel(near_ref, far_ref, own_ref, out_ref, *refs):
    *out_hbms, leave_ref, semaphores = refs
    here = lax.axis_index("seq") // 2
    rows = near_ref.shape[1]
    mean, scale = from_row_sums(far_ref[CHIPS * rows :])
    lines = row_sums([mean + own_ref[0:1, :], scale + own_ref[1:2, :]])
    leaving = []
    for distance in reversed(range(CHIPS)):
        chip = here ^ distance
        far = far_ref[pl.ds(pl.multiple_of(chip * rows, rows), rows), :].astype(jnp.float32)
        joined = (near_ref[chip].astype(jnp.float32) + far).astype(jnp.bfloat16)
        if distance:
            leave_ref[distance - 1, :rows] = joined
            leave_ref[distance - 1, rows:] = lines
            leaving.append(
                pltpu.make_async_copy(
                    leave_ref.at[distance - 1], out_hbms[distance - 1], semaphores.at[distance - 1]
                )
            )
            leaving[-1].start()
        else:
            out_ref[:rows] = joined
            out_ref[rows:] = lines
    for copy in leaving:
        copy.wait()


def join(near, far, own):
    chips, rows, unit = near.shape
    one = (rows + 16, unit)
    return pl.pallas_call(
        join_kernel,
        out_shape=(jax.ShapeDtypeStruct(one, jnp.bfloat16),) + (pltpu.HBM(one, jnp.bfloat16),) * (chips - 1),
        in_specs=[whole()] * 3,
        out_specs=(whole(),) + (whole(pltpu.HBM),) * (chips - 1),
        scratch_shapes=[pltpu.VMEM((chips - 1,) + one, jnp.bfloat16), pltpu.SemaphoreType.DMA((chips - 1,))],
        compiler_params=compiler_params(16),
        name="join",
    )(near, far, own)


def gather_kernel(a_ref, b_ref, c_ref, d_ref, out_ref):
    rows = out_ref.shape[0] - 16
    near = a_ref[...].astype(jnp.float32) + b_ref[...].astype(jnp.float32)
    far = c_ref[...].astype(jnp.float32) + d_ref[...].astype(jnp.float32)
    total = near + far
    out_ref[:rows] = total[:rows].astype(jnp.bfloat16)
    out_ref[rows:] = row_sums(from_row_sums(total[rows:]))


def gather(parts):
    return pl.pallas_call(
        gather_kernel,
        out_shape=jax.ShapeDtypeStruct(parts[0].shape, jnp.bfloat16),
        in_specs=[whole()] * 4,
        out_specs=whole(),
        compiler_params=compiler_params(16),
        name="gather",
    )(*parts)


def first_kernel(a_ref, b_ref, c_ref, d_ref, gain_ref, bias_ref, start_ref, hidden_ref):
    rows, unit = hidden_ref.shape
    parts = [ref[...].astype(jnp.float32) for ref in (a_ref, b_ref, c_ref, d_ref)]
    total = (parts[0] + parts[1]) + (parts[2] + parts[3])
    mean, scale = (row_to_column(line) for line in from_row_sums(total[rows:]))
    columns = pl.ds(pl.multiple_of(lax.axis_index("seq") * unit, unit), unit)
    gain, bias = gain_ref[0:1, columns], bias_ref[0:1, columns]
    for start in range(0, unit, LANES):
        span = slice(start, start + LANES)
        state = total[:rows, span]
        start_ref[:, span] = state.astype(jnp.bfloat16)
        hidden_ref[:, span] = ((state - mean) * scale * gain[:, span] + bias[:, span]).astype(jnp.bfloat16)


def first_hidden(parts, ln_gain, ln_bias):
    one = jax.ShapeDtypeStruct((parts[0].shape[0] - 16, parts[0].shape[1]), jnp.bfloat16)
    return pl.pallas_call(
        first_kernel,
        out_shape=(one, one),
        in_specs=[whole()] * 6,
        out_specs=(whole(), whole()),
        compiler_params=compiler_params(16),
        name="first_hidden",
    )(*parts, ln_gain, ln_bias)


def norm_kernel(layer_index, tp_count, *refs):
    part_ref, *state_refs, gain_ref, bias_ref, next_ref, cut_ref = refs
    state = part_ref[0].astype(jnp.float32)
    for source in range(1, part_ref.shape[0]):
        state = state + part_ref[source].astype(jnp.float32)
    for ref in state_refs:
        state = state + ref[...]
    next_ref[...] = state
    average = jnp.mean(state, axis=-1, keepdims=True)
    centred = state - average
    variance = jnp.mean(centred * centred, axis=-1, keepdims=True)
    gain = gain_ref[layer_index : layer_index + 1, :]
    bias = bias_ref[layer_index : layer_index + 1, :]
    normed = (centred * lax.rsqrt(variance + 1e-05) * gain + bias).astype(jnp.bfloat16)
    width = cut_ref.shape[2]
    for place in range(cut_ref.shape[0]):
        start = (place // tp_count) * width
        cut_ref[place] = normed[:, start : start + width]


def norm_rows(parts, state, ln_gain, ln_bias, layer_index, devices, tp_count):
    count, rows, width = parts.shape
    cut = width // (devices // tp_count)
    operands = [parts] + ([] if state is None else [state]) + [ln_gain, ln_bias]
    return pl.pallas_call(
        functools.partial(norm_kernel, layer_index, tp_count),
        out_shape=(
            jax.ShapeDtypeStruct((rows, width), jnp.float32),
            jax.ShapeDtypeStruct((devices, rows, cut), jnp.bfloat16),
        ),
        in_specs=[whole()] * len(operands),
        out_specs=(whole(), whole()),
        compiler_params=compiler_params(16),
        name="norm_rows",
    )(*operands)


def last_parts_kernel(tp_count, part_ref, state_ref, out_ref):
    total = part_ref[0].astype(jnp.float32)
    for chip in range(1, part_ref.shape[0]):
        total = total + part_ref[chip].astype(jnp.float32)
    mine = state_ref.shape[0]
    owner = lax.axis_index("tp")
    for place in range(tp_count):
        rows = slice(place * mine, (place + 1) * mine)
        total_rows = total[rows] + jnp.where(owner == place, 1.0, 0.0) * state_ref[...]
        out_ref[rows] = total_rows


def last_parts(parts, state, tp_count):
    return pl.pallas_call(
        functools.partial(last_parts_kernel, tp_count),
        out_shape=jax.ShapeDtypeStruct(parts.shape[1:], jnp.float32),
        in_specs=[whole(), whole()],
        out_specs=whole(),
        compiler_params=compiler_params(16),
        name="last_parts",
    )(parts, state)


def last_kernel(a_ref, b_ref, c_ref, d_ref, out_ref):
    near = a_ref[...].astype(jnp.float32) + b_ref[...].astype(jnp.float32)
    far = c_ref[...].astype(jnp.float32) + d_ref[...].astype(jnp.float32)
    out_ref[...] = (near + far).astype(jnp.bfloat16)


def last_rows(parts):
    return pl.pallas_call(
        last_kernel,
        out_shape=jax.ShapeDtypeStruct(parts[0].shape, jnp.bfloat16),
        in_specs=[whole()] * 4,
        out_specs=whole(),
        compiler_params=compiler_params(16),
        name="last_rows",
    )(*parts)


def back_kernel(new_tokens, group_ref, near_ref, far_ref):
    rows, half = near_ref.shape
    requests = group_ref.shape[1]
    rank_row = ranks(group_ref)
    line = lax.broadcasted_iota(jnp.int32, (rows, requests), 0)
    column = lax.broadcasted_iota(jnp.int32, (rows, requests), 1)
    wanted = jnp.sum(jnp.where(column == line // new_tokens, rank_row, 0), axis=1, keepdims=True)
    line = lax.broadcasted_iota(jnp.int32, near_ref.shape, 0)
    entry = lax.broadcasted_iota(jnp.int32, near_ref.shape, 1)
    share = half // CHIPS
    here = lax.axis_index("seq") // 2
    for ref, other in ((near_ref, False), (far_ref, True)):
        held = (((entry // share) ^ here) * 2 + core_parity(other)) * share + entry % share
        back = held == wanted * new_tokens + line % new_tokens
        ref[...] = jnp.where(back, 1.0, 0.0).astype(jnp.bfloat16)


def back_rows(group_of, new_tokens):
    rows = group_of.shape[0] * new_tokens
    one = jax.ShapeDtypeStruct((rows, rows // 2), jnp.bfloat16)
    return pl.pallas_call(
        functools.partial(back_kernel, new_tokens),
        out_shape=(one, one),
        in_specs=[whole()],
        out_specs=(whole(), whole()),
        compiler_params=compiler_params(16),
        name="back_rows",
    )(group_of[None, :])


def restore_kernel(near_back_ref, far_back_ref, *refs):
    *row_refs, out_ref = refs
    requests, new_tokens, width = out_ref.shape
    step = 2 * LANES
    for start in range(0, width, step):
        span = slice(start, start + step)
        near, far = (
            jnp.concatenate([ref[:, span] for ref in half], axis=0)
            for half in (row_refs[:CHIPS], row_refs[CHIPS:])
        )
        rows = jnp.dot(near_back_ref[...], near, preferred_element_type=jnp.float32) + jnp.dot(
            far_back_ref[...], far, preferred_element_type=jnp.float32
        )
        out_ref[:, :, span] = rows.reshape(requests, new_tokens, step)


def restore(backs, near, far, new_tokens):
    rows = backs[0].shape[0]
    return pl.pallas_call(
        restore_kernel,
        out_shape=jax.ShapeDtypeStruct((rows // new_tokens, new_tokens, near[0].shape[1]), jnp.float32),
        in_specs=[whole()] * (2 + 2 * CHIPS),
        out_specs=whole(),
        compiler_params=compiler_params(24),
        name="restore",
    )(*backs, *near, *far)


def core_parity(other):
    return 1 - lax.axis_index("seq") % 2 if other else lax.axis_index("seq") % 2


def heads_kernel(joins, hidden_ref, qkv_ref, *refs):
    if joins:
        arrived_ref, near_ref, *out_hbms, out_ref, semaphores = refs
    else:
        out_ref = refs[0]
    parity = core_parity(not joins)
    here = lax.axis_index("seq") // 2
    rows, unit = hidden_ref.shape
    width = qkv_ref.shape[1] // 3
    share = rows // CHIPS // 2
    half = rows // 2
    pieces = width // unit
    tall = 2 * pieces * share

    def joined(values, start):
        if joins:
            values = values + arrived_ref[start : start + values.shape[0]].astype(jnp.float32)
        return values.astype(jnp.bfloat16)

    def picked(chips):
        return jnp.concatenate(
            [
                hidden_ref[pl.ds(pl.multiple_of((2 * chip + parity) * share, share), share), :]
                for chip in chips
            ],
            axis=0,
        )

    queries = jnp.dot(picked(range(CHIPS)), qkv_ref[:, :width], preferred_element_type=jnp.float32)
    for piece in range(pieces):
        start = piece * half
        query = joined(queries[:, piece * unit : (piece + 1) * unit], start)
        if joins:
            for distance in range(CHIPS):
                out_ref[distance, tall + start : tall + start + half] = query
        else:
            out_ref[start : start + half] = query
    others = jnp.dot(
        picked([here ^ distance for distance in range(CHIPS)]), qkv_ref[:, width:], preferred_element_type=jnp.float32
    )
    base = pieces * half
    leaving = []
    for distance in reversed(range(CHIPS)):
        for piece in range(2 * pieces):
            start = base + (distance * 2 * pieces + piece) * share
            value = joined(
                others[distance * share : (distance + 1) * share, piece * unit : (piece + 1) * unit], start
            )
            if joins:
                out_ref[distance, piece * share : (piece + 1) * share] = value
            else:
                out_ref[start : start + share] = value
        if joins and distance:
            copy = pltpu.make_async_copy(
                out_ref.at[distance], out_hbms[distance - 1], semaphores.at[distance - 1]
            )
            copy.start()
            leaving.append(copy)
    if joins:
        near_ref[...] = out_ref[0]
    for copy in leaving:
        copy.wait()


def project_heads(hidden, weights_qkv, unit, arrived=None):
    rows = hidden.shape[0]
    pieces = weights_qkv.shape[1] // 3 // unit
    tall = 2 * pieces * (rows // CHIPS // 2)
    common = pieces * (rows // 2)
    extra = [] if arrived is None else [arrived]
    out_shape = jax.ShapeDtypeStruct((common + CHIPS * tall, unit), jnp.bfloat16)
    out_specs = whole()
    scratch = []
    if arrived is not None:
        one = (tall + common, unit)
        out_shape = (jax.ShapeDtypeStruct(one, jnp.bfloat16),) + (pltpu.HBM(one, jnp.bfloat16),) * (CHIPS - 1)
        out_specs = (whole(),) + (whole(pltpu.HBM),) * (CHIPS - 1)
        scratch = [pltpu.VMEM((CHIPS,) + one, jnp.bfloat16), pltpu.SemaphoreType.DMA((CHIPS - 1,))]
    return pl.pallas_call(
        functools.partial(heads_kernel, arrived is not None),
        out_shape=out_shape,
        in_specs=[whole()] * (2 + len(extra)),
        out_specs=out_specs,
        scratch_shapes=scratch,
        compiler_params=compiler_params(24),
        name="project_heads",
    )(hidden, weights_qkv, *extra)


def units_kernel(joins, hidden_ref, fc1_ref, *refs):
    arrived_ref, out_refs = (refs[0], refs[1:]) if joins else (None, refs)
    parity = core_parity(not joins)
    here = lax.axis_index("seq") // 2
    unit = fc1_ref.shape[2] // CHIPS // 2
    hidden = hidden_ref[...]
    for distance in range(CHIPS):
        target = 2 * (here ^ distance) + parity
        columns = pl.ds(pl.multiple_of(target * unit, unit), unit)
        pre = jnp.dot(hidden, fc1_ref[0, :, columns], preferred_element_type=jnp.float32)
        if joins:
            pre = pre + arrived_ref[distance].astype(jnp.float32)
            out_refs[distance][...] = pre.astype(jnp.bfloat16)
        else:
            out_refs[0][distance] = pre.astype(jnp.bfloat16)


def project_units(hidden, w_fc1, layer_index, arrived=None):
    rows = hidden.shape[0]
    unit = w_fc1.shape[2] // CHIPS // 2
    extra = [] if arrived is None else [arrived]
    if arrived is None:
        out_shape = jax.ShapeDtypeStruct((CHIPS, rows, unit), jnp.bfloat16)
    else:
        out_shape = (jax.ShapeDtypeStruct((rows, unit), jnp.bfloat16),) * CHIPS
    return pl.pallas_call(
        functools.partial(units_kernel, arrived is not None),
        grid=(1,),
        out_shape=out_shape,
        in_specs=[same_block(hidden.shape), layer_block(layer_index, w_fc1.shape[1:])]
        + [same_block(values.shape) for values in extra],
        out_specs=jax.tree.map(lambda leaf: same_block(leaf.shape), out_shape),
        compiler_params=compiler_params(24),
        name="project_units",
    )(hidden, w_fc1, *extra)


def activate_kernel(a_ref, b_ref, c_ref, d_ref, table_ref, query_ref, key_ref, value_ref):
    near = a_ref[...].astype(jnp.float32) + b_ref[...].astype(jnp.float32)
    far = c_ref[...].astype(jnp.float32) + d_ref[...].astype(jnp.float32)
    total = near + far
    share, width = key_ref.shape
    half = query_ref.shape[0]
    unit = a_ref.shape[1]
    lanes = table_ref.shape[2]
    pieces = width // unit
    own = pl.ds(pl.multiple_of((lax.axis_index("seq") // 2) * share, share), share)

    def put(target_ref, start, height, span, scale):
        for piece in range(pieces):
            for column in range(0, unit, lanes):
                first = start + piece * height
                values = total[first : first + height, column : column + lanes]
                if span is not None:
                    values = (
                        values * table_ref[0, span]
                        + pltpu.roll(values, lanes - ROT // 2, 1) * table_ref[1, span]
                        + pltpu.roll(values, ROT // 2, 1) * table_ref[2, span]
                    )
                values = values.astype(jnp.bfloat16)
                if scale is not None:
                    values = (values.astype(jnp.float32) * scale).astype(jnp.bfloat16)
                column_out = piece * unit + column
                target_ref[:, column_out : column_out + lanes] = values

    put(key_ref, 0, share, own, None)
    put(value_ref, pieces * share, share, None, None)
    put(query_ref, 2 * pieces * share, half, slice(None), 1.0 / math.sqrt(HEAD_DIM))


def activate(parts, tables, width):
    half = tables.shape[1]
    small = jax.ShapeDtypeStruct((half // CHIPS, width), jnp.bfloat16)
    return pl.pallas_call(
        activate_kernel,
        out_shape=(jax.ShapeDtypeStruct((half, width), jnp.bfloat16), small, small),
        in_specs=[whole()] * 5,
        out_specs=(whole(),) * 3,
        compiler_params=compiler_params(16),
        name="activate",
    )(*parts, tables)


def rotary_tables(positions, width):
    half = ROT // 2
    feature = lax.broadcasted_iota(jnp.int32, (1, width), 1) % HEAD_DIM
    frequency = jnp.exp((feature % half).astype(jnp.float32) * (-2.0 * math.log(10000.0) / ROT))
    angles = positions.astype(jnp.float32)[:, None] * frequency
    cosine, sine = jnp.cos(angles), jnp.sin(angles)
    return jnp.stack(
        [
            jnp.where(feature < ROT, cosine, 1.0),
            jnp.where(feature < half, -sine, 0.0),
            jnp.where((feature >= half) & (feature < ROT), sine, 0.0),
        ]
    )


def attend_kernel(
    layer_index, new_tokens,
    visit_hbm, query_ref, far_query_ref, new_key_ref, new_value_ref,
    key_hbm, value_hbm, out_ref,
    key_ref, value_ref, visit_ref, both_ref, score_ref, top_ref, sum_ref, mix_ref, semaphores, visit_semaphore,
):
    blocks = visit_ref.shape[0] // 4
    groups, tall, lanes = mix_ref.shape
    share = new_key_ref.shape[0]
    heads = tall // share
    chunks = semaphores.shape[1]
    chunk = key_ref.shape[0] // chunks

    def copy(kind, index):
        span = pl.ds(index * chunk, chunk)
        source, target = ((key_hbm, key_ref), (value_hbm, value_ref))[kind]
        return pltpu.make_async_copy(
            source.at[layer_index, span], target.at[span], semaphores.at[kind, index]
        )

    looking = pltpu.make_async_copy(visit_hbm, visit_ref, visit_semaphore)
    looking.start()
    for kind in range(2):
        for index in range(chunks):
            copy(kind, index).start()
    core = lax.axis_index("seq") % 2
    for chip in range(groups // 2):
        span = slice(chip * share, (chip + 1) * share)
        both_ref[2 * chip + core] = query_ref[span]
        both_ref[2 * chip + 1 - core] = far_query_ref[span]
    lane = lax.broadcasted_iota(jnp.int32, (share, lanes), 1)
    row = lax.broadcasted_iota(jnp.int32, (share, lanes), 0)
    top_ref[...] = jnp.full(top_ref.shape, very_negative, jnp.float32)
    sum_ref[...] = jnp.zeros(sum_ref.shape, jnp.float32)
    mix_ref[...] = jnp.zeros(mix_ref.shape, jnp.float32)

    def score(index, group, keys, mask):
        scores = []
        for pair in range(heads // 2):
            both = both_ref[group, :, pair * lanes : (pair + 1) * lanes]
            none = jnp.zeros_like(both)
            split = jnp.concatenate(
                [jnp.where(lane < HEAD_DIM, both, none), jnp.where(lane < HEAD_DIM, none, both)], axis=0
            )
            scores.append(
                lax.dot_general(
                    split, keys[:, pair * lanes : (pair + 1) * lanes], (((1,), (1,)), ((), ())),
                    preferred_element_type=jnp.float32,
                )
            )
        scores = jnp.concatenate(scores, axis=0).reshape(heads, share, BLOCK)
        scores = jnp.where(mask[None], scores, very_negative).reshape(tall, BLOCK)
        score_ref[index] = scores
        top_ref[group] = jnp.maximum(top_ref[group], scores)

    def mix(index, group, values):
        weight = jnp.exp(score_ref[index] - top_ref[group])
        sum_ref[group] += weight
        rounded = weight.astype(jnp.bfloat16)
        mix_ref[group] += jnp.concatenate(
            [
                jnp.dot(
                    rounded[pair * 2 * share : (pair + 1) * 2 * share],
                    values[:, pair * lanes : (pair + 1) * lanes],
                    preferred_element_type=jnp.float32,
                )
                for pair in range(heads // 2)
            ],
            axis=0,
        )

    own = lax.axis_index("seq")
    fill = jnp.zeros((BLOCK - share, new_key_ref.shape[1]), jnp.bfloat16)
    score(
        blocks, own, jnp.concatenate([new_key_ref[...], fill], axis=0),
        (lane // new_tokens == row // new_tokens) & (lane <= row),
    )
    looking.wait()
    owners = []
    for block in range(blocks):
        if (block * BLOCK) % chunk == 0:
            copy(0, block * BLOCK // chunk).wait()
        group, live, first, end = (visit_ref[field * blocks + block] for field in range(4))
        owners.append(group)
        score(
            block, group, key_ref[block * BLOCK : (block + 1) * BLOCK, :],
            (lane < live) & (row >= first) & (row < end),
        )
    for group in range(groups):
        top = jnp.max(top_ref[group], axis=1, keepdims=True)
        top_ref[group] = jnp.broadcast_to(top, (tall, lanes))
    mix(blocks, own, jnp.concatenate([new_value_ref[...], fill], axis=0))
    for block in range(blocks):
        if (block * BLOCK) % chunk == 0:
            copy(1, block * BLOCK // chunk).wait()
        mix(block, owners[block], value_ref[block * BLOCK : (block + 1) * BLOCK, :])

    level = jnp.zeros((tall, lanes), jnp.float32)
    column = lax.broadcasted_iota(jnp.int32, (tall, lanes), 1)

    def mean(group):
        total = jnp.sum(sum_ref[group], axis=1, keepdims=True)
        total = jnp.where(total <= 0.0, 1.0, total)
        own_level = jnp.where(column == group, top_ref[group] + jnp.log(total), 0.0)
        return mix_ref[group] / total, own_level

    for group in range(groups // 2):
        left, left_level = mean(group)
        right, right_level = mean(group + groups // 2)
        level = level + left_level + right_level
        for head in range(heads):
            rows = slice(head * share, (head + 1) * share)
            first, second = left[rows], right[rows]
            if head % 2:
                first = pltpu.roll(first, HEAD_DIM, 1)
            else:
                second = pltpu.roll(second, HEAD_DIM, 1)
            packed = jnp.where(lane < HEAD_DIM, first, second)
            out_ref[head, group * share : (group + 1) * share] = packed.astype(jnp.bfloat16)
    level = level.T[:groups]
    high = level.astype(jnp.bfloat16).astype(jnp.float32)
    middle = (level - high).astype(jnp.bfloat16).astype(jnp.float32)
    low = level - high - middle
    rest = jnp.concatenate([high, middle, low, jnp.zeros_like(low)], axis=0).astype(jnp.bfloat16)
    start = (groups // 2) * share
    for head in range(heads):
        column = head * share // lanes * lanes
        out_ref[head, start:] = rest[:, column : column + lanes]


def attend(visits, query, far_query, new_key, new_value, k_cache, v_cache, layer_index, new_tokens, groups):
    width = query.shape[1]
    rows = 2 * query.shape[0]
    slots = k_cache.shape[1]
    heads = width // HEAD_DIM
    share = rows // groups
    tall = heads * share
    lanes = 2 * HEAD_DIM
    chunks = 2
    state = pltpu.VMEM((groups, tall, lanes), jnp.float32)
    return pl.pallas_call(
        functools.partial(attend_kernel, layer_index, new_tokens),
        out_shape=jax.ShapeDtypeStruct((heads, rows // 2 + 4 * groups, lanes), jnp.bfloat16),
        in_specs=[whole(pltpu.HBM)] + [whole()] * 4 + [whole(pltpu.HBM)] * 2,
        out_specs=whole(),
        scratch_shapes=[
            pltpu.VMEM((slots, width), jnp.bfloat16),
            pltpu.VMEM((slots, width), jnp.bfloat16),
            pltpu.SMEM(visits.shape, jnp.int32),
            pltpu.VMEM((groups, share, width), jnp.bfloat16),
            pltpu.VMEM((visits.shape[0] // 4 + 1, tall, BLOCK), jnp.float32),
            state,
            state,
            state,
            pltpu.SemaphoreType.DMA((2, chunks)),
            pltpu.SemaphoreType.DMA,
        ],
        compiler_params=compiler_params(24),
        name="attend",
    )(in_hbm(visits), query, far_query, new_key, new_value, in_hbm(k_cache), in_hbm(v_cache))


def update_kernel(
    layer_index, other, tp_count, has_start, part_ref, bias_ref, out_weight_ref, fc2_ref, *refs
):
    *unit_refs, out_ref, scale_ref = refs
    if has_start:
        *unit_refs, start_ref = unit_refs
    seq_index = lax.axis_index("seq")
    parity = 1 - seq_index % 2 if other else seq_index % 2
    sources, tall, lanes = part_ref.shape
    unit = unit_refs[0].shape[1]
    share = unit_refs[0].shape[0] // sources
    groups = (tall - (sources // 2) * share) // 4
    levels = []
    for source in range(sources):
        parts = part_ref[source, (sources // 2) * share :, :].astype(jnp.float32)
        levels.append(parts[:groups] + parts[groups : 2 * groups] + parts[2 * groups : 3 * groups])
    top = functools.reduce(jnp.maximum, levels)
    scales = [jnp.exp(level - top) for level in levels]
    total = functools.reduce(jnp.add, scales)
    scales = [scale / total for scale in scales]
    blank = jnp.zeros((lanes - groups * sources, lanes), jnp.float32)
    scale_ref[...] = jnp.concatenate(scales + [blank], axis=0).T
    place = seq_index % (lanes // share)
    scale = scale_ref[pl.ds(pl.multiple_of(place * share, share), share), :]
    scale = jnp.where(parity == 0, scale, pltpu.roll(scale, lanes - 1, 1))
    lane = lax.broadcasted_iota(jnp.int32, (share, lanes), 1)
    first, second = [], []
    for pair in range(CHIPS // 2):
        rows = pl.ds(pl.multiple_of((2 * pair + parity) * share, share), share)
        mixed = jnp.zeros((share, lanes), jnp.float32)
        for source in range(sources):
            column = source * groups + 2 * pair
            left = scale[:, column : column + 1]
            right = scale[:, column + groups // 2 : column + groups // 2 + 1]
            mixed = mixed + part_ref[source, rows, :].astype(jnp.float32) * jnp.where(
                lane < HEAD_DIM, left, right
            )
        first.append(mixed[:, :HEAD_DIM])
        second.append(pltpu.roll(mixed, HEAD_DIM, 1)[:, :HEAD_DIM])
    attended = jnp.concatenate(first + second, axis=0).astype(jnp.bfloat16)
    bias = bias_ref[
        layer_index : layer_index + 1, pl.ds(pl.multiple_of(seq_index * unit, unit), unit)
    ]
    hidden, started = [], []
    for piece in range(CHIPS):
        rows = pl.ds(pl.multiple_of((2 * piece + parity) * share, share), share)
        pre = functools.reduce(jnp.add, [ref[rows, :].astype(jnp.float32) for ref in unit_refs])
        hidden.append(jax.nn.gelu(pre + bias, approximate=True).astype(jnp.bfloat16))
        if has_start:
            started.append(start_ref[rows, :].astype(jnp.float32))
    change = jnp.dot(attended, out_weight_ref[0], preferred_element_type=jnp.float32) + jnp.dot(
        jnp.concatenate(hidden, axis=0), fc2_ref[0], preferred_element_type=jnp.float32
    )
    if not has_start:
        out_ref[...] = change.astype(out_ref.dtype)
        return
    started = jnp.concatenate(started, axis=0)
    for column in range(0, change.shape[1], unit):
        here = (seq_index * unit == column) & (lax.axis_index("tp") == 0)
        out_ref[:, column : column + unit] = (
            change[:, column : column + unit] + jnp.where(here, started, 0.0)
        ).astype(out_ref.dtype)


def update(parts, units, start, b_fc1, w_out, w_fc2, layer_index, other, tp_count):
    rows = units[0].shape[0] // 2
    width = w_out.shape[2]
    lanes = parts.shape[2]
    extra = list(units) + ([] if start is None else [start])
    return pl.pallas_call(
        functools.partial(update_kernel, layer_index, other, tp_count, start is not None),
        grid=(1,),
        out_shape=jax.ShapeDtypeStruct((rows, width), jnp.bfloat16 if other else jnp.float32),
        in_specs=[
            same_block(parts.shape),
            same_block(b_fc1.shape),
            layer_block(layer_index, w_out.shape[1:]),
            layer_block(layer_index, w_fc2.shape[1:]),
        ]
        + [same_block(units[0].shape)] * len(extra),
        out_specs=same_block((rows, width)),
        scratch_shapes=[pltpu.VMEM((lanes, lanes), jnp.float32)],
        compiler_params=compiler_params(),
        name="update",
    )(parts, b_fc1, w_out, w_fc2, *extra)


def per_device(
    token_ids, embedding, group_of, prefix_len, tail_len, block_map, k_cache, v_cache,
    ln_gain, ln_bias, w_qkv, w_fc1, b_fc1, w_out, w_fc2,
):
    seq_count, tp_count = lax.axis_size("seq"), lax.axis_size("tp")
    seq_index, tp_index = lax.axis_index("seq"), lax.axis_index("tp")
    devices = seq_count * tp_count
    core = seq_index % 2
    requests, new_tokens = token_ids.shape
    rows = requests * new_tokens
    groups = prefix_len.shape[0]
    share = rows // seq_count
    mine = rows // devices
    features = embedding.shape[1]
    width_local = k_cache.shape[2]
    unit = w_fc2.shape[1]
    same_core = [[s * tp_count + p for s in range(c, seq_count, 2) for p in range(tp_count)] for c in range(2)]
    same_core_seq = [list(range(c, seq_count, 2)) for c in range(2)]

    def to_owners(half):
        parts = half.reshape(devices // 2, mine, features)
        return lax.all_to_all(parts, ("seq", "tp"), 0, 0, axis_index_groups=same_core)

    def to_chips(parts):
        return lax.all_to_all(parts, "seq", 0, 0, axis_index_groups=same_core_seq)

    def to_distances(parts):
        return [parts[0]] + [
            lax.ppermute(parts[k], "seq", [(i, i ^ (2 * k)) for i in range(seq_count)])
            for k in range(1, CHIPS)
        ]

    def over_tp(part, distance):
        return lax.ppermute(part, "tp", [(i, i ^ distance) for i in range(tp_count)])

    def from_tp(part):
        return [part] + [over_tp(part, k) for k in range(1, tp_count)]

    near, far, own = embed(token_ids, group_of, embedding, unit)
    parts = join(near, swap_cores(far, seq_count), own)
    gathered = gather(to_distances(parts))
    gathered, group_of = lax.optimization_barrier((gathered, group_of))
    rank, positions, visits = order_requests(group_of, prefix_len, tail_len, block_map, new_tokens)
    own_positions = lax.dynamic_index_in_dim(positions.reshape(CHIPS, 2, share), core, 1, keepdims=False)
    backs = back_rows(group_of, new_tokens)
    tables = rotary_tables(own_positions.reshape(-1), 2 * HEAD_DIM)
    weights_qkv = w_qkv[0].reshape(w_qkv.shape[1], -1)
    parts, backs, tables, visits = lax.optimization_barrier((from_tp(gathered), backs, tables, visits))
    start, hidden = first_hidden(parts, ln_gain, ln_bias)
    state = None
    for layer_index in range(LAYERS):
        if layer_index:
            weights_qkv = w_qkv[layer_index].reshape(w_qkv.shape[1], -1)
            state, cut = norm_rows(parts, state, ln_gain, ln_bias, layer_index, devices, tp_count)
            hidden = lax.all_to_all(cut, ("seq", "tp"), 0, 0).reshape(rows, -1)
        arriving = swap_cores(project_heads(hidden, weights_qkv, unit), seq_count)
        heads = to_distances(project_heads(hidden, weights_qkv, unit, arriving))
        arriving = swap_cores(project_units(hidden, w_fc1, layer_index), seq_count)
        units = project_units(hidden, w_fc1, layer_index, arriving)
        query, new_key, new_value = activate(heads, tables, width_local)
        units = to_distances(units)
        parts = attend(
            visits, query, swap_cores(query, seq_count), new_key, new_value,
            k_cache, v_cache, layer_index, new_tokens, groups,
        )
        parts, *units = lax.optimization_barrier((parts, *units))
        parts = lax.all_to_all(parts, "seq", 0, 0)
        arriving, half = (
            update(parts, units, start, b_fc1, w_out, w_fc2, layer_index, other, tp_count)
            for other in (True, False)
        )
        half = (half + swap_cores(arriving, seq_count).astype(jnp.float32)).astype(jnp.bfloat16)
        start = None
        if layer_index < LAYERS - 1:
            parts = to_owners(half)
    last = last_parts(to_chips(half.reshape(CHIPS, share, features)), state, tp_count)
    last = from_tp(last.astype(jnp.bfloat16))
    last = to_distances([last_rows(last)] * CHIPS)
    return restore(backs, last, [swap_cores(part, seq_count) for part in last], new_tokens)


def solution(mesh):
    in_specs = (
        P(),
        P(("seq", "tp"), None),
        P(),
        P(),
        P(),
        P("seq", None),
        P(None, "seq", "tp"),
        P(None, "seq", "tp"),
        P(),
        P(),
        P(None, "seq", None, "tp"),
        P(None, "seq", "tp"),
        P(None, "tp"),
        P(None, ("tp", "seq"), None),
        P(None, ("tp", "seq"), None),
    )
    out_specs = P()
    seq_count, tp_count = mesh.shape["seq"], mesh.shape["tp"]
    fits = tp_count == 4 and seq_count == HEADS // tp_count and seq_count == 2 * CHIPS
    return jax.shard_map(
        per_device if fits else per_device_any, mesh=mesh, in_specs=in_specs, out_specs=out_specs, check_vma=False
    )
```

```python
import functools
import math

import jax
import jax.numpy as jnp
from jax import lax
from jax.experimental import pallas as pl
from jax.experimental.pallas import tpu as pltpu
from jax.sharding import PartitionSpec as P

HEADS = 32
HEAD_DIM = 64
ROT = 32
LAYERS = 2
BLOCK = 128
SPAN = 512
CHIPS = 4
LANES = 128


very_negative = -1e30


def layer_norm(values, gain_row, bias_row):
    average = jnp.mean(values, axis=-1, keepdims=True)
    centred = values - average
    variance = jnp.mean(centred * centred, axis=-1, keepdims=True)
    return centred * lax.rsqrt(variance + 1e-05) * gain_row + bias_row


def rotary(values, positions):
    half_width = ROT // 2
    frequency = jnp.exp(
        jnp.arange(half_width, dtype=jnp.float32) * (-2.0 * math.log(10000.0) / ROT)
    )
    angles = positions.astype(jnp.float32)[:, None] * frequency[None, :]
    cosine = jnp.cos(angles)[:, None, :]
    sine_part = jnp.sin(angles)[:, None, :]
    low_half = values[..., :half_width]
    high_half = values[..., half_width:ROT]
    return jnp.concatenate(
        [
            low_half * cosine - high_half * sine_part,
            high_half * cosine + low_half * sine_part,
            values[..., ROT:],
        ],
        axis=-1,
    )


def combine_parts(left_part, right_part):
    max_left, sum_left, out_left = left_part
    max_right, sum_right, out_right = right_part
    top_value = jnp.maximum(max_left, max_right)
    scale_left = jnp.exp(max_left - top_value)
    scale_right = jnp.exp(max_right - top_value)
    return (
        top_value,
        sum_left * scale_left + sum_right * scale_right,
        out_left * scale_left[..., None] + out_right * scale_right[..., None],
    )


def full_total(values):
    return lax.psum(values, ("seq", "tp"))


def per_device_any(
    token_ids,
    embedding,
    group_of,
    prefix_len,
    tail_len,
    block_map,
    k_cache,
    v_cache,
    ln_gain,
    ln_bias,
    w_qkv,
    w_fc1,
    b_fc1,
    w_out,
    w_fc2,
):
    tp_count = lax.axis_size("tp")
    seq_index = lax.axis_index("seq")
    tp_index = lax.axis_index("tp")
    requests = token_ids.shape[0]
    new_tokens = token_ids.shape[1]
    groups = prefix_len.shape[0]
    heads_local = HEADS // tp_count
    width_local = heads_local * HEAD_DIM
    score_scale = 1.0 / math.sqrt(HEAD_DIM)
    vocab_rows = embedding.shape[0]
    first_row = (seq_index * tp_count + tp_index) * vocab_rows
    local_ids = token_ids.reshape(-1) - first_row
    inside = (local_ids >= 0) & (local_ids < vocab_rows)
    picked = jnp.take(embedding, jnp.clip(local_ids, 0, vocab_rows - 1), axis=0).astype(jnp.float32)
    picked = jnp.where(inside[:, None], picked, 0.0)
    start_states = full_total(picked).reshape(requests, new_tokens, -1)
    group_hit = group_of[:, None] == jnp.arange(groups, dtype=jnp.int32)[None, :]
    shared_len = jnp.sum(jnp.where(group_hit, prefix_len[None, :], 0), axis=1)
    base_positions = shared_len + tail_len
    seg_len = jnp.concatenate([prefix_len, tail_len])
    seg_count = seg_len.shape[0]
    blocks_local = block_map.shape[0]
    seg_blk = block_map[:, 0]
    rank_blk = block_map[:, 1]
    seg_hit = seg_blk[:, None] == jnp.arange(seg_count, dtype=jnp.int32)[None, :]
    len_blk = jnp.sum(jnp.where(seg_hit, seg_len[None, :], 0), axis=1)
    slot_positions = rank_blk[:, None] * BLOCK + jnp.arange(BLOCK, dtype=jnp.int32)[None, :]
    live_slot = ((seg_blk[:, None] >= 0) & (slot_positions < len_blk[:, None])).reshape(-1)
    seg_slot = jnp.broadcast_to(seg_blk[:, None], (blocks_local, BLOCK)).reshape(-1)
    own_tail = seg_slot[None, :] == (groups + jnp.arange(requests, dtype=jnp.int32))[:, None]
    own_prompt = seg_slot[None, :] == group_of[:, None]
    allowed = (own_tail | own_prompt) & live_slot[None, :]
    step_count = allowed.shape[1] // SPAN
    allowed_steps = allowed.reshape(requests, step_count, SPAN).transpose(1, 0, 2)
    rows_local = w_qkv.shape[1]
    unit_count = w_fc2.shape[1]
    sub_width = w_out.shape[1]
    token_index = jnp.arange(new_tokens, dtype=jnp.int32)
    new_keys = [
        jnp.zeros((requests, new_tokens, heads_local, HEAD_DIM), jnp.bfloat16)
        for layer_index in range(LAYERS)
    ]
    new_values = [
        jnp.zeros((requests, new_tokens, heads_local, HEAD_DIM), jnp.bfloat16)
        for layer_index in range(LAYERS)
    ]
    results = []
    for token_step in range(new_tokens):
        hidden_state = start_states[:, token_step]
        positions = base_positions + token_step
        for layer_index in range(LAYERS):
            normed = layer_norm(hidden_state, ln_gain[layer_index], ln_bias[layer_index]).astype(
                jnp.bfloat16
            )
            my_rows = lax.dynamic_slice_in_dim(normed, seq_index * rows_local, rows_local, 1)
            part_proj = jnp.dot(
                my_rows,
                w_qkv[layer_index].reshape(rows_local, -1),
                preferred_element_type=jnp.float32,
            )
            part_fc1 = jnp.dot(my_rows, w_fc1[layer_index], preferred_element_type=jnp.float32)
            attention_proj, fc1_all = lax.psum((part_proj, part_fc1), "seq")
            pre_act = lax.dynamic_slice_in_dim(fc1_all, seq_index * unit_count, unit_count, 1)
            pre_act = (
                pre_act
                + lax.dynamic_slice_in_dim(
                    b_fc1[layer_index], seq_index * unit_count, unit_count, 0
                )[None, :]
            )
            activated = jax.nn.gelu(pre_act, approximate=True).astype(jnp.bfloat16)
            attention_proj = attention_proj.reshape(requests, 3, heads_local, HEAD_DIM)
            queries = rotary(attention_proj[:, 0], positions).astype(jnp.bfloat16)
            key_rows = rotary(attention_proj[:, 1], positions).astype(jnp.bfloat16)
            value_rows = attention_proj[:, 2].astype(jnp.bfloat16)
            new_keys[layer_index] = new_keys[layer_index].at[:, token_step].set(key_rows)
            new_values[layer_index] = new_values[layer_index].at[:, token_step].set(value_rows)
            key_steps = k_cache[layer_index].reshape(step_count, SPAN, heads_local, HEAD_DIM)
            value_steps = v_cache[layer_index].reshape(step_count, SPAN, heads_local, HEAD_DIM)

            def cache_step(carry, inputs):
                run_max, run_sum, run_out = carry
                key_block, value_block, allow_block = inputs
                scores = (
                    jnp.einsum(
                        "rhd,shd->hrs", queries, key_block, preferred_element_type=jnp.float32
                    )
                    * score_scale
                )
                scores = jnp.where(allow_block[None], scores, very_negative)
                next_max = jnp.maximum(run_max, jnp.max(scores, axis=2))
                weights = jnp.where(allow_block[None], jnp.exp(scores - next_max[..., None]), 0.0)
                shrink = jnp.exp(run_max - next_max)
                next_sum = run_sum * shrink + jnp.sum(weights, axis=2)
                next_out = run_out * shrink[..., None] + jnp.einsum(
                    "hrs,shd->hrd",
                    weights.astype(jnp.bfloat16),
                    value_block,
                    preferred_element_type=jnp.float32,
                )
                return ((next_max, next_sum, next_out), None)

            start_carry = (
                jnp.full((heads_local, requests), very_negative, jnp.float32),
                jnp.zeros((heads_local, requests), jnp.float32),
                jnp.zeros((heads_local, requests, HEAD_DIM), jnp.float32),
            )
            (part_max, part_sum, part_out), unused = lax.scan(
                cache_step, start_carry, (key_steps, value_steps, allowed_steps)
            )
            cache_max = lax.pmax(part_max, "seq")
            factor = jnp.exp(part_max - cache_max)
            cache_sum, cache_out = (
                lax.psum((part_sum * factor).astype(jnp.bfloat16), "seq").astype(jnp.float32),
                lax.psum((part_out * factor[..., None]).astype(jnp.bfloat16), "seq").astype(
                    jnp.float32
                ),
            )
            visible = (token_index <= token_step)[None, None, :]
            fresh_scores = (
                jnp.einsum(
                    "rhd,rjhd->hrj",
                    queries,
                    new_keys[layer_index],
                    preferred_element_type=jnp.float32,
                )
                * score_scale
            )
            fresh_scores = jnp.where(visible, fresh_scores, very_negative)
            fresh_max = jnp.max(fresh_scores, axis=2)
            fresh_weights = jnp.where(visible, jnp.exp(fresh_scores - fresh_max[..., None]), 0.0)
            fresh_sum = jnp.sum(fresh_weights, axis=2)
            fresh_out = jnp.einsum(
                "hrj,rjhd->hrd",
                fresh_weights.astype(jnp.bfloat16),
                new_values[layer_index],
                preferred_element_type=jnp.float32,
            )
            joint_max, denom_total, weighted = combine_parts(
                (cache_max, cache_sum, cache_out), (fresh_max, fresh_sum, fresh_out)
            )
            attended = (weighted / denom_total[..., None]).astype(jnp.bfloat16)
            attended = attended.transpose(1, 0, 2).reshape(requests, width_local)
            my_cols = lax.dynamic_slice_in_dim(attended, seq_index * sub_width, sub_width, 1)
            update = jnp.dot(my_cols, w_out[layer_index], preferred_element_type=jnp.float32)
            update = update + jnp.dot(
                activated, w_fc2[layer_index], preferred_element_type=jnp.float32
            )
            hidden_state = hidden_state + full_total(update)
        results.append(hidden_state)
    stacked = jnp.stack(results, axis=1)
    return stacked


def swap_cores(values, seq_count):
    return lax.ppermute(values, "seq", [(i, i ^ 1) for i in range(seq_count)])


def in_hbm(values):
    return pltpu.with_memory_space_constraint(values, pltpu.HBM)


def compiler_params(megabytes=32):
    return pltpu.CompilerParams(vmem_limit_bytes=megabytes * 2**20)


def whole(memory_space=pltpu.VMEM):
    return pl.BlockSpec(memory_space=memory_space)


def layer_block(layer_index, shape):
    return pl.BlockSpec((1,) + shape, lambda step: (layer_index,) + (0,) * len(shape))


def same_block(shape):
    return pl.BlockSpec(shape, lambda step: (0,) * len(shape))


def order_kernel(new_tokens, group_ref, prefix_ref, tail_ref, map_ref, rank_ref, position_ref, visit_ref, count_ref):
    requests = group_ref.shape[0]
    groups = prefix_ref.shape[0]
    per_group = requests // groups
    blocks = map_ref.shape[1]
    for group in range(groups):
        count_ref[group] = 0

    def place(request, unused):
        group = group_ref[request]
        seat = count_ref[group]
        count_ref[group] = seat + 1
        rank = group * per_group + seat
        rank_ref[request] = rank
        start = prefix_ref[group] + tail_ref[request]
        for token in range(new_tokens):
            position_ref[rank * new_tokens + token] = start + token
        return unused

    lax.fori_loop(0, requests, place, 0)

    def look(block, unused):
        segment, depth = map_ref[0, block], map_ref[1, block]
        is_tail = segment >= groups
        request = jnp.clip(segment - groups, 0, requests - 1)
        prompt = jnp.clip(segment, 0, groups - 1)
        seat = rank_ref[request]
        first = jnp.where(is_tail, (seat % per_group) * new_tokens, 0)
        length = jnp.where(is_tail, tail_ref[request], prefix_ref[prompt])
        visit_ref[block] = jnp.where(is_tail, seat // per_group, prompt)
        visit_ref[blocks + block] = jnp.where(segment < 0, 0, length - depth * BLOCK)
        visit_ref[2 * blocks + block] = first
        visit_ref[3 * blocks + block] = jnp.where(is_tail, first + new_tokens, per_group * new_tokens)
        return unused

    lax.fori_loop(0, blocks, look, 0)


def order_requests(group_of, prefix_len, tail_len, block_map, new_tokens):
    requests = group_of.shape[0]
    smem = whole(pltpu.SMEM)
    return pl.pallas_call(
        functools.partial(order_kernel, new_tokens),
        out_shape=(
            jax.ShapeDtypeStruct((requests,), jnp.int32),
            jax.ShapeDtypeStruct((requests * new_tokens,), jnp.int32),
            jax.ShapeDtypeStruct((4 * block_map.shape[0],), jnp.int32),
        ),
        in_specs=[smem] * 4,
        out_specs=(smem, smem, smem),
        scratch_shapes=[pltpu.SMEM((prefix_len.shape[0],), jnp.int32)],
        name="order_requests",
    )(group_of, prefix_len, tail_len, block_map.T)


def thirds(values):
    high = values.astype(jnp.bfloat16).astype(jnp.float32)
    middle = (values - high).astype(jnp.bfloat16).astype(jnp.float32)
    return high, middle, values - high - middle


def row_block(rows):
    width = rows[0].shape[1]
    line = lax.broadcasted_iota(jnp.int32, (8, width), 0)
    block = jnp.zeros((8, width), jnp.float32)
    for index, row in enumerate(rows):
        block = jnp.where(line == index, row, block)
    return block


def column_to_row(column):
    return jnp.broadcast_to(column, (column.shape[0], LANES)).T[0:1]


def row_to_column(row):
    return jnp.broadcast_to(row, (LANES, row.shape[1])).T


def ranks(group_ref):
    requests = group_ref.shape[1]
    across = lax.broadcasted_iota(jnp.int32, (requests, requests), 1)
    down = lax.broadcasted_iota(jnp.int32, (requests, requests), 0)
    group_row = group_ref[0:1, :]
    group_column = jnp.sum(jnp.where(across == down, group_row, 0), axis=1, keepdims=True)
    ahead = (group_column < group_row) | ((group_column == group_row) & (down < across))
    return jnp.sum(jnp.where(ahead, 1, 0), axis=0, keepdims=True)


def row_sums(lines):
    block = row_block([part for line in lines for part in thirds(line)])
    return jnp.concatenate([block, jnp.zeros_like(block)], axis=0).astype(jnp.bfloat16)


def from_row_sums(block):
    block = block.astype(jnp.float32)
    line = lax.broadcasted_iota(jnp.int32, block.shape, 0)
    return [
        jnp.sum(jnp.where((line >= start) & (line < start + 3), block, 0.0), axis=0, keepdims=True)
        for start in (0, 3)
    ]


def embed_kernel(
    token_ref, group_ref, table_hbm, near_ref, far_ref, own_ref,
    table_ref, hot_ref, row_ref, semaphores,
):
    core = lax.axis_index("seq") % 2
    first = (lax.axis_index("seq") * lax.axis_size("tp") + lax.axis_index("tp")) * table_ref.shape[1]
    new_tokens, requests = token_ref.shape
    rows, unit = near_ref.shape[1:]
    copies = []
    for chip in range(CHIPS):
        copies.append(
            pltpu.make_async_copy(
                table_hbm.at[:, pl.ds(chip * 2 * unit, 2 * unit)], table_ref.at[chip], semaphores.at[chip]
            )
        )
        copies[-1].start()
    rank_row = ranks(group_ref)
    line = lax.broadcasted_iota(jnp.int32, (rows, requests), 0)
    ids = jnp.zeros((rows, requests), jnp.int32)
    for token in range(new_tokens):
        match = (rank_row == line // new_tokens) & (line % new_tokens == token)
        ids = jnp.where(match, token_ref[token : token + 1, :], ids)
    ids = jnp.sum(ids, axis=1, keepdims=True) - first
    entry = lax.broadcasted_iota(jnp.int32, hot_ref.shape, 1)
    hot_ref[...] = jnp.where(entry == ids, 1.0, 0.0).astype(jnp.bfloat16)
    total = jnp.zeros((rows, LANES), jnp.float32)
    for chip, copy in enumerate(copies):
        copy.wait()
        chosen = jnp.dot(hot_ref[...], table_ref[chip], preferred_element_type=jnp.float32)
        for start in range(0, 2 * unit, LANES):
            total = total + chosen[:, start : start + LANES]
        chosen = chosen.astype(jnp.bfloat16)
        row_ref[:, chip * 2 * unit : (chip + 1) * 2 * unit] = chosen
        left, right = chosen[:, :unit], chosen[:, unit:]
        near_ref[chip] = jnp.where(core == 0, left, right)
        far_ref[chip * rows : (chip + 1) * rows] = jnp.where(core == 0, right, left)
    features = row_ref.shape[1]
    mean = jnp.sum(total, axis=1, keepdims=True) * (1.0 / features)
    squares = jnp.zeros((rows, LANES), jnp.float32)
    for start in range(0, features, LANES):
        centred = row_ref[:, start : start + LANES].astype(jnp.float32) - mean
        squares = squares + centred * centred
    variance = jnp.sum(squares, axis=1, keepdims=True) * (1.0 / features)
    held = (ids >= 0) & (ids < hot_ref.shape[1])
    scale = jnp.where(held, lax.rsqrt(variance + 1e-05), 0.0)
    mean, scale = column_to_row(mean), column_to_row(scale)
    own_ref[...] = row_block([mean, scale])
    far_ref[CHIPS * rows :] = row_sums([mean, scale])


def embed(token_ids, group_of, embedding, unit):
    rows = token_ids.shape[0] * token_ids.shape[1]
    return pl.pallas_call(
        embed_kernel,
        out_shape=(
            jax.ShapeDtypeStruct((CHIPS, rows, unit), jnp.bfloat16),
            pltpu.HBM((CHIPS * rows + 16, unit), jnp.bfloat16),
            jax.ShapeDtypeStruct((8, rows), jnp.float32),
        ),
        in_specs=[whole(), whole(), whole(pltpu.HBM)],
        out_specs=(whole(),) * 3,
        scratch_shapes=[
            pltpu.VMEM((CHIPS, embedding.shape[0], 2 * unit), jnp.bfloat16),
            pltpu.VMEM((rows, embedding.shape[0]), jnp.bfloat16),
            pltpu.VMEM((rows, embedding.shape[1]), jnp.bfloat16),
            pltpu.SemaphoreType.DMA((CHIPS,)),
        ],
        compiler_params=compiler_params(24),
        name="embed",
    )(in_hbm(token_ids.T), in_hbm(group_of[None, :]), in_hbm(embedding))


def join_kernel(near_ref, far_ref, own_ref, out_ref, *refs):
    *out_hbms, leave_ref, semaphores = refs
    here = lax.axis_index("seq") // 2
    rows = near_ref.shape[1]
    mean, scale = from_row_sums(far_ref[CHIPS * rows :])
    lines = row_sums([mean + own_ref[0:1, :], scale + own_ref[1:2, :]])
    leaving = []
    for distance in reversed(range(CHIPS)):
        chip = here ^ distance
        far = far_ref[pl.ds(pl.multiple_of(chip * rows, rows), rows), :].astype(jnp.float32)
        joined = (near_ref[chip].astype(jnp.float32) + far).astype(jnp.bfloat16)
        if distance:
            leave_ref[distance - 1, :rows] = joined
            leave_ref[distance - 1, rows:] = lines
            leaving.append(
                pltpu.make_async_copy(
                    leave_ref.at[distance - 1], out_hbms[distance - 1], semaphores.at[distance - 1]
                )
            )
            leaving[-1].start()
        else:
            out_ref[:rows] = joined
            out_ref[rows:] = lines
    for copy in leaving:
        copy.wait()


def join(near, far, own):
    chips, rows, unit = near.shape
    one = (rows + 16, unit)
    return pl.pallas_call(
        join_kernel,
        out_shape=(jax.ShapeDtypeStruct(one, jnp.bfloat16),) + (pltpu.HBM(one, jnp.bfloat16),) * (chips - 1),
        in_specs=[whole()] * 3,
        out_specs=(whole(),) + (whole(pltpu.HBM),) * (chips - 1),
        scratch_shapes=[pltpu.VMEM((chips - 1,) + one, jnp.bfloat16), pltpu.SemaphoreType.DMA((chips - 1,))],
        compiler_params=compiler_params(16),
        name="join",
    )(near, far, own)


def gather_kernel(a_ref, b_ref, c_ref, d_ref, out_hbm, out_ref, semaphore):
    rows = out_ref.shape[0] - 16
    near = a_ref[...].astype(jnp.float32) + b_ref[...].astype(jnp.float32)
    far = c_ref[...].astype(jnp.float32) + d_ref[...].astype(jnp.float32)
    total = near + far
    out_ref[:rows] = total[:rows].astype(jnp.bfloat16)
    out_ref[rows:] = row_sums(from_row_sums(total[rows:]))
    copy = pltpu.make_async_copy(out_ref, out_hbm, semaphore)
    copy.start()
    copy.wait()


def gather(parts):
    return pl.pallas_call(
        gather_kernel,
        out_shape=pltpu.HBM(parts[0].shape, jnp.bfloat16),
        in_specs=[whole()] * 4,
        out_specs=whole(pltpu.HBM),
        scratch_shapes=[pltpu.VMEM(parts[0].shape, jnp.bfloat16), pltpu.SemaphoreType.DMA],
        compiler_params=compiler_params(16),
        name="gather",
    )(*parts)


def first_kernel(a_hbm, b_ref, c_ref, d_ref, gain_ref, bias_ref, start_ref, hidden_ref, a_ref, semaphore):
    rows, unit = hidden_ref.shape
    copy = pltpu.make_async_copy(a_hbm, a_ref, semaphore)
    copy.start()
    far = c_ref[...].astype(jnp.float32) + d_ref[...].astype(jnp.float32)
    copy.wait()
    total = (a_ref[...].astype(jnp.float32) + b_ref[...].astype(jnp.float32)) + far
    mean, scale = (row_to_column(line) for line in from_row_sums(total[rows:]))
    columns = pl.ds(pl.multiple_of(lax.axis_index("seq") * unit, unit), unit)
    gain, bias = gain_ref[0:1, columns], bias_ref[0:1, columns]
    for start in range(0, unit, LANES):
        span = slice(start, start + LANES)
        state = total[:rows, span]
        start_ref[:, span] = state.astype(jnp.bfloat16)
        hidden_ref[:, span] = ((state - mean) * scale * gain[:, span] + bias[:, span]).astype(jnp.bfloat16)


def first_hidden(parts, ln_gain, ln_bias):
    one = jax.ShapeDtypeStruct((parts[0].shape[0] - 16, parts[0].shape[1]), jnp.bfloat16)
    return pl.pallas_call(
        first_kernel,
        out_shape=(one, one),
        in_specs=[whole(pltpu.HBM)] + [whole()] * 5,
        out_specs=(whole(), whole()),
        scratch_shapes=[pltpu.VMEM(parts[0].shape, jnp.bfloat16), pltpu.SemaphoreType.DMA],
        compiler_params=compiler_params(16),
        name="first_hidden",
    )(in_hbm(parts[0]), *parts[1:], ln_gain, ln_bias)


def norm_kernel(layer_index, tp_count, *refs):
    *part_refs, gain_ref, bias_ref, next_ref, cut_ref = refs
    state = functools.reduce(jnp.add, [ref[...].astype(jnp.float32) for ref in part_refs])
    next_ref[...] = state
    average = jnp.mean(state, axis=-1, keepdims=True)
    centred = state - average
    variance = jnp.mean(centred * centred, axis=-1, keepdims=True)
    gain = gain_ref[layer_index : layer_index + 1, :]
    bias = bias_ref[layer_index : layer_index + 1, :]
    normed = (centred * lax.rsqrt(variance + 1e-05) * gain + bias).astype(jnp.bfloat16)
    width = cut_ref.shape[2]
    for place in range(cut_ref.shape[0]):
        start = (place // tp_count) * width
        cut_ref[place] = normed[:, start : start + width]


def norm_rows(parts, state, ln_gain, ln_bias, layer_index, devices, tp_count):
    rows, width = parts[0].shape
    cut = width // (devices // tp_count)
    operands = list(parts) + ([] if state is None else [state]) + [ln_gain, ln_bias]
    return pl.pallas_call(
        functools.partial(norm_kernel, layer_index, tp_count),
        out_shape=(
            jax.ShapeDtypeStruct((rows, width), jnp.float32),
            jax.ShapeDtypeStruct((devices, rows, cut), jnp.bfloat16),
        ),
        in_specs=[whole()] * len(operands),
        out_specs=(whole(), whole()),
        compiler_params=compiler_params(16),
        name="norm_rows",
    )(*operands)


def share_kernel(a_ref, b_ref, c_ref, d_ref, *out_refs):
    total = functools.reduce(jnp.add, [ref[...].astype(jnp.float32) for ref in (a_ref, b_ref, c_ref, d_ref)])
    mine = out_refs[0].shape[0]
    for owner in range(len(out_refs)):
        for distance, ref in enumerate(out_refs):
            @pl.when(lax.axis_index("tp") == owner ^ distance)
            def put(ref=ref, owner=owner):
                ref[...] = total[owner * mine : (owner + 1) * mine].astype(ref.dtype)


def share_rows(parts, tp_count):
    rows, width = parts[0].shape
    one = (rows // tp_count, width)
    return pl.pallas_call(
        share_kernel,
        out_shape=(jax.ShapeDtypeStruct(one, jnp.float32),)
        + (jax.ShapeDtypeStruct(one, jnp.bfloat16),) * (tp_count - 1),
        in_specs=[whole()] * 4,
        out_specs=(whole(),) * tp_count,
        compiler_params=compiler_params(16),
        name="share_rows",
    )(*parts)


def last_parts_kernel(tp_count, a_ref, b_ref, c_ref, d_ref, state_ref, out_ref):
    near = a_ref[...].astype(jnp.float32) + b_ref[...].astype(jnp.float32)
    far = c_ref[...].astype(jnp.float32) + d_ref[...].astype(jnp.float32)
    total = near + far
    mine = state_ref.shape[0]
    owner = lax.axis_index("tp")
    for place in range(tp_count):
        rows = slice(place * mine, (place + 1) * mine)
        total_rows = total[rows] + jnp.where(owner == place, 1.0, 0.0) * state_ref[...]
        out_ref[rows] = total_rows


def last_parts(parts, state, tp_count):
    return pl.pallas_call(
        functools.partial(last_parts_kernel, tp_count),
        out_shape=jax.ShapeDtypeStruct(parts[0].shape, jnp.float32),
        in_specs=[whole()] * 5,
        out_specs=whole(),
        compiler_params=compiler_params(16),
        name="last_parts",
    )(*parts, state)


def split_kernel(half_ref, arrived_ref, out_ref, *refs):
    *out_hbms, leave_ref, semaphores = refs
    share = out_ref.shape[0]
    leaving = []
    for distance in reversed(range(CHIPS)):
        rows = slice(distance * share, (distance + 1) * share)
        joined = half_ref[rows] + arrived_ref[rows].astype(jnp.float32)
        if distance:
            leave_ref[distance - 1] = joined.astype(jnp.bfloat16)
            leaving.append(
                pltpu.make_async_copy(
                    leave_ref.at[distance - 1], out_hbms[distance - 1], semaphores.at[distance - 1]
                )
            )
            leaving[-1].start()
        else:
            out_ref[...] = joined
    for copy in leaving:
        copy.wait()


def split(half, arrived):
    one = (half.shape[0] // CHIPS, half.shape[1])
    return pl.pallas_call(
        split_kernel,
        out_shape=(jax.ShapeDtypeStruct(one, jnp.float32),) + (pltpu.HBM(one, jnp.bfloat16),) * (CHIPS - 1),
        in_specs=[whole()] * 2,
        out_specs=(whole(),) + (whole(pltpu.HBM),) * (CHIPS - 1),
        scratch_shapes=[pltpu.VMEM((CHIPS - 1,) + one, jnp.bfloat16), pltpu.SemaphoreType.DMA((CHIPS - 1,))],
        compiler_params=compiler_params(16),
        name="split",
    )(half, arrived)


def last_kernel(a_ref, b_ref, c_ref, d_ref, out_ref):
    near = a_ref[...].astype(jnp.float32) + b_ref[...].astype(jnp.float32)
    far = c_ref[...].astype(jnp.float32) + d_ref[...].astype(jnp.float32)
    out_ref[...] = (near + far).astype(jnp.bfloat16)


def last_rows(parts):
    return pl.pallas_call(
        last_kernel,
        out_shape=jax.ShapeDtypeStruct(parts[0].shape, jnp.bfloat16),
        in_specs=[whole()] * 4,
        out_specs=whole(),
        compiler_params=compiler_params(16),
        name="last_rows",
    )(*parts)


def back_kernel(new_tokens, group_ref, near_ref, far_ref):
    rows, half = near_ref.shape
    requests = group_ref.shape[1]
    rank_row = ranks(group_ref)
    line = lax.broadcasted_iota(jnp.int32, (rows, requests), 0)
    column = lax.broadcasted_iota(jnp.int32, (rows, requests), 1)
    wanted = jnp.sum(jnp.where(column == line // new_tokens, rank_row, 0), axis=1, keepdims=True)
    line = lax.broadcasted_iota(jnp.int32, near_ref.shape, 0)
    entry = lax.broadcasted_iota(jnp.int32, near_ref.shape, 1)
    share = half // CHIPS
    here = lax.axis_index("seq") // 2
    for ref, other in ((near_ref, False), (far_ref, True)):
        held = (((entry // share) ^ here) * 2 + core_parity(other)) * share + entry % share
        back = held == wanted * new_tokens + line % new_tokens
        ref[...] = jnp.where(back, 1.0, 0.0).astype(jnp.bfloat16)


def back_rows(group_of, new_tokens):
    rows = group_of.shape[0] * new_tokens
    one = jax.ShapeDtypeStruct((rows, rows // 2), jnp.bfloat16)
    return pl.pallas_call(
        functools.partial(back_kernel, new_tokens),
        out_shape=(one, one),
        in_specs=[whole()],
        out_specs=(whole(), whole()),
        compiler_params=compiler_params(16),
        name="back_rows",
    )(group_of[None, :])


def restore_kernel(near_back_ref, far_back_ref, *refs):
    *row_refs, out_hbm, out_ref, semaphores = refs
    requests, new_tokens, width = out_ref.shape
    step = width // semaphores.shape[0]
    leaving = []
    for index, start in enumerate(range(0, width, step)):
        span = slice(start, start + step)
        near, far = (
            jnp.concatenate([ref[:, span] for ref in half], axis=0)
            for half in (row_refs[:CHIPS], row_refs[CHIPS:])
        )
        rows = jnp.dot(near_back_ref[...], near, preferred_element_type=jnp.float32) + jnp.dot(
            far_back_ref[...], far, preferred_element_type=jnp.float32
        )
        out_ref[:, :, span] = rows.reshape(requests, new_tokens, step)
        span = pl.ds(start, step)
        leaving.append(
            pltpu.make_async_copy(out_ref.at[:, :, span], out_hbm.at[:, :, span], semaphores.at[index])
        )
        leaving[-1].start()
    for copy in leaving:
        copy.wait()


def restore(backs, near, far, new_tokens):
    rows = backs[0].shape[0]
    shape = (rows // new_tokens, new_tokens, near[0].shape[1])
    return pl.pallas_call(
        restore_kernel,
        out_shape=pltpu.HBM(shape, jnp.float32),
        in_specs=[whole()] * (2 + 2 * CHIPS),
        out_specs=whole(pltpu.HBM),
        scratch_shapes=[pltpu.VMEM(shape, jnp.float32), pltpu.SemaphoreType.DMA((4,))],
        compiler_params=compiler_params(24),
        name="restore",
    )(*backs, *near, *far)


def core_parity(other):
    return 1 - lax.axis_index("seq") % 2 if other else lax.axis_index("seq") % 2


def heads_kernel(joins, hidden_ref, qkv_ref, *refs):
    if joins:
        arrived_ref, near_ref, *out_hbms, out_ref, semaphores = refs
    else:
        out_ref = refs[0]
    parity = core_parity(not joins)
    here = lax.axis_index("seq") // 2
    rows, unit = hidden_ref.shape
    width = qkv_ref.shape[1] // 3
    share = rows // CHIPS // 2
    half = rows // 2
    pieces = width // unit
    tall = 2 * pieces * share

    def joined(values, start):
        if joins:
            values = values + arrived_ref[start : start + values.shape[0]].astype(jnp.float32)
        return values.astype(jnp.bfloat16)

    def picked(chips):
        return jnp.concatenate(
            [
                hidden_ref[pl.ds(pl.multiple_of((2 * chip + parity) * share, share), share), :]
                for chip in chips
            ],
            axis=0,
        )

    queries = jnp.dot(picked(range(CHIPS)), qkv_ref[:, :width], preferred_element_type=jnp.float32)
    for piece in range(pieces):
        start = piece * half
        query = joined(queries[:, piece * unit : (piece + 1) * unit], start)
        if joins:
            for distance in range(CHIPS):
                out_ref[distance, tall + start : tall + start + half] = query
        else:
            out_ref[start : start + half] = query
    others = jnp.dot(
        picked([here ^ distance for distance in range(CHIPS)]), qkv_ref[:, width:], preferred_element_type=jnp.float32
    )
    base = pieces * half
    leaving = []
    for distance in reversed(range(CHIPS)):
        for piece in range(2 * pieces):
            start = base + (distance * 2 * pieces + piece) * share
            value = joined(
                others[distance * share : (distance + 1) * share, piece * unit : (piece + 1) * unit], start
            )
            if joins:
                out_ref[distance, piece * share : (piece + 1) * share] = value
            else:
                out_ref[start : start + share] = value
        if joins and distance:
            copy = pltpu.make_async_copy(
                out_ref.at[distance], out_hbms[distance - 1], semaphores.at[distance - 1]
            )
            copy.start()
            leaving.append(copy)
    if joins:
        near_ref[...] = out_ref[0]
    for copy in leaving:
        copy.wait()


def project_heads(hidden, weights_qkv, unit, arrived=None):
    rows = hidden.shape[0]
    pieces = weights_qkv.shape[1] // 3 // unit
    tall = 2 * pieces * (rows // CHIPS // 2)
    common = pieces * (rows // 2)
    extra = [] if arrived is None else [arrived]
    out_shape = jax.ShapeDtypeStruct((common + CHIPS * tall, unit), jnp.bfloat16)
    out_specs = whole()
    scratch = []
    if arrived is not None:
        one = (tall + common, unit)
        out_shape = (jax.ShapeDtypeStruct(one, jnp.bfloat16),) + (pltpu.HBM(one, jnp.bfloat16),) * (CHIPS - 1)
        out_specs = (whole(),) + (whole(pltpu.HBM),) * (CHIPS - 1)
        scratch = [pltpu.VMEM((CHIPS,) + one, jnp.bfloat16), pltpu.SemaphoreType.DMA((CHIPS - 1,))]
    return pl.pallas_call(
        functools.partial(heads_kernel, arrived is not None),
        out_shape=out_shape,
        in_specs=[whole()] * (2 + len(extra)),
        out_specs=out_specs,
        scratch_shapes=scratch,
        compiler_params=compiler_params(24),
        name="project_heads",
    )(hidden, weights_qkv, *extra)


def units_kernel(joins, hidden_ref, fc1_ref, *refs):
    arrived_ref, out_refs = (refs[0], refs[1:]) if joins else (None, refs)
    parity = core_parity(not joins)
    here = lax.axis_index("seq") // 2
    unit = fc1_ref.shape[2] // CHIPS // 2
    hidden = hidden_ref[...]
    for distance in range(CHIPS):
        target = 2 * (here ^ distance) + parity
        columns = pl.ds(pl.multiple_of(target * unit, unit), unit)
        pre = jnp.dot(hidden, fc1_ref[0, :, columns], preferred_element_type=jnp.float32)
        if joins:
            pre = pre + arrived_ref[distance].astype(jnp.float32)
            out_refs[distance][...] = pre.astype(jnp.bfloat16)
        else:
            out_refs[0][distance] = pre.astype(jnp.bfloat16)


def project_units(hidden, w_fc1, layer_index, arrived=None):
    rows = hidden.shape[0]
    unit = w_fc1.shape[2] // CHIPS // 2
    extra = [] if arrived is None else [arrived]
    if arrived is None:
        out_shape = jax.ShapeDtypeStruct((CHIPS, rows, unit), jnp.bfloat16)
    else:
        out_shape = (jax.ShapeDtypeStruct((rows, unit), jnp.bfloat16),) * CHIPS
    return pl.pallas_call(
        functools.partial(units_kernel, arrived is not None),
        grid=(1,),
        out_shape=out_shape,
        in_specs=[same_block(hidden.shape), layer_block(layer_index, w_fc1.shape[1:])]
        + [same_block(values.shape) for values in extra],
        out_specs=jax.tree.map(lambda leaf: same_block(leaf.shape), out_shape),
        compiler_params=compiler_params(24),
        name="project_units",
    )(hidden, w_fc1, *extra)


def activate_kernel(a_ref, b_ref, c_ref, d_ref, table_ref, query_ref, key_ref, value_ref):
    near = a_ref[...].astype(jnp.float32) + b_ref[...].astype(jnp.float32)
    far = c_ref[...].astype(jnp.float32) + d_ref[...].astype(jnp.float32)
    total = near + far
    share, width = key_ref.shape
    half = query_ref.shape[0]
    unit = a_ref.shape[1]
    lanes = table_ref.shape[2]
    pieces = width // unit
    own = pl.ds(pl.multiple_of((lax.axis_index("seq") // 2) * share, share), share)

    def put(target_ref, start, height, span, scale):
        for piece in range(pieces):
            for column in range(0, unit, lanes):
                first = start + piece * height
                values = total[first : first + height, column : column + lanes]
                if span is not None:
                    values = (
                        values * table_ref[0, span]
                        + pltpu.roll(values, lanes - ROT // 2, 1) * table_ref[1, span]
                        + pltpu.roll(values, ROT // 2, 1) * table_ref[2, span]
                    )
                values = values.astype(jnp.bfloat16)
                if scale is not None:
                    values = (values.astype(jnp.float32) * scale).astype(jnp.bfloat16)
                column_out = piece * unit + column
                target_ref[:, column_out : column_out + lanes] = values

    put(key_ref, 0, share, own, None)
    put(value_ref, pieces * share, share, None, None)
    put(query_ref, 2 * pieces * share, half, slice(None), 1.0 / math.sqrt(HEAD_DIM))


def activate(parts, tables, width):
    half = tables.shape[1]
    small = jax.ShapeDtypeStruct((half // CHIPS, width), jnp.bfloat16)
    return pl.pallas_call(
        activate_kernel,
        out_shape=(jax.ShapeDtypeStruct((half, width), jnp.bfloat16), small, small),
        in_specs=[whole()] * 5,
        out_specs=(whole(),) * 3,
        compiler_params=compiler_params(16),
        name="activate",
    )(*parts, tables)


def rotary_tables(positions, width):
    half = ROT // 2
    feature = lax.broadcasted_iota(jnp.int32, (1, width), 1) % HEAD_DIM
    frequency = jnp.exp((feature % half).astype(jnp.float32) * (-2.0 * math.log(10000.0) / ROT))
    angles = positions.astype(jnp.float32)[:, None] * frequency
    cosine, sine = jnp.cos(angles), jnp.sin(angles)
    return jnp.stack(
        [
            jnp.where(feature < ROT, cosine, 1.0),
            jnp.where(feature < half, -sine, 0.0),
            jnp.where((feature >= half) & (feature < ROT), sine, 0.0),
        ]
    )


def attend_kernel(
    layer_index, new_tokens,
    visit_hbm, query_ref, far_query_ref, new_key_ref, new_value_ref,
    key_hbm, value_hbm, out_ref,
    key_ref, value_ref, visit_ref, both_ref, score_ref, top_ref, sum_ref, mix_ref, semaphores, visit_semaphore,
):
    blocks = visit_ref.shape[0] // 4
    groups, tall, lanes = mix_ref.shape
    share = new_key_ref.shape[0]
    heads = tall // share
    chunks = semaphores.shape[1]
    chunk = key_ref.shape[0] // chunks

    def copy(kind, index):
        span = pl.ds(index * chunk, chunk)
        source, target = ((key_hbm, key_ref), (value_hbm, value_ref))[kind]
        return pltpu.make_async_copy(
            source.at[layer_index, span], target.at[span], semaphores.at[kind, index]
        )

    looking = pltpu.make_async_copy(visit_hbm, visit_ref, visit_semaphore)
    looking.start()
    for kind in range(2):
        for index in range(chunks):
            copy(kind, index).start()
    core = lax.axis_index("seq") % 2
    for chip in range(groups // 2):
        span = slice(chip * share, (chip + 1) * share)
        both_ref[2 * chip + core] = query_ref[span]
        both_ref[2 * chip + 1 - core] = far_query_ref[span]
    lane = lax.broadcasted_iota(jnp.int32, (share, lanes), 1)
    row = lax.broadcasted_iota(jnp.int32, (share, lanes), 0)
    top_ref[...] = jnp.full(top_ref.shape, very_negative, jnp.float32)
    sum_ref[...] = jnp.zeros(sum_ref.shape, jnp.float32)
    mix_ref[...] = jnp.zeros(mix_ref.shape, jnp.float32)

    def score(index, group, keys, mask):
        scores = []
        for pair in range(heads // 2):
            both = both_ref[group, :, pair * lanes : (pair + 1) * lanes]
            none = jnp.zeros_like(both)
            split = jnp.concatenate(
                [jnp.where(lane < HEAD_DIM, both, none), jnp.where(lane < HEAD_DIM, none, both)], axis=0
            )
            scores.append(
                lax.dot_general(
                    split, keys[:, pair * lanes : (pair + 1) * lanes], (((1,), (1,)), ((), ())),
                    preferred_element_type=jnp.float32,
                )
            )
        scores = jnp.concatenate(scores, axis=0).reshape(heads, share, BLOCK)
        scores = jnp.where(mask[None], scores, very_negative).reshape(tall, BLOCK)
        score_ref[index] = scores
        top_ref[group] = jnp.maximum(top_ref[group], scores)

    def mix(index, group, values):
        weight = jnp.exp(score_ref[index] - top_ref[group])
        sum_ref[group] += weight
        rounded = weight.astype(jnp.bfloat16)
        mix_ref[group] += jnp.concatenate(
            [
                jnp.dot(
                    rounded[pair * 2 * share : (pair + 1) * 2 * share],
                    values[:, pair * lanes : (pair + 1) * lanes],
                    preferred_element_type=jnp.float32,
                )
                for pair in range(heads // 2)
            ],
            axis=0,
        )

    own = lax.axis_index("seq")
    fill = jnp.zeros((BLOCK - share, new_key_ref.shape[1]), jnp.bfloat16)
    score(
        blocks, own, jnp.concatenate([new_key_ref[...], fill], axis=0),
        (lane // new_tokens == row // new_tokens) & (lane <= row),
    )
    looking.wait()
    owners = []
    for block in range(blocks):
        if (block * BLOCK) % chunk == 0:
            copy(0, block * BLOCK // chunk).wait()
        group, live, first, end = (visit_ref[field * blocks + block] for field in range(4))
        owners.append(group)
        score(
            block, group, key_ref[block * BLOCK : (block + 1) * BLOCK, :],
            (lane < live) & (row >= first) & (row < end),
        )
    for group in range(groups):
        top = jnp.max(top_ref[group], axis=1, keepdims=True)
        top_ref[group] = jnp.broadcast_to(top, (tall, lanes))
    mix(blocks, own, jnp.concatenate([new_value_ref[...], fill], axis=0))
    for block in range(blocks):
        if (block * BLOCK) % chunk == 0:
            copy(1, block * BLOCK // chunk).wait()
        mix(block, owners[block], value_ref[block * BLOCK : (block + 1) * BLOCK, :])

    level = jnp.zeros((tall, lanes), jnp.float32)
    column = lax.broadcasted_iota(jnp.int32, (tall, lanes), 1)

    def mean(group):
        total = jnp.sum(sum_ref[group], axis=1, keepdims=True)
        total = jnp.where(total <= 0.0, 1.0, total)
        own_level = jnp.where(column == group, top_ref[group] + jnp.log(total), 0.0)
        return mix_ref[group] / total, own_level

    for group in range(groups // 2):
        left, left_level = mean(group)
        right, right_level = mean(group + groups // 2)
        level = level + left_level + right_level
        for head in range(heads):
            rows = slice(head * share, (head + 1) * share)
            first, second = left[rows], right[rows]
            if head % 2:
                first = pltpu.roll(first, HEAD_DIM, 1)
            else:
                second = pltpu.roll(second, HEAD_DIM, 1)
            packed = jnp.where(lane < HEAD_DIM, first, second)
            out_ref[head, group * share : (group + 1) * share] = packed.astype(jnp.bfloat16)
    level = level.T[:groups]
    high = level.astype(jnp.bfloat16).astype(jnp.float32)
    middle = (level - high).astype(jnp.bfloat16).astype(jnp.float32)
    low = level - high - middle
    rest = jnp.concatenate([high, middle, low, jnp.zeros_like(low)], axis=0).astype(jnp.bfloat16)
    start = (groups // 2) * share
    for head in range(heads):
        column = head * share // lanes * lanes
        out_ref[head, start:] = rest[:, column : column + lanes]


def attend(visits, query, far_query, new_key, new_value, k_cache, v_cache, layer_index, new_tokens, groups):
    width = query.shape[1]
    rows = 2 * query.shape[0]
    slots = k_cache.shape[1]
    heads = width // HEAD_DIM
    share = rows // groups
    tall = heads * share
    lanes = 2 * HEAD_DIM
    chunks = 2
    state = pltpu.VMEM((groups, tall, lanes), jnp.float32)
    return pl.pallas_call(
        functools.partial(attend_kernel, layer_index, new_tokens),
        out_shape=jax.ShapeDtypeStruct((heads, rows // 2 + 4 * groups, lanes), jnp.bfloat16),
        in_specs=[whole(pltpu.HBM)] + [whole()] * 4 + [whole(pltpu.HBM)] * 2,
        out_specs=whole(),
        scratch_shapes=[
            pltpu.VMEM((slots, width), jnp.bfloat16),
            pltpu.VMEM((slots, width), jnp.bfloat16),
            pltpu.SMEM(visits.shape, jnp.int32),
            pltpu.VMEM((groups, share, width), jnp.bfloat16),
            pltpu.VMEM((visits.shape[0] // 4 + 1, tall, BLOCK), jnp.float32),
            state,
            state,
            state,
            pltpu.SemaphoreType.DMA((2, chunks)),
            pltpu.SemaphoreType.DMA,
        ],
        compiler_params=compiler_params(24),
        name="attend",
    )(in_hbm(visits), query, far_query, new_key, new_value, in_hbm(k_cache), in_hbm(v_cache))


def update_kernel(
    layer_index, other, tp_count, has_start, part_ref, bias_ref, out_weight_ref, fc2_ref, *refs
):
    *unit_refs, out_ref, scale_ref = refs
    if has_start:
        *unit_refs, start_ref = unit_refs
    seq_index = lax.axis_index("seq")
    parity = 1 - seq_index % 2 if other else seq_index % 2
    sources, tall, lanes = part_ref.shape
    unit = unit_refs[0].shape[1]
    share = unit_refs[0].shape[0] // sources
    groups = (tall - (sources // 2) * share) // 4
    levels = []
    for source in range(sources):
        parts = part_ref[source, (sources // 2) * share :, :].astype(jnp.float32)
        levels.append(parts[:groups] + parts[groups : 2 * groups] + parts[2 * groups : 3 * groups])
    top = functools.reduce(jnp.maximum, levels)
    scales = [jnp.exp(level - top) for level in levels]
    total = functools.reduce(jnp.add, scales)
    scales = [scale / total for scale in scales]
    blank = jnp.zeros((lanes - groups * sources, lanes), jnp.float32)
    scale_ref[...] = jnp.concatenate(scales + [blank], axis=0).T
    place = seq_index % (lanes // share)
    scale = scale_ref[pl.ds(pl.multiple_of(place * share, share), share), :]
    scale = jnp.where(parity == 0, scale, pltpu.roll(scale, lanes - 1, 1))
    here = lax.axis_index("seq") // 2
    next_scale = pltpu.roll(scale, lanes - 2, 1)
    lane = lax.broadcasted_iota(jnp.int32, (share, lanes), 1)
    first, second = [], []
    for pair in range(CHIPS // 2):
        pack = (here % 2) ^ pair
        rows = pl.ds(pl.multiple_of((2 * pack + parity) * share, share), share)
        pair_scale = jnp.where(pack == 0, scale, next_scale)
        mixed = jnp.zeros((share, lanes), jnp.float32)
        for source in range(sources):
            column = source * groups
            left = pair_scale[:, column : column + 1]
            right = pair_scale[:, column + groups // 2 : column + groups // 2 + 1]
            mixed = mixed + part_ref[source, rows, :].astype(jnp.float32) * jnp.where(
                lane < HEAD_DIM, left, right
            )
        turned = pltpu.roll(mixed, HEAD_DIM, 1)
        first.append(jnp.where(here < 2, mixed, turned)[:, :HEAD_DIM])
        second.append(jnp.where(here < 2, turned, mixed)[:, :HEAD_DIM])
    attended = jnp.concatenate(first + second, axis=0).astype(jnp.bfloat16)
    bias = bias_ref[
        layer_index : layer_index + 1, pl.ds(pl.multiple_of(seq_index * unit, unit), unit)
    ]
    hidden, started = [], []
    for piece in range(CHIPS):
        rows = pl.ds(pl.multiple_of((2 * (piece ^ here) + parity) * share, share), share)
        pre = functools.reduce(jnp.add, [ref[rows, :].astype(jnp.float32) for ref in unit_refs])
        hidden.append(jax.nn.gelu(pre + bias, approximate=True).astype(jnp.bfloat16))
        if has_start:
            started.append(start_ref[rows, :].astype(jnp.float32))
    change = jnp.dot(attended, out_weight_ref[0], preferred_element_type=jnp.float32) + jnp.dot(
        jnp.concatenate(hidden, axis=0), fc2_ref[0], preferred_element_type=jnp.float32
    )
    if not has_start:
        out_ref[...] = change.astype(out_ref.dtype)
        return
    started = jnp.concatenate(started, axis=0)
    for column in range(0, change.shape[1], unit):
        here = (seq_index * unit == column) & (lax.axis_index("tp") == 0)
        out_ref[:, column : column + unit] = (
            change[:, column : column + unit] + jnp.where(here, started, 0.0)
        ).astype(out_ref.dtype)


def update(parts, units, start, b_fc1, w_out, w_fc2, layer_index, other, tp_count):
    rows = units[0].shape[0] // 2
    width = w_out.shape[2]
    lanes = parts.shape[2]
    extra = list(units) + ([] if start is None else [start])
    return pl.pallas_call(
        functools.partial(update_kernel, layer_index, other, tp_count, start is not None),
        grid=(1,),
        out_shape=jax.ShapeDtypeStruct((rows, width), jnp.bfloat16 if other else jnp.float32),
        in_specs=[
            same_block(parts.shape),
            same_block(b_fc1.shape),
            layer_block(layer_index, w_out.shape[1:]),
            layer_block(layer_index, w_fc2.shape[1:]),
        ]
        + [same_block(units[0].shape)] * len(extra),
        out_specs=same_block((rows, width)),
        scratch_shapes=[pltpu.VMEM((lanes, lanes), jnp.float32)],
        compiler_params=compiler_params(),
        name="update",
    )(parts, b_fc1, w_out, w_fc2, *extra)


def per_device(
    token_ids, embedding, group_of, prefix_len, tail_len, block_map, k_cache, v_cache,
    ln_gain, ln_bias, w_qkv, w_fc1, b_fc1, w_out, w_fc2,
):
    seq_count, tp_count = lax.axis_size("seq"), lax.axis_size("tp")
    seq_index, tp_index = lax.axis_index("seq"), lax.axis_index("tp")
    devices = seq_count * tp_count
    core = seq_index % 2
    requests, new_tokens = token_ids.shape
    rows = requests * new_tokens
    groups = prefix_len.shape[0]
    share = rows // seq_count
    features = embedding.shape[1]
    width_local = k_cache.shape[2]
    unit = w_fc2.shape[1]

    def to_distances(parts):
        return [parts[0]] + [
            lax.ppermute(parts[k], "seq", [(i, i ^ (2 * k)) for i in range(seq_count)])
            for k in range(1, CHIPS)
        ]

    def over_tp(part, distance):
        return lax.ppermute(part, "tp", [(i, i ^ distance) for i in range(tp_count)])

    def from_tp(part):
        return [part] + [over_tp(part, k) for k in range(1, tp_count)]

    near, far, own = embed(token_ids, group_of, embedding, unit)
    parts = join(near, swap_cores(far, seq_count), own)
    gathered = gather(to_distances(parts))
    gathered, group_of = lax.optimization_barrier((gathered, group_of))
    rank, positions, visits = order_requests(group_of, prefix_len, tail_len, block_map, new_tokens)
    own_positions = lax.dynamic_index_in_dim(positions.reshape(CHIPS, 2, share), core, 1, keepdims=False)
    backs = back_rows(group_of, new_tokens)
    tables = rotary_tables(own_positions.reshape(-1), 2 * HEAD_DIM)
    weights_qkv = w_qkv[0].reshape(w_qkv.shape[1], -1)
    parts, backs, tables, visits = lax.optimization_barrier(
        (from_tp(gathered), backs, tables, visits)
    )
    start, hidden = first_hidden(parts, ln_gain, ln_bias)
    state = None
    for layer_index in range(LAYERS):
        if layer_index:
            weights_qkv = w_qkv[layer_index].reshape(w_qkv.shape[1], -1)
            state, cut = norm_rows(parts, state, ln_gain, ln_bias, layer_index, devices, tp_count)
            hidden = lax.all_to_all(cut, ("seq", "tp"), 0, 0).reshape(rows, -1)
        arriving = swap_cores(project_heads(hidden, weights_qkv, unit), seq_count)
        heads = to_distances(project_heads(hidden, weights_qkv, unit, arriving))
        arriving = swap_cores(project_units(hidden, w_fc1, layer_index), seq_count)
        units = project_units(hidden, w_fc1, layer_index, arriving)
        query, new_key, new_value = activate(heads, tables, width_local)
        units = to_distances(units)
        parts = attend(
            visits, query, swap_cores(query, seq_count), new_key, new_value,
            k_cache, v_cache, layer_index, new_tokens, groups,
        )
        parts, *units = lax.optimization_barrier((parts, *units))
        parts = lax.all_to_all(parts, "seq", 0, 0)
        arriving, half = (
            update(parts, units, start, b_fc1, w_out, w_fc2, layer_index, other, tp_count)
            for other in (True, False)
        )
        parts = to_distances(split(half, swap_cores(arriving, seq_count)))
        start = None
        if layer_index < LAYERS - 1:
            parts = share_rows(parts, tp_count)
            parts = [parts[0]] + [over_tp(parts[k], k) for k in range(1, tp_count)]
    last = last_parts(parts, state, tp_count)
    last = from_tp(last.astype(jnp.bfloat16))
    last = to_distances([last_rows(last)] * CHIPS)
    return restore(backs, last, [swap_cores(part, seq_count) for part in last], new_tokens)


def solution(mesh):
    in_specs = (
        P(),
        P(("seq", "tp"), None),
        P(),
        P(),
        P(),
        P("seq", None),
        P(None, "seq", "tp"),
        P(None, "seq", "tp"),
        P(),
        P(),
        P(None, "seq", None, "tp"),
        P(None, "seq", "tp"),
        P(None, "tp"),
        P(None, ("tp", "seq"), None),
        P(None, ("tp", "seq"), None),
    )
    out_specs = P()
    seq_count, tp_count = mesh.shape["seq"], mesh.shape["tp"]
    fits = tp_count == 4 and seq_count == HEADS // tp_count and seq_count == 2 * CHIPS
    return jax.shard_map(
        per_device if fits else per_device_any, mesh=mesh, in_specs=in_specs, out_specs=out_specs, check_vma=False
    )
```

```python
import functools
import math

import jax
import jax.numpy as jnp
from jax import lax
from jax.experimental import pallas as pl
from jax.experimental.pallas import tpu as pltpu
from jax.sharding import PartitionSpec as P

HEADS = 32
HEAD_DIM = 64
ROT = 32
LAYERS = 2
BLOCK = 128
SPAN = 512
CHIPS = 4
LANES = 128


very_negative = -1e30


def layer_norm(values, gain_row, bias_row):
    average = jnp.mean(values, axis=-1, keepdims=True)
    centred = values - average
    variance = jnp.mean(centred * centred, axis=-1, keepdims=True)
    return centred * lax.rsqrt(variance + 1e-05) * gain_row + bias_row


def rotary(values, positions):
    half_width = ROT // 2
    frequency = jnp.exp(
        jnp.arange(half_width, dtype=jnp.float32) * (-2.0 * math.log(10000.0) / ROT)
    )
    angles = positions.astype(jnp.float32)[:, None] * frequency[None, :]
    cosine = jnp.cos(angles)[:, None, :]
    sine_part = jnp.sin(angles)[:, None, :]
    low_half = values[..., :half_width]
    high_half = values[..., half_width:ROT]
    return jnp.concatenate(
        [
            low_half * cosine - high_half * sine_part,
            high_half * cosine + low_half * sine_part,
            values[..., ROT:],
        ],
        axis=-1,
    )


def combine_parts(left_part, right_part):
    max_left, sum_left, out_left = left_part
    max_right, sum_right, out_right = right_part
    top_value = jnp.maximum(max_left, max_right)
    scale_left = jnp.exp(max_left - top_value)
    scale_right = jnp.exp(max_right - top_value)
    return (
        top_value,
        sum_left * scale_left + sum_right * scale_right,
        out_left * scale_left[..., None] + out_right * scale_right[..., None],
    )


def full_total(values):
    return lax.psum(values, ("seq", "tp"))


def per_device_any(
    token_ids,
    embedding,
    group_of,
    prefix_len,
    tail_len,
    block_map,
    k_cache,
    v_cache,
    ln_gain,
    ln_bias,
    w_qkv,
    w_fc1,
    b_fc1,
    w_out,
    w_fc2,
):
    tp_count = lax.axis_size("tp")
    seq_index = lax.axis_index("seq")
    tp_index = lax.axis_index("tp")
    requests = token_ids.shape[0]
    new_tokens = token_ids.shape[1]
    groups = prefix_len.shape[0]
    heads_local = HEADS // tp_count
    width_local = heads_local * HEAD_DIM
    score_scale = 1.0 / math.sqrt(HEAD_DIM)
    vocab_rows = embedding.shape[0]
    first_row = (seq_index * tp_count + tp_index) * vocab_rows
    local_ids = token_ids.reshape(-1) - first_row
    inside = (local_ids >= 0) & (local_ids < vocab_rows)
    picked = jnp.take(embedding, jnp.clip(local_ids, 0, vocab_rows - 1), axis=0).astype(jnp.float32)
    picked = jnp.where(inside[:, None], picked, 0.0)
    start_states = full_total(picked).reshape(requests, new_tokens, -1)
    group_hit = group_of[:, None] == jnp.arange(groups, dtype=jnp.int32)[None, :]
    shared_len = jnp.sum(jnp.where(group_hit, prefix_len[None, :], 0), axis=1)
    base_positions = shared_len + tail_len
    seg_len = jnp.concatenate([prefix_len, tail_len])
    seg_count = seg_len.shape[0]
    blocks_local = block_map.shape[0]
    seg_blk = block_map[:, 0]
    rank_blk = block_map[:, 1]
    seg_hit = seg_blk[:, None] == jnp.arange(seg_count, dtype=jnp.int32)[None, :]
    len_blk = jnp.sum(jnp.where(seg_hit, seg_len[None, :], 0), axis=1)
    slot_positions = rank_blk[:, None] * BLOCK + jnp.arange(BLOCK, dtype=jnp.int32)[None, :]
    live_slot = ((seg_blk[:, None] >= 0) & (slot_positions < len_blk[:, None])).reshape(-1)
    seg_slot = jnp.broadcast_to(seg_blk[:, None], (blocks_local, BLOCK)).reshape(-1)
    own_tail = seg_slot[None, :] == (groups + jnp.arange(requests, dtype=jnp.int32))[:, None]
    own_prompt = seg_slot[None, :] == group_of[:, None]
    allowed = (own_tail | own_prompt) & live_slot[None, :]
    step_count = allowed.shape[1] // SPAN
    allowed_steps = allowed.reshape(requests, step_count, SPAN).transpose(1, 0, 2)
    rows_local = w_qkv.shape[1]
    unit_count = w_fc2.shape[1]
    sub_width = w_out.shape[1]
    token_index = jnp.arange(new_tokens, dtype=jnp.int32)
    new_keys = [
        jnp.zeros((requests, new_tokens, heads_local, HEAD_DIM), jnp.bfloat16)
        for layer_index in range(LAYERS)
    ]
    new_values = [
        jnp.zeros((requests, new_tokens, heads_local, HEAD_DIM), jnp.bfloat16)
        for layer_index in range(LAYERS)
    ]
    results = []
    for token_step in range(new_tokens):
        hidden_state = start_states[:, token_step]
        positions = base_positions + token_step
        for layer_index in range(LAYERS):
            normed = layer_norm(hidden_state, ln_gain[layer_index], ln_bias[layer_index]).astype(
                jnp.bfloat16
            )
            my_rows = lax.dynamic_slice_in_dim(normed, seq_index * rows_local, rows_local, 1)
            part_proj = jnp.dot(
                my_rows,
                w_qkv[layer_index].reshape(rows_local, -1),
                preferred_element_type=jnp.float32,
            )
            part_fc1 = jnp.dot(my_rows, w_fc1[layer_index], preferred_element_type=jnp.float32)
            attention_proj, fc1_all = lax.psum((part_proj, part_fc1), "seq")
            pre_act = lax.dynamic_slice_in_dim(fc1_all, seq_index * unit_count, unit_count, 1)
            pre_act = (
                pre_act
                + lax.dynamic_slice_in_dim(
                    b_fc1[layer_index], seq_index * unit_count, unit_count, 0
                )[None, :]
            )
            activated = jax.nn.gelu(pre_act, approximate=True).astype(jnp.bfloat16)
            attention_proj = attention_proj.reshape(requests, 3, heads_local, HEAD_DIM)
            queries = rotary(attention_proj[:, 0], positions).astype(jnp.bfloat16)
            key_rows = rotary(attention_proj[:, 1], positions).astype(jnp.bfloat16)
            value_rows = attention_proj[:, 2].astype(jnp.bfloat16)
            new_keys[layer_index] = new_keys[layer_index].at[:, token_step].set(key_rows)
            new_values[layer_index] = new_values[layer_index].at[:, token_step].set(value_rows)
            key_steps = k_cache[layer_index].reshape(step_count, SPAN, heads_local, HEAD_DIM)
            value_steps = v_cache[layer_index].reshape(step_count, SPAN, heads_local, HEAD_DIM)

            def cache_step(carry, inputs):
                run_max, run_sum, run_out = carry
                key_block, value_block, allow_block = inputs
                scores = (
                    jnp.einsum(
                        "rhd,shd->hrs", queries, key_block, preferred_element_type=jnp.float32
                    )
                    * score_scale
                )
                scores = jnp.where(allow_block[None], scores, very_negative)
                next_max = jnp.maximum(run_max, jnp.max(scores, axis=2))
                weights = jnp.where(allow_block[None], jnp.exp(scores - next_max[..., None]), 0.0)
                shrink = jnp.exp(run_max - next_max)
                next_sum = run_sum * shrink + jnp.sum(weights, axis=2)
                next_out = run_out * shrink[..., None] + jnp.einsum(
                    "hrs,shd->hrd",
                    weights.astype(jnp.bfloat16),
                    value_block,
                    preferred_element_type=jnp.float32,
                )
                return ((next_max, next_sum, next_out), None)

            start_carry = (
                jnp.full((heads_local, requests), very_negative, jnp.float32),
                jnp.zeros((heads_local, requests), jnp.float32),
                jnp.zeros((heads_local, requests, HEAD_DIM), jnp.float32),
            )
            (part_max, part_sum, part_out), unused = lax.scan(
                cache_step, start_carry, (key_steps, value_steps, allowed_steps)
            )
            cache_max = lax.pmax(part_max, "seq")
            factor = jnp.exp(part_max - cache_max)
            cache_sum, cache_out = (
                lax.psum((part_sum * factor).astype(jnp.bfloat16), "seq").astype(jnp.float32),
                lax.psum((part_out * factor[..., None]).astype(jnp.bfloat16), "seq").astype(
                    jnp.float32
                ),
            )
            visible = (token_index <= token_step)[None, None, :]
            fresh_scores = (
                jnp.einsum(
                    "rhd,rjhd->hrj",
                    queries,
                    new_keys[layer_index],
                    preferred_element_type=jnp.float32,
                )
                * score_scale
            )
            fresh_scores = jnp.where(visible, fresh_scores, very_negative)
            fresh_max = jnp.max(fresh_scores, axis=2)
            fresh_weights = jnp.where(visible, jnp.exp(fresh_scores - fresh_max[..., None]), 0.0)
            fresh_sum = jnp.sum(fresh_weights, axis=2)
            fresh_out = jnp.einsum(
                "hrj,rjhd->hrd",
                fresh_weights.astype(jnp.bfloat16),
                new_values[layer_index],
                preferred_element_type=jnp.float32,
            )
            joint_max, denom_total, weighted = combine_parts(
                (cache_max, cache_sum, cache_out), (fresh_max, fresh_sum, fresh_out)
            )
            attended = (weighted / denom_total[..., None]).astype(jnp.bfloat16)
            attended = attended.transpose(1, 0, 2).reshape(requests, width_local)
            my_cols = lax.dynamic_slice_in_dim(attended, seq_index * sub_width, sub_width, 1)
            update = jnp.dot(my_cols, w_out[layer_index], preferred_element_type=jnp.float32)
            update = update + jnp.dot(
                activated, w_fc2[layer_index], preferred_element_type=jnp.float32
            )
            hidden_state = hidden_state + full_total(update)
        results.append(hidden_state)
    stacked = jnp.stack(results, axis=1)
    return stacked


def swap_cores(values, seq_count):
    return lax.ppermute(values, "seq", [(i, i ^ 1) for i in range(seq_count)])


def in_hbm(values):
    return pltpu.with_memory_space_constraint(values, pltpu.HBM)


def compiler_params(megabytes=32):
    return pltpu.CompilerParams(vmem_limit_bytes=megabytes * 2**20)


def whole(memory_space=pltpu.VMEM):
    return pl.BlockSpec(memory_space=memory_space)


def layer_block(layer_index, shape):
    return pl.BlockSpec((1,) + shape, lambda step: (layer_index,) + (0,) * len(shape))


def same_block(shape):
    return pl.BlockSpec(shape, lambda step: (0,) * len(shape))


def order_kernel(new_tokens, group_ref, prefix_ref, tail_ref, map_ref, rank_ref, position_ref, visit_ref, count_ref):
    requests = group_ref.shape[0]
    groups = prefix_ref.shape[0]
    per_group = requests // groups
    blocks = map_ref.shape[1]
    for group in range(groups):
        count_ref[group] = 0

    def place(request, unused):
        group = group_ref[request]
        seat = count_ref[group]
        count_ref[group] = seat + 1
        rank = group * per_group + seat
        rank_ref[request] = rank
        start = prefix_ref[group] + tail_ref[request]
        for token in range(new_tokens):
            position_ref[rank * new_tokens + token] = start + token
        return unused

    lax.fori_loop(0, requests, place, 0)

    def look(block, unused):
        segment, depth = map_ref[0, block], map_ref[1, block]
        is_tail = segment >= groups
        request = jnp.clip(segment - groups, 0, requests - 1)
        prompt = jnp.clip(segment, 0, groups - 1)
        seat = rank_ref[request]
        first = jnp.where(is_tail, (seat % per_group) * new_tokens, 0)
        length = jnp.where(is_tail, tail_ref[request], prefix_ref[prompt])
        visit_ref[block] = jnp.where(is_tail, seat // per_group, prompt)
        visit_ref[blocks + block] = jnp.where(segment < 0, 0, length - depth * BLOCK)
        visit_ref[2 * blocks + block] = first
        visit_ref[3 * blocks + block] = jnp.where(is_tail, first + new_tokens, per_group * new_tokens)
        return unused

    lax.fori_loop(0, blocks, look, 0)


def order_requests(group_of, prefix_len, tail_len, block_map, new_tokens):
    requests = group_of.shape[0]
    smem = whole(pltpu.SMEM)
    return pl.pallas_call(
        functools.partial(order_kernel, new_tokens),
        out_shape=(
            jax.ShapeDtypeStruct((requests,), jnp.int32),
            jax.ShapeDtypeStruct((requests * new_tokens,), jnp.int32),
            jax.ShapeDtypeStruct((4 * block_map.shape[0],), jnp.int32),
        ),
        in_specs=[smem] * 4,
        out_specs=(smem, smem, smem),
        scratch_shapes=[pltpu.SMEM((prefix_len.shape[0],), jnp.int32)],
        name="order_requests",
    )(group_of, prefix_len, tail_len, block_map.T)


def thirds(values):
    high = values.astype(jnp.bfloat16).astype(jnp.float32)
    middle = (values - high).astype(jnp.bfloat16).astype(jnp.float32)
    return high, middle, values - high - middle


def row_block(rows):
    width = rows[0].shape[1]
    line = lax.broadcasted_iota(jnp.int32, (8, width), 0)
    block = jnp.zeros((8, width), jnp.float32)
    for index, row in enumerate(rows):
        block = jnp.where(line == index, row, block)
    return block


def column_to_row(column):
    return jnp.broadcast_to(column, (column.shape[0], LANES)).T[0:1]


def row_to_column(row):
    return jnp.broadcast_to(row, (LANES, row.shape[1])).T


def ranks(group_ref):
    requests = group_ref.shape[1]
    across = lax.broadcasted_iota(jnp.int32, (requests, requests), 1)
    down = lax.broadcasted_iota(jnp.int32, (requests, requests), 0)
    group_row = group_ref[0:1, :]
    group_column = jnp.sum(jnp.where(across == down, group_row, 0), axis=1, keepdims=True)
    ahead = (group_column < group_row) | ((group_column == group_row) & (down < across))
    return jnp.sum(jnp.where(ahead, 1, 0), axis=0, keepdims=True)


def row_sums(lines):
    block = row_block([part for line in lines for part in thirds(line)])
    return jnp.concatenate([block, jnp.zeros_like(block)], axis=0).astype(jnp.bfloat16)


def from_row_sums(block):
    block = block.astype(jnp.float32)
    line = lax.broadcasted_iota(jnp.int32, block.shape, 0)
    return [
        jnp.sum(jnp.where((line >= start) & (line < start + 3), block, 0.0), axis=0, keepdims=True)
        for start in (0, 3)
    ]


def embed_kernel(
    token_ref, group_ref, table_hbm, near_ref, far_ref, own_ref,
    table_ref, hot_ref, row_ref, semaphores,
):
    core = lax.axis_index("seq") % 2
    first = (lax.axis_index("seq") * lax.axis_size("tp") + lax.axis_index("tp")) * table_ref.shape[1]
    new_tokens, requests = token_ref.shape
    rows, unit = near_ref.shape[1:]
    copies = []
    for chip in range(CHIPS):
        copies.append(
            pltpu.make_async_copy(
                table_hbm.at[:, pl.ds(chip * 2 * unit, 2 * unit)], table_ref.at[chip], semaphores.at[chip]
            )
        )
        copies[-1].start()
    rank_row = ranks(group_ref)
    line = lax.broadcasted_iota(jnp.int32, (rows, requests), 0)
    ids = jnp.zeros((rows, requests), jnp.int32)
    for token in range(new_tokens):
        match = (rank_row == line // new_tokens) & (line % new_tokens == token)
        ids = jnp.where(match, token_ref[token : token + 1, :], ids)
    ids = jnp.sum(ids, axis=1, keepdims=True) - first
    entry = lax.broadcasted_iota(jnp.int32, hot_ref.shape, 1)
    hot_ref[...] = jnp.where(entry == ids, 1.0, 0.0).astype(jnp.bfloat16)
    total = jnp.zeros((rows, LANES), jnp.float32)
    for chip, copy in enumerate(copies):
        copy.wait()
        chosen = jnp.dot(hot_ref[...], table_ref[chip], preferred_element_type=jnp.float32)
        for start in range(0, 2 * unit, LANES):
            total = total + chosen[:, start : start + LANES]
        chosen = chosen.astype(jnp.bfloat16)
        row_ref[:, chip * 2 * unit : (chip + 1) * 2 * unit] = chosen
        left, right = chosen[:, :unit], chosen[:, unit:]
        near_ref[chip] = jnp.where(core == 0, left, right)
        far_ref[chip * rows : (chip + 1) * rows] = jnp.where(core == 0, right, left)
    features = row_ref.shape[1]
    mean = jnp.sum(total, axis=1, keepdims=True) * (1.0 / features)
    squares = jnp.zeros((rows, LANES), jnp.float32)
    for start in range(0, features, LANES):
        centred = row_ref[:, start : start + LANES].astype(jnp.float32) - mean
        squares = squares + centred * centred
    variance = jnp.sum(squares, axis=1, keepdims=True) * (1.0 / features)
    held = (ids >= 0) & (ids < hot_ref.shape[1])
    scale = jnp.where(held, lax.rsqrt(variance + 1e-05), 0.0)
    mean, scale = column_to_row(mean), column_to_row(scale)
    own_ref[...] = row_block([mean, scale])
    far_ref[CHIPS * rows :] = row_sums([mean, scale])


def embed(token_ids, group_of, embedding, unit):
    rows = token_ids.shape[0] * token_ids.shape[1]
    return pl.pallas_call(
        embed_kernel,
        out_shape=(
            jax.ShapeDtypeStruct((CHIPS, rows, unit), jnp.bfloat16),
            pltpu.HBM((CHIPS * rows + 16, unit), jnp.bfloat16),
            jax.ShapeDtypeStruct((8, rows), jnp.float32),
        ),
        in_specs=[whole(), whole(), whole(pltpu.HBM)],
        out_specs=(whole(),) * 3,
        scratch_shapes=[
            pltpu.VMEM((CHIPS, embedding.shape[0], 2 * unit), jnp.bfloat16),
            pltpu.VMEM((rows, embedding.shape[0]), jnp.bfloat16),
            pltpu.VMEM((rows, embedding.shape[1]), jnp.bfloat16),
            pltpu.SemaphoreType.DMA((CHIPS,)),
        ],
        compiler_params=compiler_params(24),
        name="embed",
    )(in_hbm(token_ids.T), in_hbm(group_of[None, :]), in_hbm(embedding))


def join_kernel(near_ref, far_ref, own_ref, out_ref, *refs):
    *out_hbms, leave_ref, semaphores = refs
    here = lax.axis_index("seq") // 2
    rows = near_ref.shape[1]
    mean, scale = from_row_sums(far_ref[CHIPS * rows :])
    lines = row_sums([mean + own_ref[0:1, :], scale + own_ref[1:2, :]])
    leaving = []
    for distance in reversed(range(CHIPS)):
        chip = here ^ distance
        far = far_ref[pl.ds(pl.multiple_of(chip * rows, rows), rows), :].astype(jnp.float32)
        joined = (near_ref[chip].astype(jnp.float32) + far).astype(jnp.bfloat16)
        if distance:
            leave_ref[distance - 1, :rows] = joined
            leave_ref[distance - 1, rows:] = lines
            leaving.append(
                pltpu.make_async_copy(
                    leave_ref.at[distance - 1], out_hbms[distance - 1], semaphores.at[distance - 1]
                )
            )
            leaving[-1].start()
        else:
            out_ref[:rows] = joined
            out_ref[rows:] = lines
    for copy in leaving:
        copy.wait()


def join(near, far, own):
    chips, rows, unit = near.shape
    one = (rows + 16, unit)
    return pl.pallas_call(
        join_kernel,
        out_shape=(jax.ShapeDtypeStruct(one, jnp.bfloat16),) + (pltpu.HBM(one, jnp.bfloat16),) * (chips - 1),
        in_specs=[whole()] * 3,
        out_specs=(whole(),) + (whole(pltpu.HBM),) * (chips - 1),
        scratch_shapes=[pltpu.VMEM((chips - 1,) + one, jnp.bfloat16), pltpu.SemaphoreType.DMA((chips - 1,))],
        compiler_params=compiler_params(16),
        name="join",
    )(near, far, own)


def gather_kernel(a_ref, b_ref, c_ref, d_ref, out_hbm, out_ref, semaphore):
    rows = out_ref.shape[0] - 16
    near = a_ref[...].astype(jnp.float32) + b_ref[...].astype(jnp.float32)
    far = c_ref[...].astype(jnp.float32) + d_ref[...].astype(jnp.float32)
    total = near + far
    out_ref[:rows] = total[:rows].astype(jnp.bfloat16)
    out_ref[rows:] = row_sums(from_row_sums(total[rows:]))
    copy = pltpu.make_async_copy(out_ref, out_hbm, semaphore)
    copy.start()
    copy.wait()


def gather(parts):
    return pl.pallas_call(
        gather_kernel,
        out_shape=pltpu.HBM(parts[0].shape, jnp.bfloat16),
        in_specs=[whole()] * 4,
        out_specs=whole(pltpu.HBM),
        scratch_shapes=[pltpu.VMEM(parts[0].shape, jnp.bfloat16), pltpu.SemaphoreType.DMA],
        compiler_params=compiler_params(16),
        name="gather",
    )(*parts)


def first_kernel(a_hbm, b_ref, c_ref, d_ref, gain_ref, bias_ref, start_ref, hidden_ref, a_ref, semaphore):
    rows, unit = hidden_ref.shape
    copy = pltpu.make_async_copy(a_hbm, a_ref, semaphore)
    copy.start()
    far = c_ref[...].astype(jnp.float32) + d_ref[...].astype(jnp.float32)
    copy.wait()
    total = (a_ref[...].astype(jnp.float32) + b_ref[...].astype(jnp.float32)) + far
    mean, scale = (row_to_column(line) for line in from_row_sums(total[rows:]))
    columns = pl.ds(pl.multiple_of(lax.axis_index("seq") * unit, unit), unit)
    gain, bias = gain_ref[0:1, columns], bias_ref[0:1, columns]
    for start in range(0, unit, LANES):
        span = slice(start, start + LANES)
        state = total[:rows, span]
        start_ref[:, span] = state.astype(jnp.bfloat16)
        hidden_ref[:, span] = ((state - mean) * scale * gain[:, span] + bias[:, span]).astype(jnp.bfloat16)


def first_hidden(parts, ln_gain, ln_bias):
    one = jax.ShapeDtypeStruct((parts[0].shape[0] - 16, parts[0].shape[1]), jnp.bfloat16)
    return pl.pallas_call(
        first_kernel,
        out_shape=(one, one),
        in_specs=[whole(pltpu.HBM)] + [whole()] * 5,
        out_specs=(whole(), whole()),
        scratch_shapes=[pltpu.VMEM(parts[0].shape, jnp.bfloat16), pltpu.SemaphoreType.DMA],
        compiler_params=compiler_params(16),
        name="first_hidden",
    )(in_hbm(parts[0]), *parts[1:], ln_gain, ln_bias)


def norm_kernel(layer_index, tp_count, *refs):
    *part_refs, gain_ref, bias_ref, next_ref, cut_ref = refs
    state = functools.reduce(jnp.add, [ref[...].astype(jnp.float32) for ref in part_refs])
    next_ref[...] = state
    average = jnp.mean(state, axis=-1, keepdims=True)
    centred = state - average
    variance = jnp.mean(centred * centred, axis=-1, keepdims=True)
    gain = gain_ref[layer_index : layer_index + 1, :]
    bias = bias_ref[layer_index : layer_index + 1, :]
    normed = (centred * lax.rsqrt(variance + 1e-05) * gain + bias).astype(jnp.bfloat16)
    width = cut_ref.shape[2]
    for place in range(cut_ref.shape[0]):
        start = (place // tp_count) * width
        cut_ref[place] = normed[:, start : start + width]


def norm_rows(parts, state, ln_gain, ln_bias, layer_index, devices, tp_count):
    rows, width = parts[0].shape
    cut = width // (devices // tp_count)
    operands = list(parts) + ([] if state is None else [state]) + [ln_gain, ln_bias]
    return pl.pallas_call(
        functools.partial(norm_kernel, layer_index, tp_count),
        out_shape=(
            jax.ShapeDtypeStruct((rows, width), jnp.float32),
            jax.ShapeDtypeStruct((devices, rows, cut), jnp.bfloat16),
        ),
        in_specs=[whole()] * len(operands),
        out_specs=(whole(), whole()),
        compiler_params=compiler_params(16),
        name="norm_rows",
    )(*operands)


def share_kernel(a_ref, b_ref, c_ref, d_ref, *out_refs):
    total = functools.reduce(jnp.add, [ref[...].astype(jnp.float32) for ref in (a_ref, b_ref, c_ref, d_ref)])
    mine = out_refs[0].shape[0]
    for owner in range(len(out_refs)):
        for distance, ref in enumerate(out_refs):
            @pl.when(lax.axis_index("tp") == owner ^ distance)
            def put(ref=ref, owner=owner):
                ref[...] = total[owner * mine : (owner + 1) * mine].astype(ref.dtype)


def share_rows(parts, tp_count):
    rows, width = parts[0].shape
    one = (rows // tp_count, width)
    return pl.pallas_call(
        share_kernel,
        out_shape=(jax.ShapeDtypeStruct(one, jnp.float32),)
        + (jax.ShapeDtypeStruct(one, jnp.bfloat16),) * (tp_count - 1),
        in_specs=[whole()] * 4,
        out_specs=(whole(),) * tp_count,
        compiler_params=compiler_params(16),
        name="share_rows",
    )(*parts)


def last_parts_kernel(tp_count, a_ref, b_ref, c_ref, d_ref, state_ref, out_ref):
    near = a_ref[...].astype(jnp.float32) + b_ref[...].astype(jnp.float32)
    far = c_ref[...].astype(jnp.float32) + d_ref[...].astype(jnp.float32)
    total = near + far
    mine = state_ref.shape[0]
    owner = lax.axis_index("tp")
    for place in range(tp_count):
        rows = slice(place * mine, (place + 1) * mine)
        total_rows = total[rows] + jnp.where(owner == place, 1.0, 0.0) * state_ref[...]
        out_ref[rows] = total_rows.astype(jnp.bfloat16)


def last_parts(parts, state, tp_count):
    return pl.pallas_call(
        functools.partial(last_parts_kernel, tp_count),
        out_shape=jax.ShapeDtypeStruct(parts[0].shape, jnp.bfloat16),
        in_specs=[whole()] * 5,
        out_specs=whole(),
        compiler_params=compiler_params(16),
        name="last_parts",
    )(*parts, state)


def split_kernel(half_ref, arrived_ref, out_ref, *refs):
    *out_hbms, leave_ref, semaphores = refs
    share = out_ref.shape[0]
    leaving = []
    for distance in reversed(range(CHIPS)):
        rows = slice(distance * share, (distance + 1) * share)
        joined = half_ref[rows] + arrived_ref[rows].astype(jnp.float32)
        if distance:
            leave_ref[distance - 1] = joined.astype(jnp.bfloat16)
            leaving.append(
                pltpu.make_async_copy(
                    leave_ref.at[distance - 1], out_hbms[distance - 1], semaphores.at[distance - 1]
                )
            )
            leaving[-1].start()
        else:
            out_ref[...] = joined
    for copy in leaving:
        copy.wait()


def split(half, arrived):
    one = (half.shape[0] // CHIPS, half.shape[1])
    return pl.pallas_call(
        split_kernel,
        out_shape=(jax.ShapeDtypeStruct(one, jnp.float32),) + (pltpu.HBM(one, jnp.bfloat16),) * (CHIPS - 1),
        in_specs=[whole()] * 2,
        out_specs=(whole(),) + (whole(pltpu.HBM),) * (CHIPS - 1),
        scratch_shapes=[pltpu.VMEM((CHIPS - 1,) + one, jnp.bfloat16), pltpu.SemaphoreType.DMA((CHIPS - 1,))],
        compiler_params=compiler_params(16),
        name="split",
    )(half, arrived)


def last_kernel(a_ref, b_ref, c_ref, d_ref, out_ref):
    near = a_ref[...].astype(jnp.float32) + b_ref[...].astype(jnp.float32)
    far = c_ref[...].astype(jnp.float32) + d_ref[...].astype(jnp.float32)
    out_ref[...] = (near + far).astype(jnp.bfloat16)


def last_rows(parts):
    return pl.pallas_call(
        last_kernel,
        out_shape=jax.ShapeDtypeStruct(parts[0].shape, jnp.bfloat16),
        in_specs=[whole()] * 4,
        out_specs=whole(),
        compiler_params=compiler_params(16),
        name="last_rows",
    )(*parts)


def back_kernel(new_tokens, group_ref, near_ref, far_ref):
    rows, half = near_ref.shape
    requests = group_ref.shape[1]
    rank_row = ranks(group_ref)
    line = lax.broadcasted_iota(jnp.int32, (rows, requests), 0)
    column = lax.broadcasted_iota(jnp.int32, (rows, requests), 1)
    wanted = jnp.sum(jnp.where(column == line // new_tokens, rank_row, 0), axis=1, keepdims=True)
    line = lax.broadcasted_iota(jnp.int32, near_ref.shape, 0)
    entry = lax.broadcasted_iota(jnp.int32, near_ref.shape, 1)
    share = half // CHIPS
    here = lax.axis_index("seq") // 2
    for ref, other in ((near_ref, False), (far_ref, True)):
        held = (((entry // share) ^ here) * 2 + core_parity(other)) * share + entry % share
        back = held == wanted * new_tokens + line % new_tokens
        ref[...] = jnp.where(back, 1.0, 0.0).astype(jnp.bfloat16)


def back_rows(group_of, new_tokens):
    rows = group_of.shape[0] * new_tokens
    one = jax.ShapeDtypeStruct((rows, rows // 2), jnp.bfloat16)
    return pl.pallas_call(
        functools.partial(back_kernel, new_tokens),
        out_shape=(one, one),
        in_specs=[whole()],
        out_specs=(whole(), whole()),
        compiler_params=compiler_params(16),
        name="back_rows",
    )(group_of[None, :])


def restore_kernel(near_back_ref, far_back_ref, *refs):
    *row_refs, out_hbm, out_ref, semaphores = refs
    requests, new_tokens, width = out_ref.shape
    step = width // semaphores.shape[0]
    leaving = []
    for index, start in enumerate(range(0, width, step)):
        span = slice(start, start + step)
        near, far = (
            jnp.concatenate([ref[:, span] for ref in half], axis=0)
            for half in (row_refs[:CHIPS], row_refs[CHIPS:])
        )
        rows = jnp.dot(near_back_ref[...], near, preferred_element_type=jnp.float32) + jnp.dot(
            far_back_ref[...], far, preferred_element_type=jnp.float32
        )
        out_ref[:, :, span] = rows.reshape(requests, new_tokens, step)
        span = pl.ds(start, step)
        leaving.append(
            pltpu.make_async_copy(out_ref.at[:, :, span], out_hbm.at[:, :, span], semaphores.at[index])
        )
        leaving[-1].start()
    for copy in leaving:
        copy.wait()


def restore(backs, near, far, new_tokens):
    rows = backs[0].shape[0]
    shape = (rows // new_tokens, new_tokens, near[0].shape[1])
    return pl.pallas_call(
        restore_kernel,
        out_shape=pltpu.HBM(shape, jnp.float32),
        in_specs=[whole()] * (2 + 2 * CHIPS),
        out_specs=whole(pltpu.HBM),
        scratch_shapes=[pltpu.VMEM(shape, jnp.float32), pltpu.SemaphoreType.DMA((4,))],
        compiler_params=compiler_params(24),
        name="restore",
    )(*backs, *near, *far)


def core_parity(other):
    return 1 - lax.axis_index("seq") % 2 if other else lax.axis_index("seq") % 2


def heads_kernel(joins, hidden_ref, qkv_ref, *refs):
    if joins:
        arrived_ref, near_ref, *out_hbms, out_ref, semaphores = refs
    else:
        out_ref = refs[0]
    parity = core_parity(not joins)
    here = lax.axis_index("seq") // 2
    rows, unit = hidden_ref.shape
    width = qkv_ref.shape[1] // 3
    share = rows // CHIPS // 2
    half = rows // 2
    pieces = width // unit
    tall = 2 * pieces * share

    def joined(values, start):
        if joins:
            values = values + arrived_ref[start : start + values.shape[0]].astype(jnp.float32)
        return values.astype(jnp.bfloat16)

    def picked(chips):
        return jnp.concatenate(
            [
                hidden_ref[pl.ds(pl.multiple_of((2 * chip + parity) * share, share), share), :]
                for chip in chips
            ],
            axis=0,
        )

    queries = jnp.dot(picked(range(CHIPS)), qkv_ref[:, :width], preferred_element_type=jnp.float32)
    for piece in range(pieces):
        start = piece * half
        query = joined(queries[:, piece * unit : (piece + 1) * unit], start)
        if joins:
            for distance in range(CHIPS):
                out_ref[distance, tall + start : tall + start + half] = query
        else:
            out_ref[start : start + half] = query
    others = jnp.dot(
        picked([here ^ distance for distance in range(CHIPS)]), qkv_ref[:, width:], preferred_element_type=jnp.float32
    )
    base = pieces * half
    leaving = []
    for distance in reversed(range(CHIPS)):
        for piece in range(2 * pieces):
            start = base + (distance * 2 * pieces + piece) * share
            value = joined(
                others[distance * share : (distance + 1) * share, piece * unit : (piece + 1) * unit], start
            )
            if joins:
                out_ref[distance, piece * share : (piece + 1) * share] = value
            else:
                out_ref[start : start + share] = value
        if joins and distance:
            copy = pltpu.make_async_copy(
                out_ref.at[distance], out_hbms[distance - 1], semaphores.at[distance - 1]
            )
            copy.start()
            leaving.append(copy)
    if joins:
        near_ref[...] = out_ref[0]
    for copy in leaving:
        copy.wait()


def project_heads(hidden, weights_qkv, unit, arrived=None):
    rows = hidden.shape[0]
    pieces = weights_qkv.shape[1] // 3 // unit
    tall = 2 * pieces * (rows // CHIPS // 2)
    common = pieces * (rows // 2)
    extra = [] if arrived is None else [arrived]
    out_shape = jax.ShapeDtypeStruct((common + CHIPS * tall, unit), jnp.bfloat16)
    out_specs = whole()
    scratch = []
    if arrived is not None:
        one = (tall + common, unit)
        out_shape = (jax.ShapeDtypeStruct(one, jnp.bfloat16),) + (pltpu.HBM(one, jnp.bfloat16),) * (CHIPS - 1)
        out_specs = (whole(),) + (whole(pltpu.HBM),) * (CHIPS - 1)
        scratch = [pltpu.VMEM((CHIPS,) + one, jnp.bfloat16), pltpu.SemaphoreType.DMA((CHIPS - 1,))]
    return pl.pallas_call(
        functools.partial(heads_kernel, arrived is not None),
        out_shape=out_shape,
        in_specs=[whole()] * (2 + len(extra)),
        out_specs=out_specs,
        scratch_shapes=scratch,
        compiler_params=compiler_params(24),
        name="project_heads",
    )(hidden, weights_qkv, *extra)


def units_kernel(joins, hidden_ref, fc1_ref, *refs):
    arrived_ref, out_refs = (refs[0], refs[1:]) if joins else (None, refs)
    parity = core_parity(not joins)
    here = lax.axis_index("seq") // 2
    unit = fc1_ref.shape[2] // CHIPS // 2
    hidden = hidden_ref[...]
    for distance in range(CHIPS):
        target = 2 * (here ^ distance) + parity
        columns = pl.ds(pl.multiple_of(target * unit, unit), unit)
        pre = jnp.dot(hidden, fc1_ref[0, :, columns], preferred_element_type=jnp.float32)
        if joins:
            pre = pre + arrived_ref[distance].astype(jnp.float32)
            out_refs[distance][...] = pre.astype(jnp.bfloat16)
        else:
            out_refs[0][distance] = pre.astype(jnp.bfloat16)


def project_units(hidden, w_fc1, layer_index, arrived=None):
    rows = hidden.shape[0]
    unit = w_fc1.shape[2] // CHIPS // 2
    extra = [] if arrived is None else [arrived]
    if arrived is None:
        out_shape = jax.ShapeDtypeStruct((CHIPS, rows, unit), jnp.bfloat16)
    else:
        out_shape = (jax.ShapeDtypeStruct((rows, unit), jnp.bfloat16),) * CHIPS
    return pl.pallas_call(
        functools.partial(units_kernel, arrived is not None),
        grid=(1,),
        out_shape=out_shape,
        in_specs=[same_block(hidden.shape), layer_block(layer_index, w_fc1.shape[1:])]
        + [same_block(values.shape) for values in extra],
        out_specs=jax.tree.map(lambda leaf: same_block(leaf.shape), out_shape),
        compiler_params=compiler_params(24),
        name="project_units",
    )(hidden, w_fc1, *extra)


def activate_kernel(a_ref, b_ref, c_ref, d_ref, table_ref, query_ref, key_ref, value_ref):
    near = a_ref[...].astype(jnp.float32) + b_ref[...].astype(jnp.float32)
    far = c_ref[...].astype(jnp.float32) + d_ref[...].astype(jnp.float32)
    total = near + far
    share, width = key_ref.shape
    half = query_ref.shape[0]
    unit = a_ref.shape[1]
    lanes = table_ref.shape[2]
    pieces = width // unit
    own = pl.ds(pl.multiple_of((lax.axis_index("seq") // 2) * share, share), share)

    def put(target_ref, start, height, span, scale):
        for piece in range(pieces):
            for column in range(0, unit, lanes):
                first = start + piece * height
                values = total[first : first + height, column : column + lanes]
                if span is not None:
                    values = (
                        values * table_ref[0, span]
                        + pltpu.roll(values, lanes - ROT // 2, 1) * table_ref[1, span]
                        + pltpu.roll(values, ROT // 2, 1) * table_ref[2, span]
                    )
                values = values.astype(jnp.bfloat16)
                if scale is not None:
                    values = (values.astype(jnp.float32) * scale).astype(jnp.bfloat16)
                column_out = piece * unit + column
                target_ref[:, column_out : column_out + lanes] = values

    put(key_ref, 0, share, own, None)
    put(value_ref, pieces * share, share, None, None)
    put(query_ref, 2 * pieces * share, half, slice(None), 1.0 / math.sqrt(HEAD_DIM))


def activate(parts, tables, width):
    half = tables.shape[1]
    small = jax.ShapeDtypeStruct((half // CHIPS, width), jnp.bfloat16)
    return pl.pallas_call(
        activate_kernel,
        out_shape=(jax.ShapeDtypeStruct((half, width), jnp.bfloat16), small, small),
        in_specs=[whole()] * 5,
        out_specs=(whole(),) * 3,
        compiler_params=compiler_params(16),
        name="activate",
    )(*parts, tables)


def rotary_tables(positions, width):
    half = ROT // 2
    feature = lax.broadcasted_iota(jnp.int32, (1, width), 1) % HEAD_DIM
    frequency = jnp.exp((feature % half).astype(jnp.float32) * (-2.0 * math.log(10000.0) / ROT))
    angles = positions.astype(jnp.float32)[:, None] * frequency
    cosine, sine = jnp.cos(angles), jnp.sin(angles)
    return jnp.stack(
        [
            jnp.where(feature < ROT, cosine, 1.0),
            jnp.where(feature < half, -sine, 0.0),
            jnp.where((feature >= half) & (feature < ROT), sine, 0.0),
        ]
    )


def attend_kernel(
    layer_index, new_tokens,
    visit_hbm, query_ref, far_query_ref, new_key_ref, new_value_ref,
    key_hbm, value_hbm, out_ref,
    key_ref, value_ref, visit_ref, both_ref, score_ref, top_ref, sum_ref, mix_ref, semaphores, visit_semaphore,
):
    blocks = visit_ref.shape[0] // 4
    groups, tall, lanes = mix_ref.shape
    share = new_key_ref.shape[0]
    heads = tall // share
    chunks = semaphores.shape[1]
    chunk = key_ref.shape[0] // chunks

    def copy(kind, index):
        span = pl.ds(index * chunk, chunk)
        source, target = ((key_hbm, key_ref), (value_hbm, value_ref))[kind]
        return pltpu.make_async_copy(
            source.at[layer_index, span], target.at[span], semaphores.at[kind, index]
        )

    looking = pltpu.make_async_copy(visit_hbm, visit_ref, visit_semaphore)
    looking.start()
    for kind in range(2):
        for index in range(chunks):
            copy(kind, index).start()
    core = lax.axis_index("seq") % 2
    for chip in range(groups // 2):
        span = slice(chip * share, (chip + 1) * share)
        both_ref[2 * chip + core] = query_ref[span]
        both_ref[2 * chip + 1 - core] = far_query_ref[span]
    lane = lax.broadcasted_iota(jnp.int32, (share, lanes), 1)
    row = lax.broadcasted_iota(jnp.int32, (share, lanes), 0)
    top_ref[...] = jnp.full(top_ref.shape, very_negative, jnp.float32)
    sum_ref[...] = jnp.zeros(sum_ref.shape, jnp.float32)
    mix_ref[...] = jnp.zeros(mix_ref.shape, jnp.float32)

    def score(index, group, keys, mask):
        scores = []
        for pair in range(heads // 2):
            both = both_ref[group, :, pair * lanes : (pair + 1) * lanes]
            none = jnp.zeros_like(both)
            split = jnp.concatenate(
                [jnp.where(lane < HEAD_DIM, both, none), jnp.where(lane < HEAD_DIM, none, both)], axis=0
            )
            scores.append(
                lax.dot_general(
                    split, keys[:, pair * lanes : (pair + 1) * lanes], (((1,), (1,)), ((), ())),
                    preferred_element_type=jnp.float32,
                )
            )
        scores = jnp.concatenate(scores, axis=0).reshape(heads, share, BLOCK)
        scores = jnp.where(mask[None], scores, very_negative).reshape(tall, BLOCK)
        score_ref[index] = scores
        top_ref[group] = jnp.maximum(top_ref[group], scores)

    def mix(index, group, values):
        weight = jnp.exp(score_ref[index] - top_ref[group])
        sum_ref[group] += weight
        rounded = weight.astype(jnp.bfloat16)
        mix_ref[group] += jnp.concatenate(
            [
                jnp.dot(
                    rounded[pair * 2 * share : (pair + 1) * 2 * share],
                    values[:, pair * lanes : (pair + 1) * lanes],
                    preferred_element_type=jnp.float32,
                )
                for pair in range(heads // 2)
            ],
            axis=0,
        )

    own = lax.axis_index("seq")
    fill = jnp.zeros((BLOCK - share, new_key_ref.shape[1]), jnp.bfloat16)
    score(
        blocks, own, jnp.concatenate([new_key_ref[...], fill], axis=0),
        (lane // new_tokens == row // new_tokens) & (lane <= row),
    )
    looking.wait()
    owners = []
    for block in range(blocks):
        if (block * BLOCK) % chunk == 0:
            copy(0, block * BLOCK // chunk).wait()
        group, live, first, end = (visit_ref[field * blocks + block] for field in range(4))
        owners.append(group)
        score(
            block, group, key_ref[block * BLOCK : (block + 1) * BLOCK, :],
            (lane < live) & (row >= first) & (row < end),
        )
    for group in range(groups):
        top = jnp.max(top_ref[group], axis=1, keepdims=True)
        top_ref[group] = jnp.broadcast_to(top, (tall, lanes))
    mix(blocks, own, jnp.concatenate([new_value_ref[...], fill], axis=0))
    for block in range(blocks):
        if (block * BLOCK) % chunk == 0:
            copy(1, block * BLOCK // chunk).wait()
        mix(block, owners[block], value_ref[block * BLOCK : (block + 1) * BLOCK, :])

    level = jnp.zeros((tall, lanes), jnp.float32)
    column = lax.broadcasted_iota(jnp.int32, (tall, lanes), 1)

    def mean(group):
        total = jnp.sum(sum_ref[group], axis=1, keepdims=True)
        total = jnp.where(total <= 0.0, 1.0, total)
        own_level = jnp.where(column == group, top_ref[group] + jnp.log(total), 0.0)
        return mix_ref[group] / total, own_level

    for group in range(groups // 2):
        left, left_level = mean(group)
        right, right_level = mean(group + groups // 2)
        level = level + left_level + right_level
        for head in range(heads):
            rows = slice(head * share, (head + 1) * share)
            first, second = left[rows], right[rows]
            if head % 2:
                first = pltpu.roll(first, HEAD_DIM, 1)
            else:
                second = pltpu.roll(second, HEAD_DIM, 1)
            packed = jnp.where(lane < HEAD_DIM, first, second)
            out_ref[head, group * share : (group + 1) * share] = packed.astype(jnp.bfloat16)
    level = level.T[:groups]
    high = level.astype(jnp.bfloat16).astype(jnp.float32)
    middle = (level - high).astype(jnp.bfloat16).astype(jnp.float32)
    low = level - high - middle
    rest = jnp.concatenate([high, middle, low, jnp.zeros_like(low)], axis=0).astype(jnp.bfloat16)
    start = (groups // 2) * share
    for head in range(heads):
        column = head * share // lanes * lanes
        out_ref[head, start:] = rest[:, column : column + lanes]


def attend(visits, query, far_query, new_key, new_value, k_cache, v_cache, layer_index, new_tokens, groups):
    width = query.shape[1]
    rows = 2 * query.shape[0]
    slots = k_cache.shape[1]
    heads = width // HEAD_DIM
    share = rows // groups
    tall = heads * share
    lanes = 2 * HEAD_DIM
    chunks = 2
    state = pltpu.VMEM((groups, tall, lanes), jnp.float32)
    return pl.pallas_call(
        functools.partial(attend_kernel, layer_index, new_tokens),
        out_shape=jax.ShapeDtypeStruct((heads, rows // 2 + 4 * groups, lanes), jnp.bfloat16),
        in_specs=[whole(pltpu.HBM)] + [whole()] * 4 + [whole(pltpu.HBM)] * 2,
        out_specs=whole(),
        scratch_shapes=[
            pltpu.VMEM((slots, width), jnp.bfloat16),
            pltpu.VMEM((slots, width), jnp.bfloat16),
            pltpu.SMEM(visits.shape, jnp.int32),
            pltpu.VMEM((groups, share, width), jnp.bfloat16),
            pltpu.VMEM((visits.shape[0] // 4 + 1, tall, BLOCK), jnp.float32),
            state,
            state,
            state,
            pltpu.SemaphoreType.DMA((2, chunks)),
            pltpu.SemaphoreType.DMA,
        ],
        compiler_params=compiler_params(24),
        name="attend",
    )(in_hbm(visits), query, far_query, new_key, new_value, in_hbm(k_cache), in_hbm(v_cache))


def update_kernel(
    layer_index, other, tp_count, has_start, part_ref, bias_ref, out_weight_ref, fc2_ref, *refs
):
    *unit_refs, out_ref, scale_ref = refs
    if has_start:
        *unit_refs, start_ref = unit_refs
    seq_index = lax.axis_index("seq")
    parity = 1 - seq_index % 2 if other else seq_index % 2
    sources, tall, lanes = part_ref.shape
    unit = unit_refs[0].shape[1]
    share = unit_refs[0].shape[0] // sources
    groups = (tall - (sources // 2) * share) // 4
    levels = []
    for source in range(sources):
        parts = part_ref[source, (sources // 2) * share :, :].astype(jnp.float32)
        levels.append(parts[:groups] + parts[groups : 2 * groups] + parts[2 * groups : 3 * groups])
    top = functools.reduce(jnp.maximum, levels)
    scales = [jnp.exp(level - top) for level in levels]
    total = functools.reduce(jnp.add, scales)
    scales = [scale / total for scale in scales]
    blank = jnp.zeros((lanes - groups * sources, lanes), jnp.float32)
    scale_ref[...] = jnp.concatenate(scales + [blank], axis=0).T
    place = seq_index % (lanes // share)
    scale = scale_ref[pl.ds(pl.multiple_of(place * share, share), share), :]
    scale = jnp.where(parity == 0, scale, pltpu.roll(scale, lanes - 1, 1))
    here = lax.axis_index("seq") // 2
    next_scale = pltpu.roll(scale, lanes - 2, 1)
    lane = lax.broadcasted_iota(jnp.int32, (share, lanes), 1)
    first, second = [], []
    for pair in range(CHIPS // 2):
        pack = (here % 2) ^ pair
        rows = pl.ds(pl.multiple_of((2 * pack + parity) * share, share), share)
        pair_scale = jnp.where(pack == 0, scale, next_scale)
        mixed = jnp.zeros((share, lanes), jnp.float32)
        for source in range(sources):
            column = source * groups
            left = pair_scale[:, column : column + 1]
            right = pair_scale[:, column + groups // 2 : column + groups // 2 + 1]
            mixed = mixed + part_ref[source, rows, :].astype(jnp.float32) * jnp.where(
                lane < HEAD_DIM, left, right
            )
        turned = pltpu.roll(mixed, HEAD_DIM, 1)
        first.append(jnp.where(here < 2, mixed, turned)[:, :HEAD_DIM])
        second.append(jnp.where(here < 2, turned, mixed)[:, :HEAD_DIM])
    attended = jnp.concatenate(first + second, axis=0).astype(jnp.bfloat16)
    bias = bias_ref[
        layer_index : layer_index + 1, pl.ds(pl.multiple_of(seq_index * unit, unit), unit)
    ]
    hidden, started = [], []
    for piece in range(CHIPS):
        rows = pl.ds(pl.multiple_of((2 * (piece ^ here) + parity) * share, share), share)
        pre = functools.reduce(jnp.add, [ref[rows, :].astype(jnp.float32) for ref in unit_refs])
        hidden.append(jax.nn.gelu(pre + bias, approximate=True).astype(jnp.bfloat16))
        if has_start:
            started.append(start_ref[rows, :].astype(jnp.float32))
    change = jnp.dot(attended, out_weight_ref[0], preferred_element_type=jnp.float32) + jnp.dot(
        jnp.concatenate(hidden, axis=0), fc2_ref[0], preferred_element_type=jnp.float32
    )
    if not has_start:
        out_ref[...] = change.astype(out_ref.dtype)
        return
    started = jnp.concatenate(started, axis=0)
    for column in range(0, change.shape[1], unit):
        here = (seq_index * unit == column) & (lax.axis_index("tp") == 0)
        out_ref[:, column : column + unit] = (
            change[:, column : column + unit] + jnp.where(here, started, 0.0)
        ).astype(out_ref.dtype)


def update(parts, units, start, b_fc1, w_out, w_fc2, layer_index, other, tp_count):
    rows = units[0].shape[0] // 2
    width = w_out.shape[2]
    lanes = parts.shape[2]
    extra = list(units) + ([] if start is None else [start])
    return pl.pallas_call(
        functools.partial(update_kernel, layer_index, other, tp_count, start is not None),
        grid=(1,),
        out_shape=jax.ShapeDtypeStruct((rows, width), jnp.bfloat16 if other else jnp.float32),
        in_specs=[
            same_block(parts.shape),
            same_block(b_fc1.shape),
            layer_block(layer_index, w_out.shape[1:]),
            layer_block(layer_index, w_fc2.shape[1:]),
        ]
        + [same_block(units[0].shape)] * len(extra),
        out_specs=same_block((rows, width)),
        scratch_shapes=[pltpu.VMEM((lanes, lanes), jnp.float32)],
        compiler_params=compiler_params(),
        name="update",
    )(parts, b_fc1, w_out, w_fc2, *extra)


def per_device(
    token_ids, embedding, group_of, prefix_len, tail_len, block_map, k_cache, v_cache,
    ln_gain, ln_bias, w_qkv, w_fc1, b_fc1, w_out, w_fc2,
):
    seq_count, tp_count = lax.axis_size("seq"), lax.axis_size("tp")
    seq_index, tp_index = lax.axis_index("seq"), lax.axis_index("tp")
    devices = seq_count * tp_count
    core = seq_index % 2
    requests, new_tokens = token_ids.shape
    rows = requests * new_tokens
    groups = prefix_len.shape[0]
    share = rows // seq_count
    features = embedding.shape[1]
    width_local = k_cache.shape[2]
    unit = w_fc2.shape[1]

    def to_distances(parts):
        return [parts[0]] + [
            lax.ppermute(parts[k], "seq", [(i, i ^ (2 * k)) for i in range(seq_count)])
            for k in range(1, CHIPS)
        ]

    def over_tp(part, distance):
        return lax.ppermute(part, "tp", [(i, i ^ distance) for i in range(tp_count)])

    def from_tp(part):
        return [part] + [over_tp(part, k) for k in range(1, tp_count)]

    near, far, own = embed(token_ids, group_of, embedding, unit)
    parts = join(near, swap_cores(far, seq_count), own)
    gathered = gather(to_distances(parts))
    gathered, group_of = lax.optimization_barrier((gathered, group_of))
    rank, positions, visits = order_requests(group_of, prefix_len, tail_len, block_map, new_tokens)
    own_positions = lax.dynamic_index_in_dim(positions.reshape(CHIPS, 2, share), core, 1, keepdims=False)
    backs = back_rows(group_of, new_tokens)
    tables = rotary_tables(own_positions.reshape(-1), 2 * HEAD_DIM)
    weights_qkv = w_qkv[0].reshape(w_qkv.shape[1], -1)
    parts, backs, tables, visits = lax.optimization_barrier(
        (from_tp(gathered), backs, tables, visits)
    )
    start, hidden = first_hidden(parts, ln_gain, ln_bias)
    state = None
    for layer_index in range(LAYERS):
        if layer_index:
            weights_qkv = w_qkv[layer_index].reshape(w_qkv.shape[1], -1)
            state, cut = norm_rows(parts, state, ln_gain, ln_bias, layer_index, devices, tp_count)
            hidden = lax.all_to_all(cut, ("seq", "tp"), 0, 0).reshape(rows, -1)
        arriving = swap_cores(project_heads(hidden, weights_qkv, unit), seq_count)
        heads = to_distances(project_heads(hidden, weights_qkv, unit, arriving))
        arriving = swap_cores(project_units(hidden, w_fc1, layer_index), seq_count)
        units = project_units(hidden, w_fc1, layer_index, arriving)
        heads, units = lax.optimization_barrier((heads, units))
        query, new_key, new_value = activate(heads, tables, width_local)
        units = to_distances(units)
        parts = attend(
            visits, query, swap_cores(query, seq_count), new_key, new_value,
            k_cache, v_cache, layer_index, new_tokens, groups,
        )
        parts, *units = lax.optimization_barrier((parts, *units))
        parts = lax.all_to_all(parts, "seq", 0, 0)
        arriving, half = (
            update(parts, units, start, b_fc1, w_out, w_fc2, layer_index, other, tp_count)
            for other in (True, False)
        )
        parts = to_distances(split(half, swap_cores(arriving, seq_count)))
        start = None
        if layer_index < LAYERS - 1:
            parts = share_rows(parts, tp_count)
            parts = [parts[0]] + [over_tp(parts[k], k) for k in range(1, tp_count)]
    last = last_parts(parts, state, tp_count)
    last = from_tp(last)
    last = to_distances([last_rows(last)] * CHIPS)
    return restore(backs, last, [swap_cores(part, seq_count) for part in last], new_tokens)


def solution(mesh):
    in_specs = (
        P(),
        P(("seq", "tp"), None),
        P(),
        P(),
        P(),
        P("seq", None),
        P(None, "seq", "tp"),
        P(None, "seq", "tp"),
        P(),
        P(),
        P(None, "seq", None, "tp"),
        P(None, "seq", "tp"),
        P(None, "tp"),
        P(None, ("tp", "seq"), None),
        P(None, ("tp", "seq"), None),
    )
    out_specs = P()
    seq_count, tp_count = mesh.shape["seq"], mesh.shape["tp"]
    fits = tp_count == 4 and seq_count == HEADS // tp_count and seq_count == 2 * CHIPS
    return jax.shard_map(
        per_device if fits else per_device_any, mesh=mesh, in_specs=in_specs, out_specs=out_specs, check_vma=False
    )
```

```python
import functools
import math

import jax
import jax.numpy as jnp
from jax import lax
from jax.experimental import pallas as pl
from jax.experimental.pallas import tpu as pltpu
from jax.sharding import PartitionSpec as P

HEADS = 32
HEAD_DIM = 64
ROT = 32
LAYERS = 2
BLOCK = 128
SPAN = 512
CHIPS = 4
LANES = 128


very_negative = -1e30


def layer_norm(values, gain_row, bias_row):
    average = jnp.mean(values, axis=-1, keepdims=True)
    centred = values - average
    variance = jnp.mean(centred * centred, axis=-1, keepdims=True)
    return centred * lax.rsqrt(variance + 1e-05) * gain_row + bias_row


def rotary(values, positions):
    half_width = ROT // 2
    frequency = jnp.exp(
        jnp.arange(half_width, dtype=jnp.float32) * (-2.0 * math.log(10000.0) / ROT)
    )
    angles = positions.astype(jnp.float32)[:, None] * frequency[None, :]
    cosine = jnp.cos(angles)[:, None, :]
    sine_part = jnp.sin(angles)[:, None, :]
    low_half = values[..., :half_width]
    high_half = values[..., half_width:ROT]
    return jnp.concatenate(
        [
            low_half * cosine - high_half * sine_part,
            high_half * cosine + low_half * sine_part,
            values[..., ROT:],
        ],
        axis=-1,
    )


def combine_parts(left_part, right_part):
    max_left, sum_left, out_left = left_part
    max_right, sum_right, out_right = right_part
    top_value = jnp.maximum(max_left, max_right)
    scale_left = jnp.exp(max_left - top_value)
    scale_right = jnp.exp(max_right - top_value)
    return (
        top_value,
        sum_left * scale_left + sum_right * scale_right,
        out_left * scale_left[..., None] + out_right * scale_right[..., None],
    )


def full_total(values):
    return lax.psum(values, ("seq", "tp"))


def per_device_any(
    token_ids,
    embedding,
    group_of,
    prefix_len,
    tail_len,
    block_map,
    k_cache,
    v_cache,
    ln_gain,
    ln_bias,
    w_qkv,
    w_fc1,
    b_fc1,
    w_out,
    w_fc2,
):
    tp_count = lax.axis_size("tp")
    seq_index = lax.axis_index("seq")
    tp_index = lax.axis_index("tp")
    requests = token_ids.shape[0]
    new_tokens = token_ids.shape[1]
    groups = prefix_len.shape[0]
    heads_local = HEADS // tp_count
    width_local = heads_local * HEAD_DIM
    score_scale = 1.0 / math.sqrt(HEAD_DIM)
    vocab_rows = embedding.shape[0]
    first_row = (seq_index * tp_count + tp_index) * vocab_rows
    local_ids = token_ids.reshape(-1) - first_row
    inside = (local_ids >= 0) & (local_ids < vocab_rows)
    picked = jnp.take(embedding, jnp.clip(local_ids, 0, vocab_rows - 1), axis=0).astype(jnp.float32)
    picked = jnp.where(inside[:, None], picked, 0.0)
    start_states = full_total(picked).reshape(requests, new_tokens, -1)
    group_hit = group_of[:, None] == jnp.arange(groups, dtype=jnp.int32)[None, :]
    shared_len = jnp.sum(jnp.where(group_hit, prefix_len[None, :], 0), axis=1)
    base_positions = shared_len + tail_len
    seg_len = jnp.concatenate([prefix_len, tail_len])
    seg_count = seg_len.shape[0]
    blocks_local = block_map.shape[0]
    seg_blk = block_map[:, 0]
    rank_blk = block_map[:, 1]
    seg_hit = seg_blk[:, None] == jnp.arange(seg_count, dtype=jnp.int32)[None, :]
    len_blk = jnp.sum(jnp.where(seg_hit, seg_len[None, :], 0), axis=1)
    slot_positions = rank_blk[:, None] * BLOCK + jnp.arange(BLOCK, dtype=jnp.int32)[None, :]
    live_slot = ((seg_blk[:, None] >= 0) & (slot_positions < len_blk[:, None])).reshape(-1)
    seg_slot = jnp.broadcast_to(seg_blk[:, None], (blocks_local, BLOCK)).reshape(-1)
    own_tail = seg_slot[None, :] == (groups + jnp.arange(requests, dtype=jnp.int32))[:, None]
    own_prompt = seg_slot[None, :] == group_of[:, None]
    allowed = (own_tail | own_prompt) & live_slot[None, :]
    step_count = allowed.shape[1] // SPAN
    allowed_steps = allowed.reshape(requests, step_count, SPAN).transpose(1, 0, 2)
    rows_local = w_qkv.shape[1]
    unit_count = w_fc2.shape[1]
    sub_width = w_out.shape[1]
    token_index = jnp.arange(new_tokens, dtype=jnp.int32)
    new_keys = [
        jnp.zeros((requests, new_tokens, heads_local, HEAD_DIM), jnp.bfloat16)
        for layer_index in range(LAYERS)
    ]
    new_values = [
        jnp.zeros((requests, new_tokens, heads_local, HEAD_DIM), jnp.bfloat16)
        for layer_index in range(LAYERS)
    ]
    results = []
    for token_step in range(new_tokens):
        hidden_state = start_states[:, token_step]
        positions = base_positions + token_step
        for layer_index in range(LAYERS):
            normed = layer_norm(hidden_state, ln_gain[layer_index], ln_bias[layer_index]).astype(
                jnp.bfloat16
            )
            my_rows = lax.dynamic_slice_in_dim(normed, seq_index * rows_local, rows_local, 1)
            part_proj = jnp.dot(
                my_rows,
                w_qkv[layer_index].reshape(rows_local, -1),
                preferred_element_type=jnp.float32,
            )
            part_fc1 = jnp.dot(my_rows, w_fc1[layer_index], preferred_element_type=jnp.float32)
            attention_proj, fc1_all = lax.psum((part_proj, part_fc1), "seq")
            pre_act = lax.dynamic_slice_in_dim(fc1_all, seq_index * unit_count, unit_count, 1)
            pre_act = (
                pre_act
                + lax.dynamic_slice_in_dim(
                    b_fc1[layer_index], seq_index * unit_count, unit_count, 0
                )[None, :]
            )
            activated = jax.nn.gelu(pre_act, approximate=True).astype(jnp.bfloat16)
            attention_proj = attention_proj.reshape(requests, 3, heads_local, HEAD_DIM)
            queries = rotary(attention_proj[:, 0], positions).astype(jnp.bfloat16)
            key_rows = rotary(attention_proj[:, 1], positions).astype(jnp.bfloat16)
            value_rows = attention_proj[:, 2].astype(jnp.bfloat16)
            new_keys[layer_index] = new_keys[layer_index].at[:, token_step].set(key_rows)
            new_values[layer_index] = new_values[layer_index].at[:, token_step].set(value_rows)
            key_steps = k_cache[layer_index].reshape(step_count, SPAN, heads_local, HEAD_DIM)
            value_steps = v_cache[layer_index].reshape(step_count, SPAN, heads_local, HEAD_DIM)

            def cache_step(carry, inputs):
                run_max, run_sum, run_out = carry
                key_block, value_block, allow_block = inputs
                scores = (
                    jnp.einsum(
                        "rhd,shd->hrs", queries, key_block, preferred_element_type=jnp.float32
                    )
                    * score_scale
                )
                scores = jnp.where(allow_block[None], scores, very_negative)
                next_max = jnp.maximum(run_max, jnp.max(scores, axis=2))
                weights = jnp.where(allow_block[None], jnp.exp(scores - next_max[..., None]), 0.0)
                shrink = jnp.exp(run_max - next_max)
                next_sum = run_sum * shrink + jnp.sum(weights, axis=2)
                next_out = run_out * shrink[..., None] + jnp.einsum(
                    "hrs,shd->hrd",
                    weights.astype(jnp.bfloat16),
                    value_block,
                    preferred_element_type=jnp.float32,
                )
                return ((next_max, next_sum, next_out), None)

            start_carry = (
                jnp.full((heads_local, requests), very_negative, jnp.float32),
                jnp.zeros((heads_local, requests), jnp.float32),
                jnp.zeros((heads_local, requests, HEAD_DIM), jnp.float32),
            )
            (part_max, part_sum, part_out), unused = lax.scan(
                cache_step, start_carry, (key_steps, value_steps, allowed_steps)
            )
            cache_max = lax.pmax(part_max, "seq")
            factor = jnp.exp(part_max - cache_max)
            cache_sum, cache_out = (
                lax.psum((part_sum * factor).astype(jnp.bfloat16), "seq").astype(jnp.float32),
                lax.psum((part_out * factor[..., None]).astype(jnp.bfloat16), "seq").astype(
                    jnp.float32
                ),
            )
            visible = (token_index <= token_step)[None, None, :]
            fresh_scores = (
                jnp.einsum(
                    "rhd,rjhd->hrj",
                    queries,
                    new_keys[layer_index],
                    preferred_element_type=jnp.float32,
                )
                * score_scale
            )
            fresh_scores = jnp.where(visible, fresh_scores, very_negative)
            fresh_max = jnp.max(fresh_scores, axis=2)
            fresh_weights = jnp.where(visible, jnp.exp(fresh_scores - fresh_max[..., None]), 0.0)
            fresh_sum = jnp.sum(fresh_weights, axis=2)
            fresh_out = jnp.einsum(
                "hrj,rjhd->hrd",
                fresh_weights.astype(jnp.bfloat16),
                new_values[layer_index],
                preferred_element_type=jnp.float32,
            )
            joint_max, denom_total, weighted = combine_parts(
                (cache_max, cache_sum, cache_out), (fresh_max, fresh_sum, fresh_out)
            )
            attended = (weighted / denom_total[..., None]).astype(jnp.bfloat16)
            attended = attended.transpose(1, 0, 2).reshape(requests, width_local)
            my_cols = lax.dynamic_slice_in_dim(attended, seq_index * sub_width, sub_width, 1)
            update = jnp.dot(my_cols, w_out[layer_index], preferred_element_type=jnp.float32)
            update = update + jnp.dot(
                activated, w_fc2[layer_index], preferred_element_type=jnp.float32
            )
            hidden_state = hidden_state + full_total(update)
        results.append(hidden_state)
    stacked = jnp.stack(results, axis=1)
    return stacked


def swap_cores(values, seq_count):
    return lax.ppermute(values, "seq", [(i, i ^ 1) for i in range(seq_count)])


def in_hbm(values):
    return pltpu.with_memory_space_constraint(values, pltpu.HBM)


def compiler_params(megabytes=32):
    return pltpu.CompilerParams(vmem_limit_bytes=megabytes * 2**20)


def whole(memory_space=pltpu.VMEM):
    return pl.BlockSpec(memory_space=memory_space)


def layer_block(layer_index, shape):
    return pl.BlockSpec((1,) + shape, lambda step: (layer_index,) + (0,) * len(shape))


def same_block(shape):
    return pl.BlockSpec(shape, lambda step: (0,) * len(shape))


def order_kernel(new_tokens, group_ref, prefix_ref, tail_ref, map_ref, rank_ref, position_ref, visit_ref, count_ref):
    requests = group_ref.shape[0]
    groups = prefix_ref.shape[0]
    per_group = requests // groups
    blocks = map_ref.shape[1]
    for group in range(groups):
        count_ref[group] = 0

    def place(request, unused):
        group = group_ref[request]
        seat = count_ref[group]
        count_ref[group] = seat + 1
        rank = group * per_group + seat
        rank_ref[request] = rank
        start = prefix_ref[group] + tail_ref[request]
        for token in range(new_tokens):
            position_ref[rank * new_tokens + token] = start + token
        return unused

    lax.fori_loop(0, requests, place, 0)

    def look(block, unused):
        segment, depth = map_ref[0, block], map_ref[1, block]
        is_tail = segment >= groups
        request = jnp.clip(segment - groups, 0, requests - 1)
        prompt = jnp.clip(segment, 0, groups - 1)
        seat = rank_ref[request]
        first = jnp.where(is_tail, (seat % per_group) * new_tokens, 0)
        length = jnp.where(is_tail, tail_ref[request], prefix_ref[prompt])
        visit_ref[block] = jnp.where(is_tail, seat // per_group, prompt)
        visit_ref[blocks + block] = jnp.where(segment < 0, 0, length - depth * BLOCK)
        visit_ref[2 * blocks + block] = first
        visit_ref[3 * blocks + block] = jnp.where(is_tail, first + new_tokens, per_group * new_tokens)
        return unused

    lax.fori_loop(0, blocks, look, 0)


def order_requests(group_of, prefix_len, tail_len, block_map, new_tokens):
    requests = group_of.shape[0]
    smem = whole(pltpu.SMEM)
    return pl.pallas_call(
        functools.partial(order_kernel, new_tokens),
        out_shape=(
            jax.ShapeDtypeStruct((requests,), jnp.int32),
            jax.ShapeDtypeStruct((requests * new_tokens,), jnp.int32),
            jax.ShapeDtypeStruct((4 * block_map.shape[0],), jnp.int32),
        ),
        in_specs=[smem] * 4,
        out_specs=(smem, smem, smem),
        scratch_shapes=[pltpu.SMEM((prefix_len.shape[0],), jnp.int32)],
        name="order_requests",
    )(group_of, prefix_len, tail_len, block_map.T)


def thirds(values):
    high = values.astype(jnp.bfloat16).astype(jnp.float32)
    middle = (values - high).astype(jnp.bfloat16).astype(jnp.float32)
    return high, middle, values - high - middle


def row_block(rows):
    width = rows[0].shape[1]
    line = lax.broadcasted_iota(jnp.int32, (8, width), 0)
    block = jnp.zeros((8, width), jnp.float32)
    for index, row in enumerate(rows):
        block = jnp.where(line == index, row, block)
    return block


def column_to_row(column):
    return jnp.broadcast_to(column, (column.shape[0], LANES)).T[0:1]


def row_to_column(row):
    return jnp.broadcast_to(row, (LANES, row.shape[1])).T


def ranks(group_ref):
    requests = group_ref.shape[1]
    across = lax.broadcasted_iota(jnp.int32, (requests, requests), 1)
    down = lax.broadcasted_iota(jnp.int32, (requests, requests), 0)
    group_row = group_ref[0:1, :]
    group_column = jnp.sum(jnp.where(across == down, group_row, 0), axis=1, keepdims=True)
    ahead = (group_column < group_row) | ((group_column == group_row) & (down < across))
    return jnp.sum(jnp.where(ahead, 1, 0), axis=0, keepdims=True)


def row_sums(lines):
    block = row_block([part for line in lines for part in thirds(line)])
    return jnp.concatenate([block, jnp.zeros_like(block)], axis=0).astype(jnp.bfloat16)


def from_row_sums(block):
    block = block.astype(jnp.float32)
    line = lax.broadcasted_iota(jnp.int32, block.shape, 0)
    return [
        jnp.sum(jnp.where((line >= start) & (line < start + 3), block, 0.0), axis=0, keepdims=True)
        for start in (0, 3)
    ]


def embed_kernel(
    token_ref, group_ref, table_hbm, near_ref, far_ref, own_ref,
    table_ref, hot_ref, row_ref, semaphores,
):
    core = lax.axis_index("seq") % 2
    first = (lax.axis_index("seq") * lax.axis_size("tp") + lax.axis_index("tp")) * table_ref.shape[1]
    new_tokens, requests = token_ref.shape
    rows, unit = near_ref.shape[1:]
    copies = []
    for chip in range(CHIPS):
        copies.append(
            pltpu.make_async_copy(
                table_hbm.at[:, pl.ds(chip * 2 * unit, 2 * unit)], table_ref.at[chip], semaphores.at[chip]
            )
        )
        copies[-1].start()
    rank_row = ranks(group_ref)
    line = lax.broadcasted_iota(jnp.int32, (rows, requests), 0)
    ids = jnp.zeros((rows, requests), jnp.int32)
    for token in range(new_tokens):
        match = (rank_row == line // new_tokens) & (line % new_tokens == token)
        ids = jnp.where(match, token_ref[token : token + 1, :], ids)
    ids = jnp.sum(ids, axis=1, keepdims=True) - first
    entry = lax.broadcasted_iota(jnp.int32, hot_ref.shape, 1)
    hot_ref[...] = jnp.where(entry == ids, 1.0, 0.0).astype(jnp.bfloat16)
    total = jnp.zeros((rows, LANES), jnp.float32)
    for chip, copy in enumerate(copies):
        copy.wait()
        chosen = jnp.dot(hot_ref[...], table_ref[chip], preferred_element_type=jnp.float32)
        for start in range(0, 2 * unit, LANES):
            total = total + chosen[:, start : start + LANES]
        chosen = chosen.astype(jnp.bfloat16)
        row_ref[:, chip * 2 * unit : (chip + 1) * 2 * unit] = chosen
        left, right = chosen[:, :unit], chosen[:, unit:]
        near_ref[chip] = jnp.where(core == 0, left, right)
        far_ref[chip * rows : (chip + 1) * rows] = jnp.where(core == 0, right, left)
    features = row_ref.shape[1]
    mean = jnp.sum(total, axis=1, keepdims=True) * (1.0 / features)
    squares = jnp.zeros((rows, LANES), jnp.float32)
    for start in range(0, features, LANES):
        centred = row_ref[:, start : start + LANES].astype(jnp.float32) - mean
        squares = squares + centred * centred
    variance = jnp.sum(squares, axis=1, keepdims=True) * (1.0 / features)
    held = (ids >= 0) & (ids < hot_ref.shape[1])
    scale = jnp.where(held, lax.rsqrt(variance + 1e-05), 0.0)
    mean, scale = column_to_row(mean), column_to_row(scale)
    own_ref[...] = row_block([mean, scale])
    far_ref[CHIPS * rows :] = row_sums([mean, scale])


def embed(token_ids, group_of, embedding, unit):
    rows = token_ids.shape[0] * token_ids.shape[1]
    return pl.pallas_call(
        embed_kernel,
        out_shape=(
            jax.ShapeDtypeStruct((CHIPS, rows, unit), jnp.bfloat16),
            pltpu.HBM((CHIPS * rows + 16, unit), jnp.bfloat16),
            jax.ShapeDtypeStruct((8, rows), jnp.float32),
        ),
        in_specs=[whole(), whole(), whole(pltpu.HBM)],
        out_specs=(whole(),) * 3,
        scratch_shapes=[
            pltpu.VMEM((CHIPS, embedding.shape[0], 2 * unit), jnp.bfloat16),
            pltpu.VMEM((rows, embedding.shape[0]), jnp.bfloat16),
            pltpu.VMEM((rows, embedding.shape[1]), jnp.bfloat16),
            pltpu.SemaphoreType.DMA((CHIPS,)),
        ],
        compiler_params=compiler_params(24),
        name="embed",
    )(in_hbm(token_ids.T), in_hbm(group_of[None, :]), in_hbm(embedding))


def join_kernel(near_ref, far_ref, own_ref, out_ref, *refs):
    *out_hbms, leave_ref, semaphores = refs
    here = lax.axis_index("seq") // 2
    rows = near_ref.shape[1]
    mean, scale = from_row_sums(far_ref[CHIPS * rows :])
    lines = row_sums([mean + own_ref[0:1, :], scale + own_ref[1:2, :]])
    leaving = []
    for distance in reversed(range(CHIPS)):
        chip = here ^ distance
        far = far_ref[pl.ds(pl.multiple_of(chip * rows, rows), rows), :].astype(jnp.float32)
        joined = (near_ref[chip].astype(jnp.float32) + far).astype(jnp.bfloat16)
        if distance:
            leave_ref[distance - 1, :rows] = joined
            leave_ref[distance - 1, rows:] = lines
            leaving.append(
                pltpu.make_async_copy(
                    leave_ref.at[distance - 1], out_hbms[distance - 1], semaphores.at[distance - 1]
                )
            )
            leaving[-1].start()
        else:
            out_ref[:rows] = joined
            out_ref[rows:] = lines
    for copy in leaving:
        copy.wait()


def join(near, far, own):
    chips, rows, unit = near.shape
    one = (rows + 16, unit)
    return pl.pallas_call(
        join_kernel,
        out_shape=(jax.ShapeDtypeStruct(one, jnp.bfloat16),) + (pltpu.HBM(one, jnp.bfloat16),) * (chips - 1),
        in_specs=[whole()] * 3,
        out_specs=(whole(),) + (whole(pltpu.HBM),) * (chips - 1),
        scratch_shapes=[pltpu.VMEM((chips - 1,) + one, jnp.bfloat16), pltpu.SemaphoreType.DMA((chips - 1,))],
        compiler_params=compiler_params(16),
        name="join",
    )(near, far, own)


def gather_kernel(a_ref, b_ref, c_ref, d_ref, out_hbm, out_ref, semaphore):
    rows = out_ref.shape[0] - 16
    near = a_ref[...].astype(jnp.float32) + b_ref[...].astype(jnp.float32)
    far = c_ref[...].astype(jnp.float32) + d_ref[...].astype(jnp.float32)
    total = near + far
    out_ref[:rows] = total[:rows].astype(jnp.bfloat16)
    out_ref[rows:] = row_sums(from_row_sums(total[rows:]))
    copy = pltpu.make_async_copy(out_ref, out_hbm, semaphore)
    copy.start()
    copy.wait()


def gather(parts):
    return pl.pallas_call(
        gather_kernel,
        out_shape=pltpu.HBM(parts[0].shape, jnp.bfloat16),
        in_specs=[whole()] * 4,
        out_specs=whole(pltpu.HBM),
        scratch_shapes=[pltpu.VMEM(parts[0].shape, jnp.bfloat16), pltpu.SemaphoreType.DMA],
        compiler_params=compiler_params(16),
        name="gather",
    )(*parts)


def first_kernel(a_hbm, b_ref, c_ref, d_ref, gain_ref, bias_ref, start_ref, hidden_ref, a_ref, semaphore):
    rows, unit = hidden_ref.shape
    copy = pltpu.make_async_copy(a_hbm, a_ref, semaphore)
    copy.start()
    far = c_ref[...].astype(jnp.float32) + d_ref[...].astype(jnp.float32)
    copy.wait()
    total = (a_ref[...].astype(jnp.float32) + b_ref[...].astype(jnp.float32)) + far
    mean, scale = (row_to_column(line) for line in from_row_sums(total[rows:]))
    columns = pl.ds(pl.multiple_of(lax.axis_index("seq") * unit, unit), unit)
    gain, bias = gain_ref[0:1, columns], bias_ref[0:1, columns]
    for start in range(0, unit, LANES):
        span = slice(start, start + LANES)
        state = total[:rows, span]
        start_ref[:, span] = state.astype(jnp.bfloat16)
        hidden_ref[:, span] = ((state - mean) * scale * gain[:, span] + bias[:, span]).astype(jnp.bfloat16)


def first_hidden(parts, ln_gain, ln_bias):
    one = jax.ShapeDtypeStruct((parts[0].shape[0] - 16, parts[0].shape[1]), jnp.bfloat16)
    return pl.pallas_call(
        first_kernel,
        out_shape=(one, one),
        in_specs=[whole(pltpu.HBM)] + [whole()] * 5,
        out_specs=(whole(), whole()),
        scratch_shapes=[pltpu.VMEM(parts[0].shape, jnp.bfloat16), pltpu.SemaphoreType.DMA],
        compiler_params=compiler_params(16),
        name="first_hidden",
    )(in_hbm(parts[0]), *parts[1:], ln_gain, ln_bias)


def norm_kernel(layer_index, tp_count, *refs):
    *part_refs, gain_ref, bias_ref, next_ref, cut_ref = refs
    state = functools.reduce(jnp.add, [ref[...].astype(jnp.float32) for ref in part_refs])
    next_ref[...] = state
    average = jnp.mean(state, axis=-1, keepdims=True)
    centred = state - average
    variance = jnp.mean(centred * centred, axis=-1, keepdims=True)
    gain = gain_ref[layer_index : layer_index + 1, :]
    bias = bias_ref[layer_index : layer_index + 1, :]
    normed = (centred * lax.rsqrt(variance + 1e-05) * gain + bias).astype(jnp.bfloat16)
    width = cut_ref.shape[2]
    for place in range(cut_ref.shape[0]):
        start = (place // tp_count) * width
        cut_ref[place] = normed[:, start : start + width]


def norm_rows(parts, state, ln_gain, ln_bias, layer_index, devices, tp_count):
    rows, width = parts[0].shape
    cut = width // (devices // tp_count)
    operands = list(parts) + ([] if state is None else [state]) + [ln_gain, ln_bias]
    return pl.pallas_call(
        functools.partial(norm_kernel, layer_index, tp_count),
        out_shape=(
            pltpu.HBM((rows, width), jnp.float32),
            jax.ShapeDtypeStruct((devices, rows, cut), jnp.bfloat16),
        ),
        in_specs=[whole()] * len(operands),
        out_specs=(whole(), whole()),
        compiler_params=compiler_params(16),
        name="norm_rows",
    )(*operands)


def share_kernel(a_ref, b_ref, c_ref, d_ref, *out_refs):
    total = functools.reduce(jnp.add, [ref[...].astype(jnp.float32) for ref in (a_ref, b_ref, c_ref, d_ref)])
    mine = out_refs[0].shape[0]
    for owner in range(len(out_refs)):
        for distance, ref in enumerate(out_refs):
            @pl.when(lax.axis_index("tp") == owner ^ distance)
            def put(ref=ref, owner=owner):
                ref[...] = total[owner * mine : (owner + 1) * mine].astype(ref.dtype)


def share_rows(parts, tp_count):
    rows, width = parts[0].shape
    one = (rows // tp_count, width)
    return pl.pallas_call(
        share_kernel,
        out_shape=(jax.ShapeDtypeStruct(one, jnp.float32),)
        + (jax.ShapeDtypeStruct(one, jnp.bfloat16),) * (tp_count - 1),
        in_specs=[whole()] * 4,
        out_specs=(whole(),) * tp_count,
        compiler_params=compiler_params(16),
        name="share_rows",
    )(*parts)


def last_parts_kernel(tp_count, a_ref, b_ref, c_ref, d_ref, state_ref, out_ref):
    near = a_ref[...].astype(jnp.float32) + b_ref[...].astype(jnp.float32)
    far = c_ref[...].astype(jnp.float32) + d_ref[...].astype(jnp.float32)
    total = near + far
    mine = state_ref.shape[0]
    owner = lax.axis_index("tp")
    for place in range(tp_count):
        rows = slice(place * mine, (place + 1) * mine)
        total_rows = total[rows] + jnp.where(owner == place, 1.0, 0.0) * state_ref[...]
        out_ref[rows] = total_rows.astype(jnp.bfloat16)


def last_parts(parts, state, tp_count):
    return pl.pallas_call(
        functools.partial(last_parts_kernel, tp_count),
        out_shape=jax.ShapeDtypeStruct(parts[0].shape, jnp.bfloat16),
        in_specs=[whole()] * 5,
        out_specs=whole(),
        compiler_params=compiler_params(16),
        name="last_parts",
    )(*parts, state)


def split_kernel(half_ref, arrived_ref, out_ref, *refs):
    *out_hbms, leave_ref, semaphores = refs
    share = out_ref.shape[0]
    leaving = []
    for distance in reversed(range(CHIPS)):
        rows = slice(distance * share, (distance + 1) * share)
        joined = half_ref[rows] + arrived_ref[rows].astype(jnp.float32)
        if distance:
            leave_ref[distance - 1] = joined.astype(jnp.bfloat16)
            leaving.append(
                pltpu.make_async_copy(
                    leave_ref.at[distance - 1], out_hbms[distance - 1], semaphores.at[distance - 1]
                )
            )
            leaving[-1].start()
        else:
            out_ref[...] = joined
    for copy in leaving:
        copy.wait()


def split(half, arrived):
    one = (half.shape[0] // CHIPS, half.shape[1])
    return pl.pallas_call(
        split_kernel,
        out_shape=(jax.ShapeDtypeStruct(one, jnp.float32),) + (pltpu.HBM(one, jnp.bfloat16),) * (CHIPS - 1),
        in_specs=[whole()] * 2,
        out_specs=(whole(),) + (whole(pltpu.HBM),) * (CHIPS - 1),
        scratch_shapes=[pltpu.VMEM((CHIPS - 1,) + one, jnp.bfloat16), pltpu.SemaphoreType.DMA((CHIPS - 1,))],
        compiler_params=compiler_params(16),
        name="split",
    )(half, arrived)


def last_kernel(a_ref, b_ref, c_ref, d_ref, out_ref):
    near = a_ref[...].astype(jnp.float32) + b_ref[...].astype(jnp.float32)
    far = c_ref[...].astype(jnp.float32) + d_ref[...].astype(jnp.float32)
    out_ref[...] = (near + far).astype(jnp.bfloat16)


def last_rows(parts):
    return pl.pallas_call(
        last_kernel,
        out_shape=jax.ShapeDtypeStruct(parts[0].shape, jnp.bfloat16),
        in_specs=[whole()] * 4,
        out_specs=whole(),
        compiler_params=compiler_params(16),
        name="last_rows",
    )(*parts)


def back_kernel(new_tokens, group_ref, near_ref, far_ref):
    rows, half = near_ref.shape
    requests = group_ref.shape[1]
    rank_row = ranks(group_ref)
    line = lax.broadcasted_iota(jnp.int32, (rows, requests), 0)
    column = lax.broadcasted_iota(jnp.int32, (rows, requests), 1)
    wanted = jnp.sum(jnp.where(column == line // new_tokens, rank_row, 0), axis=1, keepdims=True)
    line = lax.broadcasted_iota(jnp.int32, near_ref.shape, 0)
    entry = lax.broadcasted_iota(jnp.int32, near_ref.shape, 1)
    share = half // CHIPS
    here = lax.axis_index("seq") // 2
    for ref, other in ((near_ref, False), (far_ref, True)):
        held = (((entry // share) ^ here) * 2 + core_parity(other)) * share + entry % share
        back = held == wanted * new_tokens + line % new_tokens
        ref[...] = jnp.where(back, 1.0, 0.0).astype(jnp.bfloat16)


def back_rows(group_of, new_tokens):
    rows = group_of.shape[0] * new_tokens
    one = jax.ShapeDtypeStruct((rows, rows // 2), jnp.bfloat16)
    return pl.pallas_call(
        functools.partial(back_kernel, new_tokens),
        out_shape=(one, one),
        in_specs=[whole()],
        out_specs=(whole(), whole()),
        compiler_params=compiler_params(16),
        name="back_rows",
    )(group_of[None, :])


def restore_kernel(near_back_ref, far_back_ref, *refs):
    *row_refs, out_hbm, out_ref, semaphores = refs
    requests, new_tokens, width = out_ref.shape
    step = width // semaphores.shape[0]
    leaving = []
    for index, start in enumerate(range(0, width, step)):
        span = slice(start, start + step)
        near, far = (
            jnp.concatenate([ref[:, span] for ref in half], axis=0)
            for half in (row_refs[:CHIPS], row_refs[CHIPS:])
        )
        rows = jnp.dot(near_back_ref[...], near, preferred_element_type=jnp.float32) + jnp.dot(
            far_back_ref[...], far, preferred_element_type=jnp.float32
        )
        out_ref[:, :, span] = rows.reshape(requests, new_tokens, step)
        span = pl.ds(start, step)
        leaving.append(
            pltpu.make_async_copy(out_ref.at[:, :, span], out_hbm.at[:, :, span], semaphores.at[index])
        )
        leaving[-1].start()
    for copy in leaving:
        copy.wait()


def restore(backs, near, far, new_tokens):
    rows = backs[0].shape[0]
    shape = (rows // new_tokens, new_tokens, near[0].shape[1])
    return pl.pallas_call(
        restore_kernel,
        out_shape=pltpu.HBM(shape, jnp.float32),
        in_specs=[whole()] * (2 + 2 * CHIPS),
        out_specs=whole(pltpu.HBM),
        scratch_shapes=[pltpu.VMEM(shape, jnp.float32), pltpu.SemaphoreType.DMA((4,))],
        compiler_params=compiler_params(24),
        name="restore",
    )(*backs, *near, *far)


def core_parity(other):
    return 1 - lax.axis_index("seq") % 2 if other else lax.axis_index("seq") % 2


def heads_kernel(joins, hidden_ref, qkv_ref, *refs):
    if joins:
        arrived_ref, near_ref, *out_hbms, out_ref, semaphores = refs
    else:
        out_ref = refs[0]
    parity = core_parity(not joins)
    here = lax.axis_index("seq") // 2
    rows, unit = hidden_ref.shape
    width = qkv_ref.shape[1] // 3
    share = rows // CHIPS // 2
    half = rows // 2
    pieces = width // unit
    tall = 2 * pieces * share

    def joined(values, start):
        if joins:
            values = values + arrived_ref[start : start + values.shape[0]].astype(jnp.float32)
        return values.astype(jnp.bfloat16)

    def picked(chips):
        return jnp.concatenate(
            [
                hidden_ref[pl.ds(pl.multiple_of((2 * chip + parity) * share, share), share), :]
                for chip in chips
            ],
            axis=0,
        )

    queries = jnp.dot(picked(range(CHIPS)), qkv_ref[:, :width], preferred_element_type=jnp.float32)
    for piece in range(pieces):
        start = piece * half
        query = joined(queries[:, piece * unit : (piece + 1) * unit], start)
        if joins:
            for distance in range(CHIPS):
                out_ref[distance, tall + start : tall + start + half] = query
        else:
            out_ref[start : start + half] = query
    others = jnp.dot(
        picked([here ^ distance for distance in range(CHIPS)]), qkv_ref[:, width:], preferred_element_type=jnp.float32
    )
    base = pieces * half
    leaving = []
    for distance in reversed(range(CHIPS)):
        for piece in range(2 * pieces):
            start = base + (distance * 2 * pieces + piece) * share
            value = joined(
                others[distance * share : (distance + 1) * share, piece * unit : (piece + 1) * unit], start
            )
            if joins:
                out_ref[distance, piece * share : (piece + 1) * share] = value
            else:
                out_ref[start : start + share] = value
        if joins and distance:
            copy = pltpu.make_async_copy(
                out_ref.at[distance], out_hbms[distance - 1], semaphores.at[distance - 1]
            )
            copy.start()
            leaving.append(copy)
    if joins:
        near_ref[...] = out_ref[0]
    for copy in leaving:
        copy.wait()


def project_heads(hidden, weights_qkv, unit, arrived=None):
    rows = hidden.shape[0]
    pieces = weights_qkv.shape[1] // 3 // unit
    tall = 2 * pieces * (rows // CHIPS // 2)
    common = pieces * (rows // 2)
    extra = [] if arrived is None else [arrived]
    out_shape = jax.ShapeDtypeStruct((common + CHIPS * tall, unit), jnp.bfloat16)
    out_specs = whole()
    scratch = []
    if arrived is not None:
        one = (tall + common, unit)
        out_shape = (jax.ShapeDtypeStruct(one, jnp.bfloat16),) + (pltpu.HBM(one, jnp.bfloat16),) * (CHIPS - 1)
        out_specs = (whole(),) + (whole(pltpu.HBM),) * (CHIPS - 1)
        scratch = [pltpu.VMEM((CHIPS,) + one, jnp.bfloat16), pltpu.SemaphoreType.DMA((CHIPS - 1,))]
    return pl.pallas_call(
        functools.partial(heads_kernel, arrived is not None),
        out_shape=out_shape,
        in_specs=[whole()] * (2 + len(extra)),
        out_specs=out_specs,
        scratch_shapes=scratch,
        compiler_params=compiler_params(24),
        name="project_heads",
    )(hidden, weights_qkv, *extra)


def units_kernel(joins, hidden_ref, fc1_ref, *refs):
    arrived_ref, out_refs = (refs[0], refs[1:]) if joins else (None, refs)
    parity = core_parity(not joins)
    here = lax.axis_index("seq") // 2
    unit = fc1_ref.shape[2] // CHIPS // 2
    hidden = hidden_ref[...]
    for distance in range(CHIPS):
        target = 2 * (here ^ distance) + parity
        columns = pl.ds(pl.multiple_of(target * unit, unit), unit)
        pre = jnp.dot(hidden, fc1_ref[0, :, columns], preferred_element_type=jnp.float32)
        if joins:
            pre = pre + arrived_ref[distance].astype(jnp.float32)
            out_refs[distance][...] = pre.astype(jnp.bfloat16)
        else:
            out_refs[0][distance] = pre.astype(jnp.bfloat16)


def project_units(hidden, w_fc1, layer_index, arrived=None):
    rows = hidden.shape[0]
    unit = w_fc1.shape[2] // CHIPS // 2
    extra = [] if arrived is None else [arrived]
    if arrived is None:
        out_shape = jax.ShapeDtypeStruct((CHIPS, rows, unit), jnp.bfloat16)
    else:
        out_shape = (jax.ShapeDtypeStruct((rows, unit), jnp.bfloat16),) * CHIPS
    return pl.pallas_call(
        functools.partial(units_kernel, arrived is not None),
        grid=(1,),
        out_shape=out_shape,
        in_specs=[same_block(hidden.shape), layer_block(layer_index, w_fc1.shape[1:])]
        + [same_block(values.shape) for values in extra],
        out_specs=jax.tree.map(lambda leaf: same_block(leaf.shape), out_shape),
        compiler_params=compiler_params(24),
        name="project_units",
    )(hidden, w_fc1, *extra)


def activate_kernel(a_ref, b_ref, c_ref, d_ref, table_ref, query_ref, key_ref, value_ref):
    near = a_ref[...].astype(jnp.float32) + b_ref[...].astype(jnp.float32)
    far = c_ref[...].astype(jnp.float32) + d_ref[...].astype(jnp.float32)
    total = near + far
    share, width = key_ref.shape
    half = query_ref.shape[0]
    unit = a_ref.shape[1]
    lanes = table_ref.shape[2]
    pieces = width // unit
    own = pl.ds(pl.multiple_of((lax.axis_index("seq") // 2) * share, share), share)

    def put(target_ref, start, height, span, scale):
        for piece in range(pieces):
            for column in range(0, unit, lanes):
                first = start + piece * height
                values = total[first : first + height, column : column + lanes]
                if span is not None:
                    values = (
                        values * table_ref[0, span]
                        + pltpu.roll(values, lanes - ROT // 2, 1) * table_ref[1, span]
                        + pltpu.roll(values, ROT // 2, 1) * table_ref[2, span]
                    )
                values = values.astype(jnp.bfloat16)
                if scale is not None:
                    values = (values.astype(jnp.float32) * scale).astype(jnp.bfloat16)
                column_out = piece * unit + column
                target_ref[:, column_out : column_out + lanes] = values

    put(key_ref, 0, share, own, None)
    put(value_ref, pieces * share, share, None, None)
    put(query_ref, 2 * pieces * share, half, slice(None), 1.0 / math.sqrt(HEAD_DIM))


def activate(parts, tables, width):
    half = tables.shape[1]
    small = jax.ShapeDtypeStruct((half // CHIPS, width), jnp.bfloat16)
    return pl.pallas_call(
        activate_kernel,
        out_shape=(jax.ShapeDtypeStruct((half, width), jnp.bfloat16), small, small),
        in_specs=[whole()] * 5,
        out_specs=(whole(),) * 3,
        compiler_params=compiler_params(16),
        name="activate",
    )(*parts, tables)


def rotary_tables(positions, width):
    half = ROT // 2
    feature = lax.broadcasted_iota(jnp.int32, (1, width), 1) % HEAD_DIM
    frequency = jnp.exp((feature % half).astype(jnp.float32) * (-2.0 * math.log(10000.0) / ROT))
    angles = positions.astype(jnp.float32)[:, None] * frequency
    cosine, sine = jnp.cos(angles), jnp.sin(angles)
    return jnp.stack(
        [
            jnp.where(feature < ROT, cosine, 1.0),
            jnp.where(feature < half, -sine, 0.0),
            jnp.where((feature >= half) & (feature < ROT), sine, 0.0),
        ]
    )


def attend_kernel(
    layer_index, new_tokens,
    visit_hbm, query_ref, far_query_ref, new_key_ref, new_value_ref,
    key_hbm, value_hbm, out_ref,
    key_ref, value_ref, visit_ref, both_ref, score_ref, top_ref, sum_ref, mix_ref, semaphores, visit_semaphore,
):
    blocks = visit_ref.shape[0] // 4
    groups, tall, lanes = mix_ref.shape
    share = new_key_ref.shape[0]
    heads = tall // share
    chunks = semaphores.shape[1]
    chunk = key_ref.shape[0] // chunks

    def copy(kind, index):
        span = pl.ds(index * chunk, chunk)
        source, target = ((key_hbm, key_ref), (value_hbm, value_ref))[kind]
        return pltpu.make_async_copy(
            source.at[layer_index, span], target.at[span], semaphores.at[kind, index]
        )

    looking = pltpu.make_async_copy(visit_hbm, visit_ref, visit_semaphore)
    looking.start()
    for kind in range(2):
        for index in range(chunks):
            copy(kind, index).start()
    core = lax.axis_index("seq") % 2
    for chip in range(groups // 2):
        span = slice(chip * share, (chip + 1) * share)
        both_ref[2 * chip + core] = query_ref[span]
        both_ref[2 * chip + 1 - core] = far_query_ref[span]
    lane = lax.broadcasted_iota(jnp.int32, (share, lanes), 1)
    row = lax.broadcasted_iota(jnp.int32, (share, lanes), 0)
    top_ref[...] = jnp.full(top_ref.shape, very_negative, jnp.float32)
    sum_ref[...] = jnp.zeros(sum_ref.shape, jnp.float32)
    mix_ref[...] = jnp.zeros(mix_ref.shape, jnp.float32)

    def score(index, group, keys, mask):
        scores = []
        for pair in range(heads // 2):
            both = both_ref[group, :, pair * lanes : (pair + 1) * lanes]
            none = jnp.zeros_like(both)
            split = jnp.concatenate(
                [jnp.where(lane < HEAD_DIM, both, none), jnp.where(lane < HEAD_DIM, none, both)], axis=0
            )
            scores.append(
                lax.dot_general(
                    split, keys[:, pair * lanes : (pair + 1) * lanes], (((1,), (1,)), ((), ())),
                    preferred_element_type=jnp.float32,
                )
            )
        scores = jnp.concatenate(scores, axis=0).reshape(heads, share, BLOCK)
        scores = jnp.where(mask[None], scores, very_negative).reshape(tall, BLOCK)
        score_ref[index] = scores
        top_ref[group] = jnp.maximum(top_ref[group], scores)

    def mix(index, group, values):
        weight = jnp.exp(score_ref[index] - top_ref[group])
        sum_ref[group] += weight
        rounded = weight.astype(jnp.bfloat16)
        mix_ref[group] += jnp.concatenate(
            [
                jnp.dot(
                    rounded[pair * 2 * share : (pair + 1) * 2 * share],
                    values[:, pair * lanes : (pair + 1) * lanes],
                    preferred_element_type=jnp.float32,
                )
                for pair in range(heads // 2)
            ],
            axis=0,
        )

    own = lax.axis_index("seq")
    fill = jnp.zeros((BLOCK - share, new_key_ref.shape[1]), jnp.bfloat16)
    score(
        blocks, own, jnp.concatenate([new_key_ref[...], fill], axis=0),
        (lane // new_tokens == row // new_tokens) & (lane <= row),
    )
    looking.wait()
    owners = []
    for block in range(blocks):
        if (block * BLOCK) % chunk == 0:
            copy(0, block * BLOCK // chunk).wait()
        group, live, first, end = (visit_ref[field * blocks + block] for field in range(4))
        owners.append(group)
        score(
            block, group, key_ref[block * BLOCK : (block + 1) * BLOCK, :],
            (lane < live) & (row >= first) & (row < end),
        )
    for group in range(groups):
        top = jnp.max(top_ref[group], axis=1, keepdims=True)
        top_ref[group] = jnp.broadcast_to(top, (tall, lanes))
    mix(blocks, own, jnp.concatenate([new_value_ref[...], fill], axis=0))
    for block in range(blocks):
        if (block * BLOCK) % chunk == 0:
            copy(1, block * BLOCK // chunk).wait()
        mix(block, owners[block], value_ref[block * BLOCK : (block + 1) * BLOCK, :])

    level = jnp.zeros((tall, lanes), jnp.float32)
    column = lax.broadcasted_iota(jnp.int32, (tall, lanes), 1)

    def mean(group):
        total = jnp.sum(sum_ref[group], axis=1, keepdims=True)
        total = jnp.where(total <= 0.0, 1.0, total)
        own_level = jnp.where(column == group, top_ref[group] + jnp.log(total), 0.0)
        return mix_ref[group] / total, own_level

    for group in range(groups // 2):
        left, left_level = mean(group)
        right, right_level = mean(group + groups // 2)
        level = level + left_level + right_level
        for head in range(heads):
            rows = slice(head * share, (head + 1) * share)
            first, second = left[rows], right[rows]
            if head % 2:
                first = pltpu.roll(first, HEAD_DIM, 1)
            else:
                second = pltpu.roll(second, HEAD_DIM, 1)
            packed = jnp.where(lane < HEAD_DIM, first, second)
            out_ref[head, group * share : (group + 1) * share] = packed.astype(jnp.bfloat16)
    level = level.T[:groups]
    high = level.astype(jnp.bfloat16).astype(jnp.float32)
    middle = (level - high).astype(jnp.bfloat16).astype(jnp.float32)
    low = level - high - middle
    rest = jnp.concatenate([high, middle, low, jnp.zeros_like(low)], axis=0).astype(jnp.bfloat16)
    start = (groups // 2) * share
    for head in range(heads):
        column = head * share // lanes * lanes
        out_ref[head, start:] = rest[:, column : column + lanes]


def attend(visits, query, far_query, new_key, new_value, k_cache, v_cache, layer_index, new_tokens, groups):
    width = query.shape[1]
    rows = 2 * query.shape[0]
    slots = k_cache.shape[1]
    heads = width // HEAD_DIM
    share = rows // groups
    tall = heads * share
    lanes = 2 * HEAD_DIM
    chunks = 2
    state = pltpu.VMEM((groups, tall, lanes), jnp.float32)
    return pl.pallas_call(
        functools.partial(attend_kernel, layer_index, new_tokens),
        out_shape=jax.ShapeDtypeStruct((heads, rows // 2 + 4 * groups, lanes), jnp.bfloat16),
        in_specs=[whole(pltpu.HBM)] + [whole()] * 4 + [whole(pltpu.HBM)] * 2,
        out_specs=whole(),
        scratch_shapes=[
            pltpu.VMEM((slots, width), jnp.bfloat16),
            pltpu.VMEM((slots, width), jnp.bfloat16),
            pltpu.SMEM(visits.shape, jnp.int32),
            pltpu.VMEM((groups, share, width), jnp.bfloat16),
            pltpu.VMEM((visits.shape[0] // 4 + 1, tall, BLOCK), jnp.float32),
            state,
            state,
            state,
            pltpu.SemaphoreType.DMA((2, chunks)),
            pltpu.SemaphoreType.DMA,
        ],
        compiler_params=compiler_params(24),
        name="attend",
    )(in_hbm(visits), query, far_query, new_key, new_value, in_hbm(k_cache), in_hbm(v_cache))


def update_kernel(
    layer_index, other, tp_count, has_start, part_ref, bias_ref, out_weight_ref, fc2_ref, *refs
):
    *unit_refs, out_ref, scale_ref = refs
    if has_start:
        *unit_refs, start_ref = unit_refs
    seq_index = lax.axis_index("seq")
    parity = 1 - seq_index % 2 if other else seq_index % 2
    sources, tall, lanes = part_ref.shape
    unit = unit_refs[0].shape[1]
    share = unit_refs[0].shape[0] // sources
    groups = (tall - (sources // 2) * share) // 4
    levels = []
    for source in range(sources):
        parts = part_ref[source, (sources // 2) * share :, :].astype(jnp.float32)
        levels.append(parts[:groups] + parts[groups : 2 * groups] + parts[2 * groups : 3 * groups])
    top = functools.reduce(jnp.maximum, levels)
    scales = [jnp.exp(level - top) for level in levels]
    total = functools.reduce(jnp.add, scales)
    scales = [scale / total for scale in scales]
    blank = jnp.zeros((lanes - groups * sources, lanes), jnp.float32)
    scale_ref[...] = jnp.concatenate(scales + [blank], axis=0).T
    place = seq_index % (lanes // share)
    scale = scale_ref[pl.ds(pl.multiple_of(place * share, share), share), :]
    scale = jnp.where(parity == 0, scale, pltpu.roll(scale, lanes - 1, 1))
    here = lax.axis_index("seq") // 2
    next_scale = pltpu.roll(scale, lanes - 2, 1)
    lane = lax.broadcasted_iota(jnp.int32, (share, lanes), 1)
    first, second = [], []
    for pair in range(CHIPS // 2):
        pack = (here % 2) ^ pair
        rows = pl.ds(pl.multiple_of((2 * pack + parity) * share, share), share)
        pair_scale = jnp.where(pack == 0, scale, next_scale)
        mixed = jnp.zeros((share, lanes), jnp.float32)
        for source in range(sources):
            column = source * groups
            left = pair_scale[:, column : column + 1]
            right = pair_scale[:, column + groups // 2 : column + groups // 2 + 1]
            mixed = mixed + part_ref[source, rows, :].astype(jnp.float32) * jnp.where(
                lane < HEAD_DIM, left, right
            )
        turned = pltpu.roll(mixed, HEAD_DIM, 1)
        first.append(jnp.where(here < 2, mixed, turned)[:, :HEAD_DIM])
        second.append(jnp.where(here < 2, turned, mixed)[:, :HEAD_DIM])
    attended = jnp.concatenate(first + second, axis=0).astype(jnp.bfloat16)
    bias = bias_ref[
        layer_index : layer_index + 1, pl.ds(pl.multiple_of(seq_index * unit, unit), unit)
    ]
    hidden, started = [], []
    for piece in range(CHIPS):
        rows = pl.ds(pl.multiple_of((2 * (piece ^ here) + parity) * share, share), share)
        pre = functools.reduce(jnp.add, [ref[rows, :].astype(jnp.float32) for ref in unit_refs])
        hidden.append(jax.nn.gelu(pre + bias, approximate=True).astype(jnp.bfloat16))
        if has_start:
            started.append(start_ref[rows, :].astype(jnp.float32))
    change = jnp.dot(attended, out_weight_ref[0], preferred_element_type=jnp.float32) + jnp.dot(
        jnp.concatenate(hidden, axis=0), fc2_ref[0], preferred_element_type=jnp.float32
    )
    if not has_start:
        out_ref[...] = change.astype(out_ref.dtype)
        return
    started = jnp.concatenate(started, axis=0)
    for column in range(0, change.shape[1], unit):
        here = (seq_index * unit == column) & (lax.axis_index("tp") == 0)
        out_ref[:, column : column + unit] = (
            change[:, column : column + unit] + jnp.where(here, started, 0.0)
        ).astype(out_ref.dtype)


def update(parts, units, start, b_fc1, w_out, w_fc2, layer_index, other, tp_count):
    rows = units[0].shape[0] // 2
    width = w_out.shape[2]
    lanes = parts.shape[2]
    extra = list(units) + ([] if start is None else [start])
    return pl.pallas_call(
        functools.partial(update_kernel, layer_index, other, tp_count, start is not None),
        grid=(1,),
        out_shape=jax.ShapeDtypeStruct((rows, width), jnp.bfloat16 if other else jnp.float32),
        in_specs=[
            same_block(parts.shape),
            same_block(b_fc1.shape),
            layer_block(layer_index, w_out.shape[1:]),
            layer_block(layer_index, w_fc2.shape[1:]),
        ]
        + [same_block(units[0].shape)] * len(extra),
        out_specs=same_block((rows, width)),
        scratch_shapes=[pltpu.VMEM((lanes, lanes), jnp.float32)],
        compiler_params=compiler_params(),
        name="update",
    )(parts, b_fc1, w_out, w_fc2, *extra)


def per_device(
    token_ids, embedding, group_of, prefix_len, tail_len, block_map, k_cache, v_cache,
    ln_gain, ln_bias, w_qkv, w_fc1, b_fc1, w_out, w_fc2,
):
    seq_count, tp_count = lax.axis_size("seq"), lax.axis_size("tp")
    seq_index, tp_index = lax.axis_index("seq"), lax.axis_index("tp")
    devices = seq_count * tp_count
    core = seq_index % 2
    requests, new_tokens = token_ids.shape
    rows = requests * new_tokens
    groups = prefix_len.shape[0]
    share = rows // seq_count
    features = embedding.shape[1]
    width_local = k_cache.shape[2]
    unit = w_fc2.shape[1]

    def to_distances(parts):
        return [parts[0]] + [
            lax.ppermute(parts[k], "seq", [(i, i ^ (2 * k)) for i in range(seq_count)])
            for k in range(1, CHIPS)
        ]

    def over_tp(part, distance):
        return lax.ppermute(part, "tp", [(i, i ^ distance) for i in range(tp_count)])

    def from_tp(part):
        return [part] + [over_tp(part, k) for k in range(1, tp_count)]

    near, far, own = embed(token_ids, group_of, embedding, unit)
    parts = join(near, swap_cores(far, seq_count), own)
    gathered = gather(to_distances(parts))
    gathered, group_of = lax.optimization_barrier((gathered, group_of))
    rank, positions, visits = order_requests(group_of, prefix_len, tail_len, block_map, new_tokens)
    own_positions = lax.dynamic_index_in_dim(positions.reshape(CHIPS, 2, share), core, 1, keepdims=False)
    backs = back_rows(group_of, new_tokens)
    tables = rotary_tables(own_positions.reshape(-1), 2 * HEAD_DIM)
    weights_qkv = w_qkv[0].reshape(w_qkv.shape[1], -1)
    parts, backs, tables, visits = lax.optimization_barrier(
        (from_tp(gathered), backs, tables, visits)
    )
    start, hidden = first_hidden(parts, ln_gain, ln_bias)
    state = None
    for layer_index in range(LAYERS):
        if layer_index:
            weights_qkv = w_qkv[layer_index].reshape(w_qkv.shape[1], -1)
            state, cut = norm_rows(parts, state, ln_gain, ln_bias, layer_index, devices, tp_count)
            hidden = lax.all_to_all(cut, ("seq", "tp"), 0, 0).reshape(rows, -1)
        arriving = swap_cores(project_heads(hidden, weights_qkv, unit), seq_count)
        heads = to_distances(project_heads(hidden, weights_qkv, unit, arriving))
        arriving = swap_cores(project_units(hidden, w_fc1, layer_index), seq_count)
        units = project_units(hidden, w_fc1, layer_index, arriving)
        heads, units = lax.optimization_barrier((heads, units))
        query, new_key, new_value = activate(heads, tables, width_local)
        units = to_distances(units)
        parts = attend(
            visits, query, swap_cores(query, seq_count), new_key, new_value,
            k_cache, v_cache, layer_index, new_tokens, groups,
        )
        parts, *units = lax.optimization_barrier((parts, *units))
        parts = lax.all_to_all(parts, "seq", 0, 0)
        arriving, half = (
            update(parts, units, start, b_fc1, w_out, w_fc2, layer_index, other, tp_count)
            for other in (True, False)
        )
        parts = to_distances(split(half, swap_cores(arriving, seq_count)))
        start = None
        if layer_index < LAYERS - 1:
            parts = share_rows(parts, tp_count)
            parts = [parts[0]] + [over_tp(parts[k], k) for k in range(1, tp_count)]
    last = last_parts(parts, state, tp_count)
    last = from_tp(last)
    last = to_distances([last_rows(last)] * CHIPS)
    return restore(backs, last, [swap_cores(part, seq_count) for part in last], new_tokens)


def solution(mesh):
    in_specs = (
        P(),
        P(("seq", "tp"), None),
        P(),
        P(),
        P(),
        P("seq", None),
        P(None, "seq", "tp"),
        P(None, "seq", "tp"),
        P(),
        P(),
        P(None, "seq", None, "tp"),
        P(None, "seq", "tp"),
        P(None, "tp"),
        P(None, ("tp", "seq"), None),
        P(None, ("tp", "seq"), None),
    )
    out_specs = P()
    seq_count, tp_count = mesh.shape["seq"], mesh.shape["tp"]
    fits = tp_count == 4 and seq_count == HEADS // tp_count and seq_count == 2 * CHIPS
    return jax.shard_map(
        per_device if fits else per_device_any, mesh=mesh, in_specs=in_specs, out_specs=out_specs, check_vma=False
    )
```
